256 devices in a mesh: section: 2 (over x_lo), gr: 8 (over y, core), gc: 16 (over x_hi, z).
Axes of the slice: x: 4 (x_hi: 2, x_lo: 2; x = x_hi * 2 + x_lo), y: 4, z: 8, core: 2. Of those that a mesh axis runs over, the one named last changes fastest.
Arguments:
- pair: bfloat16 [2, 512, 512, 128], P(None, 'gr', 'gc'), may hold values from -6 to 6
- single: bfloat16 [2, 512, 384], P(None, 'gr'), may hold values from -6 to 6
- lengths: int32 [2], replicated, may hold values from 256 to 512, as said below
- tri_in: bfloat16 [2, 128, 512], P('section'), may hold values from -0.5 to 0.5
- tri_gate: bfloat16 [2, 128, 128], P('section'), may hold values from -0.5 to 0.5
- tri_out: bfloat16 [2, 128, 128], P('section'), may hold values from -0.5 to 0.5
- pt_in: bfloat16 [2, 128, 1024], P('section'), may hold values from -0.5 to 0.5
- pt_out: bfloat16 [2, 512, 128], P('section'), may hold values from -0.25 to 0.25
- st_in: bfloat16 [2, 384, 3072], P('section'), may hold values from -0.3125 to 0.3125
- st_out: bfloat16 [2, 1536, 384], P('section'), may hold values from -0.15625 to 0.15625
Outputs:
- pair_out: bfloat16 [2, 2, 512, 512, 128], P('section', None, 'gr', 'gc')
- single_out: bfloat16 [2, 2, 512, 384], P('section', None, 'gr')
The draws below stay inside these ranges and needn't reach their ends.
Inputs may be any that keep to these rules, and one draw needn't show every extreme that they name: `lengths`: each micro-batch's count of real tokens at the start of the crop; some micro-batch is a full crop of 512 and some has exactly half.
All inputs are finite; a program needn't handle non-finite values.
Results may differ from the reference program's by a relative error of at most 0.024.
Values may be sent and summed in bfloat16 or wider, within the bound.
A program may use at most 128 MiB of HBM per device.

```python
import jax
import jax.numpy as jnp
from jax import lax

CZ = 128
HT = 128
CS = 384
FZ = 512
FS = 1536
MB = 2
N = 512


def draw_lengths(key, part):
    key = jax.random.fold_in(key, 11)
    first_key, second_key = jax.random.split(key)
    values = jax.random.randint(first_key, (MB,), N // 2, N + 1, dtype=jnp.int32)
    order = jax.random.permutation(second_key, MB)
    values = values.at[order[0]].set(N)
    values = values.at[order[1]].set(N // 2)
    return values.astype(jnp.int32)


def shard_levels(own_key, shape, cuts, smallest, high):
    level, own = 1.0, jax.random.fold_in(own_key, 6)
    for axis_at, shards_of in cuts:
        heights = jnp.exp(jax.random.uniform(jax.random.fold_in(own, axis_at), (shards_of,), jnp.float32, smallest / len(cuts), high / len(cuts)))
        level = level * jnp.repeat(heights, shape[axis_at] // shards_of).reshape([-1 if axis == axis_at else 1 for axis in range(len(shape))])
    return level


def centred(key, dims, width, most, shards=(), kind=jnp.bfloat16):
    drawn = jax.random.normal(key, dims, jnp.float32) * width
    if len(shards) > 0:
        drawn = shard_levels(key, dims, shards, -0.22, 0.18) * drawn
    return jnp.clip(drawn, min=-most, max=most).astype(kind)


def setup_inputs(seed: int = 0) -> dict:
    splits = jax.random.split(jax.random.key(seed), 11)
    return {
        "pair": centred(splits[0], (MB, N, N, CZ), 1.0, 6.0, ((1, 8), (2, 16))),
        "single": centred(splits[1], (MB, N, CS), 1.0, 6.0, ((1, 8),)),
        "lengths": draw_lengths(jax.random.fold_in(splits[10], 71), 0),
        "tri_in": centred(splits[3], (2, CZ, 4 * HT), CZ ** -0.5, 0.5, ((0, 2),)),
        "tri_gate": centred(splits[4], (2, CZ, CZ), CZ ** -0.5, 0.5, ((0, 2),)),
        "tri_out": centred(splits[5], (2, HT, CZ), HT ** -0.5, 0.5, ((0, 2),)),
        "pt_in": centred(splits[6], (2, CZ, 2 * FZ), CZ ** -0.5, 0.5, ((0, 2),)),
        "pt_out": centred(splits[7], (2, FZ, CZ), FZ ** -0.5, 0.25, ((0, 2),)),
        "st_in": centred(splits[8], (2, CS, 2 * FS), CS ** -0.5, 0.3125, ((0, 2),)),
        "st_out": centred(splits[9], (2, FS, CS), FS ** -0.5, 0.15625, ((0, 2),)),
    }


def normalize(values, axis):
    center = values - lax.optimization_barrier(jnp.mean(values, axis=axis, keepdims=True))
    spread = lax.optimization_barrier(jnp.mean(center * center, axis=axis, keepdims=True))
    return center * lax.rsqrt(spread + 1e-05)

def run_block(pair_in, single_in, length, weights):
    tri_in, tri_gate, tri_out, pt_in, pt_out, st_in, st_out = weights
    hidden_width = tri_out.shape[0]
    pair_hidden = pt_out.shape[0]
    single_hidden = st_out.shape[0]
    pair_full = pair_in.astype(jnp.float32)
    normed = normalize(pair_full, -1).astype(jnp.bfloat16)
    projected = jnp.dot(normed, tri_in, preferred_element_type=jnp.float32)
    positions = jnp.arange(N, dtype=jnp.int32)
    inside = (positions < length).astype(jnp.float32)
    pair_mask = (inside[:, None] * inside[None, :])[:, :, None]
    left_gated = (jax.nn.sigmoid(projected[..., :hidden_width]) * projected[..., hidden_width:2 * hidden_width] * pair_mask).astype(jnp.bfloat16)
    right_gated = (jax.nn.sigmoid(projected[..., 2 * hidden_width:3 * hidden_width]) * projected[..., 3 * hidden_width:] * pair_mask).astype(jnp.bfloat16)
    triangle = jnp.einsum('ikh,jkh->ijh', left_gated.astype(jnp.float32), right_gated.astype(jnp.float32), precision=lax.Precision.HIGHEST)
    settled = normalize(triangle, -1).astype(jnp.bfloat16)
    gate_value = jax.nn.sigmoid(jnp.dot(normed, tri_gate, preferred_element_type=jnp.float32))
    update = jnp.dot(settled, tri_out, preferred_element_type=jnp.float32)
    updated = (pair_full + gate_value * update).astype(jnp.bfloat16)
    updated_full = updated.astype(jnp.float32)
    trans_in = normalize(updated_full, -1).astype(jnp.bfloat16)
    widened = jnp.dot(trans_in, pt_in, preferred_element_type=jnp.float32)
    inner = (jax.nn.silu(widened[..., :pair_hidden]) * widened[..., pair_hidden:]).astype(jnp.bfloat16)
    pair_next = (updated_full + jnp.dot(inner, pt_out, preferred_element_type=jnp.float32)).astype(jnp.bfloat16)
    single_full = single_in.astype(jnp.float32)
    single_normed = normalize(single_full, -1).astype(jnp.bfloat16)
    single_wide = jnp.dot(single_normed, st_in, preferred_element_type=jnp.float32)
    single_inner = (jax.nn.silu(single_wide[..., :single_hidden]) * single_wide[..., single_hidden:]).astype(jnp.bfloat16)
    single_next = (single_full + jnp.dot(single_inner, st_out, preferred_element_type=jnp.float32)).astype(jnp.bfloat16)
    return (pair_next, single_next)

def reference(pair, single, lengths, tri_in, tri_gate, tri_out, pt_in, pt_out, st_in, st_out):
    first_pairs = []
    first_singles = []
    second_pairs = []
    second_singles = []
    for micro in range(MB):
        first_weights = (tri_in[0], tri_gate[0], tri_out[0], pt_in[0], pt_out[0], st_in[0], st_out[0])
        second_weights = (tri_in[1], tri_gate[1], tri_out[1], pt_in[1], pt_out[1], st_in[1], st_out[1])
        pair_one, single_one = run_block(pair[micro], single[micro], lengths[micro], first_weights)
        pair_two, single_two = run_block(pair_one, single_one, lengths[micro], second_weights)
        first_pairs.append(pair_one)
        first_singles.append(single_one)
        second_pairs.append(pair_two)
        second_singles.append(single_two)
    pair_out = jnp.stack([jnp.stack(first_pairs), jnp.stack(second_pairs)])
    single_out = jnp.stack([jnp.stack(first_singles), jnp.stack(second_singles)])
    return (pair_out, single_out)
```

```python
import jax
import jax.numpy as jnp
from jax import lax
from jax.experimental import pallas as pl
from jax.experimental.pallas import tpu as pltpu
from jax.sharding import PartitionSpec as P

MESH = pl.DeviceIdType.MESH


def shifted(value, axis, steps):
    count = lax.axis_size(axis)
    initial, last = (max(0, -steps), min(count, count - steps))
    return lax.ppermute(value, axis, [(source, source + steps) for source in range(initial, last)])


def normalize(values, axis):
    center = values - jnp.mean(values, axis=axis, keepdims=True)
    spread = jnp.mean(center * center, axis=axis, keepdims=True)
    return center * lax.rsqrt(spread + 1e-05)


def exchange_kernel(source, landed, send_sem, recv_sem):
    arrays, peers = source.shape[0], source.shape[1]
    rows_count, cols_count = lax.axis_size("gr"), lax.axis_size("gc")
    row, col = lax.axis_index("gr"), lax.axis_index("gc")
    mine = row * cols_count + col

    def partner(step):
        return (
            lax.rem(row + step // cols_count, rows_count),
            lax.rem(col + step % cols_count, cols_count),
        )

    barrier = pltpu.get_barrier_semaphore()

    def greet(step, carry):
        to_row, to_col = partner(step)
        pl.semaphore_signal(
            barrier, inc=1, device_id={"gr": to_row, "gc": to_col}, device_id_type=MESH
        )
        return carry

    lax.fori_loop(1, peers, greet, 0)
    pl.semaphore_wait(barrier, peers - 1)
    for array in range(arrays):

        def send(step, carry):
            to_row, to_col = partner(step)
            pltpu.make_async_remote_copy(
                src_ref=source.at[array, to_row * cols_count + to_col],
                dst_ref=landed.at[array, mine],
                send_sem=send_sem.at[array],
                recv_sem=recv_sem.at[array],
                device_id={"gr": to_row, "gc": to_col},
                device_id_type=MESH,
            ).start()
            return carry

        lax.fori_loop(1, peers, send, 0)
        pltpu.make_async_copy(
            source.at[array, mine], landed.at[array, mine], recv_sem.at[array]
        ).start()
    for array in range(arrays):
        whole = landed.at[array]
        pltpu.make_async_copy(whole, whole, recv_sem.at[array]).wait()
        others = landed.at[array, pl.ds(0, peers - 1)]
        pltpu.make_async_copy(others, others, send_sem.at[array]).wait()


def exchange(blocks, collective_id):
    arrays = blocks.shape[0]
    return pl.pallas_call(
        exchange_kernel,
        out_shape=jax.ShapeDtypeStruct(blocks.shape, blocks.dtype),
        in_specs=[pl.BlockSpec(memory_space=pltpu.VMEM)],
        out_specs=pl.BlockSpec(memory_space=pltpu.VMEM),
        scratch_shapes=[
            pltpu.SemaphoreType.DMA((arrays,)),
            pltpu.SemaphoreType.DMA((arrays,)),
        ],
        compiler_params=pltpu.CompilerParams(
            collective_id=collective_id, has_side_effects=True, vmem_limit_bytes=32 << 20
        ),
    )(blocks)


def triangle_sum(left_gated, right_gated):
    depth_all, rows_tile, cols_tile = left_gated.shape
    grid_rows, grid_cols = lax.axis_size("gr"), lax.axis_size("gc")
    both = jnp.stack([left_gated, right_gated]).reshape(2, depth_all, 16, 128)
    landed = exchange(both, 0).reshape(2, grid_rows, grid_cols, rows_tile, cols_tile)
    whole = landed.swapaxes(2, 3).reshape(2, grid_rows * rows_tile, grid_cols * cols_tile)
    product = jnp.einsum("ik,jk->ij", whole[0], whole[1], preferred_element_type=jnp.float32)
    tiles = product.astype(jnp.bfloat16).reshape(grid_rows, rows_tile, grid_cols, cols_tile)
    back = exchange(tiles.swapaxes(1, 2).reshape(1, depth_all, 16, 128), 1)
    return back.reshape(depth_all, rows_tile, cols_tile).astype(jnp.float32)


def pair_block(tile, length, weights):
    tri_in, tri_gate, tri_out, pt_in, pt_out, st_in, st_out = weights
    rows_tile, cols_tile, width = tile.shape
    hidden_width = tri_out.shape[0]
    pair_hidden = pt_out.shape[0]
    row_start = lax.axis_index("gr") * rows_tile
    col_start = lax.axis_index("gc") * cols_tile
    row_inside = (row_start + jnp.arange(rows_tile, dtype=jnp.int32) < length).astype(jnp.float32)
    col_inside = (col_start + jnp.arange(cols_tile, dtype=jnp.int32) < length).astype(jnp.float32)
    tile_mask = row_inside[:, None] * col_inside[None, :]
    pair_full = tile.astype(jnp.float32)
    normed = normalize(pair_full, 2).astype(jnp.bfloat16)
    projected = jnp.einsum("ijc,cf->fij", normed, tri_in, preferred_element_type=jnp.float32)
    left_gated = (
        jax.nn.sigmoid(projected[:hidden_width])
        * projected[hidden_width : 2 * hidden_width]
        * tile_mask
    ).astype(jnp.bfloat16)
    right_gated = (
        jax.nn.sigmoid(projected[2 * hidden_width : 3 * hidden_width])
        * projected[3 * hidden_width :]
        * tile_mask
    ).astype(jnp.bfloat16)
    triangle = triangle_sum(left_gated, right_gated)
    settled = normalize(triangle, 0).astype(jnp.bfloat16)
    gate_value = jax.nn.sigmoid(
        jnp.einsum("ijc,cd->ijd", normed, tri_gate, preferred_element_type=jnp.float32)
    )
    update = jnp.einsum("hij,hc->ijc", settled, tri_out, preferred_element_type=jnp.float32)
    updated = (pair_full + gate_value * update).astype(jnp.bfloat16)
    updated_full = updated.astype(jnp.float32)
    trans_in = normalize(updated_full, 2).astype(jnp.bfloat16)
    widened = jnp.dot(trans_in, pt_in, preferred_element_type=jnp.float32)
    inner = (jax.nn.silu(widened[..., :pair_hidden]) * widened[..., pair_hidden:]).astype(
        jnp.bfloat16
    )
    return (updated_full + jnp.dot(inner, pt_out, preferred_element_type=jnp.float32)).astype(
        jnp.bfloat16
    )


def single_block(rows_in, weights):
    tri_in, tri_gate, tri_out, pt_in, pt_out, st_in, st_out = weights
    single_hidden = st_out.shape[0]
    single_full = rows_in.astype(jnp.float32)
    single_normed = normalize(single_full, 1).astype(jnp.bfloat16)
    single_wide = jnp.dot(single_normed, st_in, preferred_element_type=jnp.float32)
    single_inner = (
        jax.nn.silu(single_wide[:, :single_hidden]) * single_wide[:, single_hidden:]
    ).astype(jnp.bfloat16)
    return (single_full + jnp.dot(single_inner, st_out, preferred_element_type=jnp.float32)).astype(
        jnp.bfloat16
    )


def on_device(pair, single, lengths, tri_in, tri_gate, tri_out, pt_in, pt_out, st_in, st_out):
    weights = (tri_in[0], tri_gate[0], tri_out[0], pt_in[0], pt_out[0], st_in[0], st_out[0])
    section_index = lax.axis_index("section")
    leading = section_index == 0
    micro_count = pair.shape[0]
    first_pairs = []
    first_singles = []
    for micro in range(micro_count):
        first_pairs.append(pair_block(pair[micro], lengths[micro], weights))
        first_singles.append(single_block(single[micro], weights))
    stacked_pairs = jnp.stack(first_pairs)
    stacked_singles = jnp.stack(first_singles)
    moved_pairs, moved_singles = shifted((stacked_pairs, stacked_singles), "section", 1)
    second_pairs = []
    second_singles = []
    for micro in range(micro_count):
        second_pairs.append(pair_block(moved_pairs[micro], lengths[micro], weights))
        second_singles.append(single_block(moved_singles[micro], weights))
    pair_store = jnp.where(leading, stacked_pairs, jnp.stack(second_pairs))
    single_store = jnp.where(leading, stacked_singles, jnp.stack(second_singles))
    return (pair_store[None], single_store[None])


def solution(mesh):
    in_specs = (
        P(None, "gr", "gc", None),
        P(None, "gr", None),
        P(),
        P("section", None, None),
        P("section", None, None),
        P("section", None, None),
        P("section", None, None),
        P("section", None, None),
        P("section", None, None),
        P("section", None, None),
    )
    out_specs = (P("section", None, "gr", "gc", None), P("section", None, "gr", None))
    return jax.shard_map(
        on_device, mesh=mesh, in_specs=in_specs, out_specs=out_specs, check_vma=False
    )
```

```python
import jax
import jax.numpy as jnp
from jax import lax
from jax.experimental import pallas as pl
from jax.experimental.pallas import tpu as pltpu
from jax.sharding import PartitionSpec as P

MESH = pl.DeviceIdType.MESH
FULL, HALF = 0, 1
BF = jnp.bfloat16
F32 = jnp.float32


def dot(a, b):
    return jnp.dot(a, b, preferred_element_type=F32)


def dot_nt(a, b):
    return lax.dot_general(a, b, (((1,), (1,)), ((), ())), preferred_element_type=F32)


def sigmoid(v):
    return 0.5 + 0.5 * jnp.tanh(0.5 * v)


def norm_lanes(v):
    center = v - jnp.mean(v, axis=-1, keepdims=True)
    spread = jnp.mean(center * center, axis=-1, keepdims=True)
    return center * lax.rsqrt(spread + 1e-05)


def iota(shape, axis):
    return lax.broadcasted_iota(jnp.int32, shape, axis)


def trunk_kernel(
    zin, sin, tin, tgate, tout, pin, pout, st_in, st_out,
    out, sout,
    w_tin, w_gate, w_out, w_pin, w_pout, w_t, st_in_v, st_out_v, sin_next,
    zmid, zlast, normed, stage, settled, perm, order_full, order_half,
    sbuf, rbuf_full, rbuf_half, lm_full, raw_full, all_full, lm_half, raw_half, all_half,
    ts_full, ts_half, tr_full, tr_half,
    fwd_send, fwd_recv, sib_send, sib_recv, back_send, back_recv,
    w_send, w_recv, st_sem, single_send, single_recv, out_send, out_recv,
):
    sec, gr, gc = lax.axis_index("section"), lax.axis_index("gr"), lax.axis_index("gc")
    y, core = lax.shift_right_logical(gr, 1), lax.bitwise_and(gr, 1)
    sy = sec * 4 + y
    me = gc * 8 + sy
    me_half = gc * 4 + sec * 2 + y
    active = jnp.logical_and(y < 2, gc < 8)
    peer = {"section": 1 - sec, "gr": gr, "gc": gc}
    sibling = {"section": sec, "gr": gr + 1 - 2 * core, "gc": gc}

    def place(step):
        to_gc = lax.bitwise_and(gc + step, 15)
        to_sy = lax.bitwise_and(sy + lax.shift_right_logical(step, 4), 7)
        to_sec = lax.shift_right_logical(to_sy, 2)
        to_y = lax.bitwise_and(to_sy, 3)
        return to_gc, to_sy, {"section": to_sec, "gr": to_y * 2 + core, "gc": to_gc}

    st_copies = [
        pltpu.make_async_copy(st_in, st_in_v, st_sem.at[0]),
        pltpu.make_async_copy(st_out, st_out_v, st_sem.at[1]),
    ]
    for copy in st_copies:
        copy.start()

    barrier = pltpu.get_barrier_semaphore()

    def greet(step, carry):
        pl.semaphore_signal(barrier, inc=1, device_id=place(step)[2], device_id_type=MESH)
        return carry

    pl.semaphore_signal(barrier, inc=1, device_id=sibling, device_id_type=MESH)
    lax.fori_loop(1, 128, greet, 0)

    weights = [(tin, w_tin), (tgate, w_gate), (tout, w_out), (pin, w_pin), (pout, w_pout)]
    for own, held in weights:
        held[sec] = own[...]

    from_lane, to_lane = iota((128, 512), 0), iota((128, 512), 1)
    for low in range(4):
        target = (from_lane >> 5) * 128 + low * 32 + (from_lane & 31)
        perm[low] = jnp.where(to_lane == target, 1.0, 0.0).astype(BF)
    o, i = iota((256, 256), 0), iota((256, 256), 1)
    source = (o & 3) * 64 + ((o >> 5) & 1) * 32 + (o >> 6) * 8 + ((o >> 2) & 7)
    order_full[...] = jnp.where(i == source, 1.0, 0.0).astype(BF)
    o, i = iota((128, 128), 0), iota((128, 128), 1)
    source = (o & 3) * 32 + ((o >> 5) & 1) * 16 + (o >> 6) * 8 + ((o >> 2) & 7)
    order_half[...] = jnp.where(i == source, 1.0, 0.0).astype(BF)

    for kind in (FULL, HALF):
        for part in range(4):
            rows = pl.ds(part * 256, 256)
            normed[kind, rows] = norm_lanes(zin[kind, rows].astype(F32)).astype(BF)

    pl.semaphore_wait(barrier, 128)

    def weight_copy(index):
        own, held = weights[index]
        return pltpu.make_async_remote_copy(
            own, held.at[sec], w_send.at[index], w_recv.at[index],
            device_id=peer, device_id_type=MESH,
        )

    weight_copy(0).start()

    def await_weight(block, index):
        @pl.when(sec != block)
        def _():
            held = weights[index][1].at[block]
            pltpu.make_async_copy(held, held, w_recv.at[index]).wait()

    def project(block, kind):
        for part in range(4):
            rows = pl.ds(part * 256, 256)
            p = dot_nt(w_t[...], normed[kind, rows])
            left = sigmoid(p[0:128]) * p[128:256]
            right = sigmoid(p[256:384]) * p[384:512]
            for sub in range(2):
                cols = slice(sub * 128, sub * 128 + 128)
                stage[pl.ds(part * 2 + sub, 128, stride=16), :] = left[:, cols]
                stage[pl.ds(8 + part * 2 + sub, 128, stride=16), :] = right[:, cols]
        for part in range(8):
            values = stage[part * 256 : part * 256 + 256, :].astype(BF)
            sbuf[block, kind, part * 16 : part * 16 + 16] = values.reshape(16, 16, 128)

    def send_forward(block, kind):
        rbuf, slot = (rbuf_full, me) if kind == FULL else (rbuf_half, me_half)

        def send(step, carry):
            to_gc, to_sy, device = place(step)
            pltpu.make_async_remote_copy(
                sbuf.at[block, kind, to_gc * 8 + to_sy], rbuf.at[block, slot],
                fwd_send.at[block, kind], fwd_recv.at[block, kind],
                device_id=device, device_id_type=MESH,
            ).start()
            return carry

        lax.fori_loop(1, 128, send, 0)
        pltpu.make_async_copy(
            sbuf.at[block, kind, me], rbuf.at[block, slot], fwd_recv.at[block, kind]
        ).start()

    def forward(block, kind):
        if kind == FULL:
            project(block, kind)
            send_forward(block, kind)
        else:

            @pl.when(active)
            def _():
                project(block, kind)
                send_forward(block, kind)

    def triangle(block, kind):
        full = kind == FULL
        rbuf, lm, raw, whole, ts, order, groups, tiles = (
            (rbuf_full, lm_full, raw_full, all_full, ts_full, order_full, 4, 8)
            if full
            else (rbuf_half, lm_half, raw_half, all_half, ts_half, order_half, 2, 4)
        )
        depth = groups * 128
        rows = tiles * 8
        landed = rbuf.at[block]
        pltpu.make_async_copy(landed, landed, fwd_recv.at[block, kind]).wait()
        for g in range(groups):
            total = None
            for low in range(4):
                col = g * 4 + low
                block_in = rbuf[block, col * tiles : (col + 1) * tiles].reshape(tiles * 16, 128)
                term = dot(block_in, perm[low])
                total = term if total is None else total + term
            total = total.reshape(tiles, 16, 512)
            left = total[:, 0:8].reshape(rows, 512).astype(BF)
            right = total[:, 8:16].reshape(rows, 512).astype(BF)
            for low in range(4):
                cols = slice(low * 128, low * 128 + 128)
                lm[low * rows : (low + 1) * rows, g * 128 : g * 128 + 128] = left[:, cols]
                raw[low * rows : (low + 1) * rows, g * 128 : g * 128 + 128] = right[:, cols]
        ordered = dot(order[...], raw[...]).astype(BF)
        whole[block, core] = ordered.reshape(tiles // 2, 64, depth)
        mine = whole.at[block, core]
        pltpu.make_async_remote_copy(
            mine, mine, sib_send.at[block, kind], sib_recv.at[block, kind],
            device_id=sibling, device_id_type=MESH,
        ).start()
        other = whole.at[block, 1 - core]
        pltpu.make_async_copy(other, other, sib_recv.at[block, kind]).wait()
        for g in range(groups):
            right = jnp.concatenate(
                [whole[block, 0, g], whole[block, 1, g]], axis=0
            )
            product = dot_nt(lm[...], right).astype(BF)
            total = None
            for low in range(4):
                term = dot(product[low * rows : (low + 1) * rows], perm[low])
                total = term if total is None else total + term
            total = total.astype(BF)
            for low in range(4):
                ts[block, g * 4 + low] = total[:, low * 128 : low * 128 + 128].reshape(
                    tiles, 8, 128
                )

    def send_back(block, kind):
        if kind == FULL:

            def send(step, carry):
                to_gc, to_sy, device = place(step)
                pltpu.make_async_remote_copy(
                    ts_full.at[block, to_gc, to_sy], tr_full.at[block, me],
                    back_send.at[block, kind], back_recv.at[block, kind],
                    device_id=device, device_id_type=MESH,
                ).start()
                return carry

            lax.fori_loop(1, 128, send, 0)
            pltpu.make_async_copy(
                ts_full.at[block, gc, sy], tr_full.at[block, me], back_recv.at[block, kind]
            ).start()
        else:

            def send(step, carry):
                to_gc = lax.bitwise_and(gc + step, 7)
                to_q = lax.bitwise_and(sec * 2 + y + lax.shift_right_logical(step, 3), 3)
                to_sec, to_y = lax.shift_right_logical(to_q, 1), lax.bitwise_and(to_q, 1)
                itself = jnp.logical_and(
                    to_gc == gc, jnp.logical_and(to_sec == sec, to_y == y)
                )

                @pl.when(itself)
                def _():
                    pltpu.make_async_copy(
                        ts_half.at[block, to_gc, to_q], tr_half.at[block, me],
                        back_recv.at[block, kind],
                    ).start()

                @pl.when(jnp.logical_not(itself))
                def _():
                    pltpu.make_async_remote_copy(
                        ts_half.at[block, to_gc, to_q], tr_half.at[block, me],
                        back_send.at[block, kind], back_recv.at[block, kind],
                        device_id={"section": to_sec, "gr": to_y * 2 + core, "gc": to_gc},
                        device_id_type=MESH,
                    ).start()

                return carry

            lax.fori_loop(0, 32, send, 0)

    def finish(block, kind):
        z = zin if block == 0 else zmid
        znext = zmid if block == 0 else zlast
        tr = tr_full if kind == FULL else tr_half
        landed = tr.at[block]
        if kind == FULL:
            pltpu.make_async_copy(landed, landed, back_recv.at[block, kind]).wait()
        else:

            @pl.when(active)
            def _():
                pltpu.make_async_copy(landed, landed, back_recv.at[block, kind]).wait()

            @pl.when(jnp.logical_not(active))
            def _():
                tr[block] = jnp.zeros((128, 8, 128), BF)

        values = tr[block].astype(F32)
        center = values - jnp.mean(values, axis=0, keepdims=True)
        spread = jnp.mean(center * center, axis=0, keepdims=True)
        center = center * lax.rsqrt(spread + 1e-05)
        stage[0:1024, :] = center.reshape(1024, 128)
        for r in range(8):
            tile = stage[pl.ds(r, 128, stride=8), :]
            settled[r * 128 : r * 128 + 128] = tile.T.astype(BF)
        for part in range(4):
            rows = pl.ds(part * 256, 256)
            gate = sigmoid(dot(normed[kind, rows], w_gate[block]))
            update = dot(settled[rows], w_out[block])
            updated = (z[kind, rows].astype(F32) + gate * update).astype(BF)
            updated = updated.astype(F32)
            trans_in = norm_lanes(updated).astype(BF)
            gates = dot(trans_in, w_pin[block, :, 0:512])
            ups = dot(trans_in, w_pin[block, :, 512:1024])
            inner = (gates * sigmoid(gates) * ups).astype(BF)
            done = (updated + dot(inner, w_pout[block])).astype(BF)
            znext[kind, rows] = done
            if block == 0:
                normed[kind, rows] = norm_lanes(done.astype(F32)).astype(BF)

    def deliver(block, kind):
        znext = zmid if block == 0 else zlast

        @pl.when(sec == block)
        def _():
            out[kind, sec] = znext[kind]

        @pl.when(sec != block)
        def _():
            pltpu.make_async_remote_copy(
                znext.at[kind], out.at[kind, sec], out_send.at[kind], out_recv.at[kind],
                device_id=peer, device_id_type=MESH,
            ).start()

    def single(rows_in):
        value = rows_in[...].astype(F32)
        value_in = norm_lanes(value).astype(BF)
        total = value
        for part in range(6):
            cols = part * 256
            gates = dot(value_in, st_in_v[:, cols : cols + 256])
            ups = dot(value_in, st_in_v[:, 1536 + cols : 1536 + cols + 256])
            inner = (gates * sigmoid(gates) * ups).astype(BF)
            total = total + dot(inner, st_out_v[cols : cols + 256])
        sout[...] = total.astype(BF)

    single_copy = pltpu.make_async_remote_copy(
        sout, sin_next, single_send, single_recv, device_id=peer, device_id_type=MESH
    )

    for block in range(2):
        await_weight(block, 0)
        w_t[...] = w_tin[block].astype(F32).T.astype(BF)
        if block == 0:
            forward(block, FULL)
            for index in range(1, 5):
                weight_copy(index).start()
            forward(block, HALF)
        else:
            forward(block, FULL)
            finish(0, HALF)
            deliver(0, HALF)
            forward(block, HALF)

        @pl.when(sec == block)
        def _():
            if block == 0:
                for copy in st_copies:
                    copy.wait()
                single(sin)
                single_copy.start()
            else:
                for copy in st_copies:
                    copy.wait()
                single_copy.wait_recv()
                single(sin_next)

        triangle(block, FULL)
        send_back(block, FULL)
        triangle(block, HALF)
        send_back(block, HALF)
        for index in range(1, 5):
            await_weight(block, index)
        finish(block, FULL)
        deliver(block, FULL)
    finish(1, HALF)
    deliver(1, HALF)

    for block in range(2):
        for kind in (FULL, HALF):
            sent = rbuf_full.at[block, pl.ds(0, 127)]
            wait_sent = pltpu.make_async_copy(sent, sent, fwd_send.at[block, kind])
            if kind == FULL:
                wait_sent.wait()
            else:
                pl.when(active)(wait_sent.wait)
            whole = all_full if kind == FULL else all_half
            mine = whole.at[block, core]
            pltpu.make_async_copy(mine, mine, sib_send.at[block, kind]).wait()
            if kind == FULL:
                sent = tr_full.at[block, pl.ds(0, 127)]
                pltpu.make_async_copy(sent, sent, back_send.at[block, kind]).wait()
            else:

                @pl.when(active)
                def _():
                    sent = tr_half.at[block, pl.ds(0, 31)]
                    pltpu.make_async_copy(sent, sent, back_send.at[block, kind]).wait()

                @pl.when(jnp.logical_not(active))
                def _():
                    sent = tr_half.at[block, pl.ds(0, 32)]
                    pltpu.make_async_copy(sent, sent, back_send.at[block, kind]).wait()

    for index in range(5):
        weight_copy(index).wait_send()
    pl.when(sec == 0)(single_copy.wait_send)
    for kind in (FULL, HALF):
        given = zlast.at[kind]
        pltpu.make_async_copy(given, given, out_send.at[kind]).wait()
        taken = out.at[kind, 1 - sec]
        pltpu.make_async_copy(taken, taken, out_recv.at[kind]).wait()


def trunk(zin, sin, tin, tgate, tout, pin, pout, st_in, st_out):
    vmem = pl.BlockSpec(memory_space=pltpu.VMEM)
    anywhere = pl.BlockSpec(memory_space=pl.ANY)
    dma = pltpu.SemaphoreType.DMA
    return pl.pallas_call(
        trunk_kernel,
        out_shape=(
            jax.ShapeDtypeStruct((2, 2, 1024, 128), BF),
            jax.ShapeDtypeStruct((128, 384), BF),
        ),
        in_specs=[vmem] * 7 + [anywhere] * 2,
        out_specs=(vmem, vmem),
        scratch_shapes=[
            pltpu.VMEM((2, 128, 512), BF),
            pltpu.VMEM((2, 128, 128), BF),
            pltpu.VMEM((2, 128, 128), BF),
            pltpu.VMEM((2, 128, 1024), BF),
            pltpu.VMEM((2, 512, 128), BF),
            pltpu.VMEM((512, 128), BF),
            pltpu.VMEM((384, 3072), BF),
            pltpu.VMEM((1536, 384), BF),
            pltpu.VMEM((128, 384), BF),
            pltpu.VMEM((2, 1024, 128), BF),
            pltpu.VMEM((2, 1024, 128), BF),
            pltpu.VMEM((2, 1024, 128), BF),
            pltpu.VMEM((2048, 128), F32),
            pltpu.VMEM((1024, 128), BF),
            pltpu.VMEM((4, 128, 512), BF),
            pltpu.VMEM((256, 256), BF),
            pltpu.VMEM((128, 128), BF),
            pltpu.VMEM((2, 2, 128, 16, 128), BF),
            pltpu.VMEM((2, 128, 16, 128), BF),
            pltpu.VMEM((2, 32, 16, 128), BF),
            pltpu.VMEM((256, 512), BF),
            pltpu.VMEM((256, 512), BF),
            pltpu.VMEM((2, 2, 4, 64, 512), BF),
            pltpu.VMEM((128, 256), BF),
            pltpu.VMEM((128, 256), BF),
            pltpu.VMEM((2, 2, 2, 64, 256), BF),
            pltpu.VMEM((2, 16, 8, 8, 128), BF),
            pltpu.VMEM((2, 8, 4, 8, 128), BF),
            pltpu.VMEM((2, 128, 8, 128), BF),
            pltpu.VMEM((2, 128, 8, 128), BF),
            dma((2, 2)),
            dma((2, 2)),
            dma((2, 2)),
            dma((2, 2)),
            dma((2, 2)),
            dma((2, 2)),
            dma((5,)),
            dma((5,)),
            dma((2,)),
            dma,
            dma,
            dma((2,)),
            dma((2,)),
        ],
        compiler_params=pltpu.CompilerParams(
            collective_id=0, has_side_effects=True, vmem_limit_bytes=56 << 20
        ),
    )(zin, sin, tin, tgate, tout, pin, pout, st_in, st_out)


def on_device(pair, single, lengths, tri_in, tri_gate, tri_out, pt_in, pt_out, st_in, st_out):
    first_full = lengths[0] > lengths[1]
    start = lax.axis_index("section") * 32
    part = lax.dynamic_slice_in_dim(pair, start, 32, 1).reshape(2, 1024, 128)
    zin = jnp.where(first_full, part, part[::-1])
    out, sout = trunk(
        zin,
        single.reshape(128, 384),
        tri_in[0], tri_gate[0], tri_out[0], pt_in[0], pt_out[0], st_in[0], st_out[0],
    )
    out = out.reshape(2, 64, 32, 128)
    out = jnp.where(first_full, out, out[::-1])
    return out[None], sout.reshape(1, 2, 64, 384)


def solution(mesh):
    section = P("section", None, None)
    in_specs = (P(None, "gr", "gc", None), P(None, "gr", None), P()) + (section,) * 7
    out_specs = (P("section", None, "gr", "gc", None), P("section", None, "gr", None))
    return jax.shard_map(
        on_device, mesh=mesh, in_specs=in_specs, out_specs=out_specs, check_vma=False
    )
```

```python
import jax
import jax.numpy as jnp
from jax import lax
from jax.experimental import pallas as pl
from jax.experimental.pallas import tpu as pltpu
from jax.sharding import PartitionSpec as P

MESH = pl.DeviceIdType.MESH
FULL, HALF = 0, 1
BF = jnp.bfloat16
F32 = jnp.float32


def dot(a, b):
    return jnp.dot(a, b, preferred_element_type=F32)


def dot_nt(a, b):
    return lax.dot_general(a, b, (((1,), (1,)), ((), ())), preferred_element_type=F32)


def sigmoid(v):
    return 0.5 + 0.5 * jnp.tanh(0.5 * v)


def norm_lanes(v):
    center = v - jnp.mean(v, axis=-1, keepdims=True)
    spread = jnp.mean(center * center, axis=-1, keepdims=True)
    return center * lax.rsqrt(spread + 1e-05)


def iota(shape, axis):
    return lax.broadcasted_iota(jnp.int32, shape, axis)


def trunk_kernel(
    lengths, pair, sin, tin, tgate, tout, pin, pout, st_in, st_out,
    out, sout,
    w_tin, w_gate, w_out, w_pin, w_pout, w_t, st_in_v, st_out_v, sin_next,
    zin, zout, normed, stage, settled, perm, order_full, order_half,
    sbuf, rbuf_full, rbuf_half, lm_full, raw_full, all_full, lm_half, raw_half, all_half,
    ts_full, ts_half, tr_full, tr_half,
    fwd_send, fwd_recv, sib_send, sib_recv, back_send, back_recv,
    met, w_send, w_recv, st_sem, single_send, single_recv, out_send, out_recv,
):
    sec, gr, gc = lax.axis_index("section"), lax.axis_index("gr"), lax.axis_index("gc")
    y, core = lax.shift_right_logical(gr, 1), lax.bitwise_and(gr, 1)
    sy = sec * 4 + y
    me = gc * 8 + sy
    me_half = gc * 4 + sec * 2 + y
    active = jnp.logical_and(y < 2, gc < 8)
    peer = {"section": 1 - sec, "gr": gr, "gc": gc}
    sibling = {"section": sec, "gr": gr + 1 - 2 * core, "gc": gc}

    def place(step):
        to_gc = lax.bitwise_and(gc + step, 15)
        to_sy = lax.bitwise_and(sy + lax.shift_right_logical(step, 4), 7)
        to_sec = lax.shift_right_logical(to_sy, 2)
        to_y = lax.bitwise_and(to_sy, 3)
        return to_gc, to_sy, {"section": to_sec, "gr": to_y * 2 + core, "gc": to_gc}

    st_copies = [
        pltpu.make_async_copy(st_in, st_in_v, st_sem.at[0]),
        pltpu.make_async_copy(st_out, st_out_v, st_sem.at[1]),
    ]
    for copy in st_copies:
        copy.start()

    barrier = pltpu.get_barrier_semaphore()

    def greet_line(semaphore):
        def greet(step, carry):
            to_gc = lax.bitwise_and(gc + step, 15)
            pl.semaphore_signal(
                semaphore, inc=1, device_id={"section": sec, "gr": gr, "gc": to_gc},
                device_id_type=MESH,
            )
            return carry

        lax.fori_loop(1, 16, greet, 0)

    pl.semaphore_signal(barrier, inc=1, device_id=sibling, device_id_type=MESH)
    for step in range(1, 8):
        pl.semaphore_signal(
            barrier, inc=1, device_id=place(step * 16)[2], device_id_type=MESH
        )
    greet_line(barrier)

    weights = [(tin, w_tin), (tgate, w_gate), (tout, w_out), (pin, w_pin), (pout, w_pout)]
    for own, held in weights:
        held[sec] = own[...]

    def weight_copy(index):
        own, held = weights[index]
        return pltpu.make_async_remote_copy(
            own, held.at[sec], w_send.at[index], w_recv.at[index],
            device_id=peer, device_id_type=MESH,
        )

    pl.semaphore_wait(barrier, 23)
    weight_copy(0).start()
    greet_line(met)

    from_lane, to_lane = iota((128, 512), 0), iota((128, 512), 1)
    for low in range(4):
        target = (from_lane >> 5) * 128 + low * 32 + (from_lane & 31)
        perm[low] = jnp.where(to_lane == target, 1.0, 0.0).astype(BF)
    o, i = iota((256, 256), 0), iota((256, 256), 1)
    source = (o & 3) * 64 + ((o >> 5) & 1) * 32 + (o >> 6) * 8 + ((o >> 2) & 7)
    order_full[...] = jnp.where(i == source, 1.0, 0.0).astype(BF)
    o, i = iota((128, 128), 0), iota((128, 128), 1)
    source = (o & 3) * 32 + ((o >> 5) & 1) * 16 + (o >> 6) * 8 + ((o >> 2) & 7)
    order_half[...] = jnp.where(i == source, 1.0, 0.0).astype(BF)

    first = jnp.where(lengths[0] > lengths[1], 0, 1)
    for kind, crop in ((FULL, first), (HALF, 1 - first)):
        for part in range(4):
            rows = pl.ds(part * 256, 256)
            z = pair[crop, pl.ds(sec * 32 + part * 8, 8)].reshape(256, 128)
            zin[kind, rows] = z
            normed[kind, rows] = norm_lanes(z.astype(F32)).astype(BF)

    pl.semaphore_wait(met, 15)

    def await_weight(block, index):
        @pl.when(sec != block)
        def _():
            held = weights[index][1].at[block]
            pltpu.make_async_copy(held, held, w_recv.at[index]).wait()

    def project(block, kind):
        for part in range(4):
            rows = pl.ds(part * 256, 256)
            p = dot_nt(w_t[...], normed[kind, rows])
            left = sigmoid(p[0:128]) * p[128:256]
            right = sigmoid(p[256:384]) * p[384:512]
            for sub in range(2):
                cols = slice(sub * 128, sub * 128 + 128)
                stage[pl.ds(part * 2 + sub, 128, stride=16), :] = left[:, cols]
                stage[pl.ds(8 + part * 2 + sub, 128, stride=16), :] = right[:, cols]
        for part in range(8):
            values = stage[part * 256 : part * 256 + 256, :].astype(BF)
            sbuf[block, kind, part * 16 : part * 16 + 16] = values.reshape(16, 16, 128)

    def send_forward(block, kind):
        rbuf, slot = (rbuf_full, me) if kind == FULL else (rbuf_half, me_half)

        def send(step, carry):
            to_gc, to_sy, device = place(step)
            pltpu.make_async_remote_copy(
                sbuf.at[block, kind, to_gc * 8 + to_sy], rbuf.at[block, slot],
                fwd_send.at[block, kind], fwd_recv.at[block, kind],
                device_id=device, device_id_type=MESH,
            ).start()
            return carry

        lax.fori_loop(1, 128, send, 0)
        pltpu.make_async_copy(
            sbuf.at[block, kind, me], rbuf.at[block, slot], fwd_recv.at[block, kind]
        ).start()

    def forward(block, kind):
        if kind == FULL:
            project(block, kind)
            send_forward(block, kind)
        else:

            @pl.when(active)
            def _():
                project(block, kind)
                send_forward(block, kind)

    def triangle(block, kind):
        full = kind == FULL
        rbuf, lm, raw, whole, ts, order, groups, tiles = (
            (rbuf_full, lm_full, raw_full, all_full, ts_full, order_full, 4, 8)
            if full
            else (rbuf_half, lm_half, raw_half, all_half, ts_half, order_half, 2, 4)
        )
        depth = groups * 128
        rows = tiles * 8
        landed = rbuf.at[block]
        pltpu.make_async_copy(landed, landed, fwd_recv.at[block, kind]).wait()
        for g in range(groups):
            total = None
            for low in range(4):
                col = g * 4 + low
                block_in = rbuf[block, col * tiles : (col + 1) * tiles].reshape(tiles * 16, 128)
                term = dot(block_in, perm[low])
                total = term if total is None else total + term
            total = total.reshape(tiles, 16, 512)
            left = total[:, 0:8].reshape(rows, 512).astype(BF)
            right = total[:, 8:16].reshape(rows, 512).astype(BF)
            for low in range(4):
                cols = slice(low * 128, low * 128 + 128)
                lm[low * rows : (low + 1) * rows, g * 128 : g * 128 + 128] = left[:, cols]
                raw[low * rows : (low + 1) * rows, g * 128 : g * 128 + 128] = right[:, cols]
        ordered = dot(order[...], raw[...]).astype(BF)
        whole[block, core] = ordered.reshape(tiles // 2, 64, depth)
        mine = whole.at[block, core]
        pltpu.make_async_remote_copy(
            mine, mine, sib_send.at[block, kind], sib_recv.at[block, kind],
            device_id=sibling, device_id_type=MESH,
        ).start()
        other = whole.at[block, 1 - core]
        pltpu.make_async_copy(other, other, sib_recv.at[block, kind]).wait()
        for g in range(groups):
            right = jnp.concatenate(
                [whole[block, 0, g], whole[block, 1, g]], axis=0
            )
            product = dot_nt(lm[...], right).astype(BF)
            total = None
            for low in range(4):
                term = dot(product[low * rows : (low + 1) * rows], perm[low])
                total = term if total is None else total + term
            total = total.astype(BF)
            for low in range(4):
                ts[block, g * 4 + low] = total[:, low * 128 : low * 128 + 128].reshape(
                    tiles, 8, 128
                )

    def send_back(block, kind):
        if kind == FULL:

            def send(step, carry):
                to_gc, to_sy, device = place(step)
                pltpu.make_async_remote_copy(
                    ts_full.at[block, to_gc, to_sy], tr_full.at[block, me],
                    back_send.at[block, kind], back_recv.at[block, kind],
                    device_id=device, device_id_type=MESH,
                ).start()
                return carry

            lax.fori_loop(1, 128, send, 0)
            pltpu.make_async_copy(
                ts_full.at[block, gc, sy], tr_full.at[block, me], back_recv.at[block, kind]
            ).start()
        else:

            def send(step, carry):
                to_gc = lax.bitwise_and(gc + step, 7)
                to_q = lax.bitwise_and(sec * 2 + y + lax.shift_right_logical(step, 3), 3)
                to_sec, to_y = lax.shift_right_logical(to_q, 1), lax.bitwise_and(to_q, 1)
                itself = jnp.logical_and(
                    to_gc == gc, jnp.logical_and(to_sec == sec, to_y == y)
                )

                @pl.when(itself)
                def _():
                    pltpu.make_async_copy(
                        ts_half.at[block, to_gc, to_q], tr_half.at[block, me],
                        back_recv.at[block, kind],
                    ).start()

                @pl.when(jnp.logical_not(itself))
                def _():
                    pltpu.make_async_remote_copy(
                        ts_half.at[block, to_gc, to_q], tr_half.at[block, me],
                        back_send.at[block, kind], back_recv.at[block, kind],
                        device_id={"section": to_sec, "gr": to_y * 2 + core, "gc": to_gc},
                        device_id_type=MESH,
                    ).start()

                return carry

            lax.fori_loop(0, 32, send, 0)

    def finish(block, kind):
        z = zin if block == 0 else zout.at[0]
        tr = tr_full if kind == FULL else tr_half
        landed = tr.at[block]
        if kind == FULL:
            pltpu.make_async_copy(landed, landed, back_recv.at[block, kind]).wait()
        else:

            @pl.when(active)
            def _():
                pltpu.make_async_copy(landed, landed, back_recv.at[block, kind]).wait()

            @pl.when(jnp.logical_not(active))
            def _():
                tr[block] = jnp.zeros((128, 8, 128), BF)

        values = tr[block].astype(F32)
        center = values - jnp.mean(values, axis=0, keepdims=True)
        spread = jnp.mean(center * center, axis=0, keepdims=True)
        center = center * lax.rsqrt(spread + 1e-05)
        stage[0:1024, :] = center.reshape(1024, 128)
        for r in range(8):
            tile = stage[pl.ds(r, 128, stride=8), :]
            settled[r * 128 : r * 128 + 128] = tile.T.astype(BF)
        for part in range(4):
            rows = pl.ds(part * 256, 256)
            gate = sigmoid(dot(normed[kind, rows], w_gate[block]))
            update = dot(settled[rows], w_out[block])
            updated = (z[kind, rows].astype(F32) + gate * update).astype(BF)
            updated = updated.astype(F32)
            trans_in = norm_lanes(updated).astype(BF)
            gates = dot(trans_in, w_pin[block, :, 0:512])
            ups = dot(trans_in, w_pin[block, :, 512:1024])
            inner = (gates * sigmoid(gates) * ups).astype(BF)
            done = (updated + dot(inner, w_pout[block])).astype(BF)
            zout[block, kind, rows] = done
            if block == 0:
                normed[kind, rows] = norm_lanes(done.astype(F32)).astype(BF)
            else:
                deliver(block, kind, part, 1)

    def deliver(block, kind, part=0, parts=4):
        rows = pl.ds(part * 256, parts * 256)

        @pl.when(sec == block)
        def _():
            out[kind, sec, rows] = zout[block, kind, rows]

        @pl.when(sec != block)
        def _():
            pltpu.make_async_remote_copy(
                zout.at[block, kind, rows], out.at[kind, sec, rows],
                out_send.at[kind], out_recv.at[kind],
                device_id=peer, device_id_type=MESH,
            ).start()

    def single(rows_in):
        value = rows_in[...].astype(F32)
        value_in = norm_lanes(value).astype(BF)
        total = value
        for part in range(6):
            cols = part * 256
            gates = dot(value_in, st_in_v[:, cols : cols + 256])
            ups = dot(value_in, st_in_v[:, 1536 + cols : 1536 + cols + 256])
            inner = (gates * sigmoid(gates) * ups).astype(BF)
            total = total + dot(inner, st_out_v[cols : cols + 256])
        sout[...] = total.astype(BF)

    single_copy = pltpu.make_async_remote_copy(
        sout, sin_next, single_send, single_recv, device_id=peer, device_id_type=MESH
    )

    def start_block(block):
        await_weight(block, 0)
        w_t[...] = w_tin[block].astype(F32).T.astype(BF)

    def more_weights():
        for index in range(1, 5):
            weight_copy(index).start()

    def rest_weights(block):
        for index in range(1, 5):
            await_weight(block, index)

    def single_turn(block):
        @pl.when(sec == block)
        def _():
            for copy in st_copies:
                copy.wait()
            if block == 0:
                single(sin)
                single_copy.start()
            else:
                single_copy.wait_recv()
                single(sin_next)

    start_block(0)
    forward(0, FULL)
    more_weights()
    forward(0, HALF)
    single_turn(0)
    triangle(0, FULL)
    send_back(0, FULL)
    triangle(0, HALF)
    send_back(0, HALF)
    rest_weights(0)
    finish(0, FULL)
    start_block(1)
    forward(1, FULL)
    deliver(0, FULL)
    finish(0, HALF)
    forward(1, HALF)
    deliver(0, HALF)
    single_turn(1)
    triangle(1, FULL)
    send_back(1, FULL)
    triangle(1, HALF)
    send_back(1, HALF)
    rest_weights(1)
    finish(1, FULL)
    finish(1, HALF)

    def end_forward(block, kind):
        sent = rbuf_full.at[block, pl.ds(0, 127)]
        copy = pltpu.make_async_copy(sent, sent, fwd_send.at[block, kind])
        if kind == FULL:
            copy.wait()
        else:
            pl.when(active)(copy.wait)

    def end_triangle(block, kind):
        mine = (all_full if kind == FULL else all_half).at[block, core]
        pltpu.make_async_copy(mine, mine, sib_send.at[block, kind]).wait()

    def end_back(block, kind):
        def wait(count):
            sent = tr_full.at[block, pl.ds(0, count)]
            pltpu.make_async_copy(sent, sent, back_send.at[block, kind]).wait()

        if kind == FULL:
            wait(127)
        else:
            pl.when(active)(lambda: wait(31))
            pl.when(jnp.logical_not(active))(lambda: wait(32))

    def end_rest():
        for index in range(5):
            weight_copy(index).wait_send()
        pl.when(sec == 0)(single_copy.wait_send)

    def end_deliver(kind):
        given = zout.at[0, kind]
        pltpu.make_async_copy(given, given, out_send.at[kind]).wait()
        taken = out.at[kind, 1 - sec]
        pltpu.make_async_copy(taken, taken, out_recv.at[kind]).wait()

    for block in range(2):
        for kind in (FULL, HALF):
            end_forward(block, kind)
            end_triangle(block, kind)
            end_back(block, kind)
    end_rest()
    end_deliver(FULL)
    end_deliver(HALF)


def trunk(lengths, pair, sin, tin, tgate, tout, pin, pout, st_in, st_out):
    vmem = pl.BlockSpec(memory_space=pltpu.VMEM)
    anywhere = pl.BlockSpec(memory_space=pl.ANY)
    dma = pltpu.SemaphoreType.DMA
    return pl.pallas_call(
        trunk_kernel,
        out_shape=(
            jax.ShapeDtypeStruct((2, 2, 1024, 128), BF),
            jax.ShapeDtypeStruct((128, 384), BF),
        ),
        in_specs=[pl.BlockSpec(memory_space=pltpu.SMEM)] + [vmem] * 7 + [anywhere] * 2,
        out_specs=(vmem, vmem),
        scratch_shapes=[
            pltpu.VMEM((2, 128, 512), BF),
            pltpu.VMEM((2, 128, 128), BF),
            pltpu.VMEM((2, 128, 128), BF),
            pltpu.VMEM((2, 128, 1024), BF),
            pltpu.VMEM((2, 512, 128), BF),
            pltpu.VMEM((512, 128), BF),
            pltpu.VMEM((384, 3072), BF),
            pltpu.VMEM((1536, 384), BF),
            pltpu.VMEM((128, 384), BF),
            pltpu.VMEM((2, 1024, 128), BF),
            pltpu.VMEM((2, 2, 1024, 128), BF),
            pltpu.VMEM((2, 1024, 128), BF),
            pltpu.VMEM((2048, 128), F32),
            pltpu.VMEM((1024, 128), BF),
            pltpu.VMEM((4, 128, 512), BF),
            pltpu.VMEM((256, 256), BF),
            pltpu.VMEM((128, 128), BF),
            pltpu.VMEM((2, 2, 128, 16, 128), BF),
            pltpu.VMEM((2, 128, 16, 128), BF),
            pltpu.VMEM((2, 32, 16, 128), BF),
            pltpu.VMEM((256, 512), BF),
            pltpu.VMEM((256, 512), BF),
            pltpu.VMEM((2, 2, 4, 64, 512), BF),
            pltpu.VMEM((128, 256), BF),
            pltpu.VMEM((128, 256), BF),
            pltpu.VMEM((2, 2, 2, 64, 256), BF),
            pltpu.VMEM((2, 16, 8, 8, 128), BF),
            pltpu.VMEM((2, 8, 4, 8, 128), BF),
            pltpu.VMEM((2, 128, 8, 128), BF),
            pltpu.VMEM((2, 128, 8, 128), BF),
            dma((2, 2)),
            dma((2, 2)),
            dma((2, 2)),
            dma((2, 2)),
            dma((2, 2)),
            dma((2, 2)),
            pltpu.SemaphoreType.REGULAR,
            dma((5,)),
            dma((5,)),
            dma((2,)),
            dma,
            dma,
            dma((2,)),
            dma((2,)),
        ],
        compiler_params=pltpu.CompilerParams(
            collective_id=0, has_side_effects=True, vmem_limit_bytes=56 << 20
        ),
    )(lengths, pair, sin, tin, tgate, tout, pin, pout, st_in, st_out)


def restore_kernel(lengths, staged, staged_single, out, sout, sems):
    first = jnp.where(lengths[0] > lengths[1], 0, 1)
    copies = [
        pltpu.make_async_copy(staged.at[micro ^ first, half], out.at[0, micro, half], sems.at[micro, half])
        for micro in range(2)
        for half in range(2)
    ]
    copies.append(pltpu.make_async_copy(staged_single, sout, sems.at[2, 0]))
    for copy in copies:
        copy.start()
    for copy in copies:
        copy.wait()


def restore(lengths, staged, staged_single):
    anywhere = pl.BlockSpec(memory_space=pl.ANY)
    return pl.pallas_call(
        restore_kernel,
        out_shape=(
            jax.ShapeDtypeStruct((1, 2, 2, 1024, 128), BF),
            jax.ShapeDtypeStruct((128, 384), BF),
        ),
        in_specs=[pl.BlockSpec(memory_space=pltpu.SMEM), anywhere, anywhere],
        out_specs=(anywhere, anywhere),
        scratch_shapes=[pltpu.SemaphoreType.DMA((3, 2))],
    )(lengths, staged, staged_single)


def on_device(pair, single, lengths, tri_in, tri_gate, tri_out, pt_in, pt_out, st_in, st_out):
    staged, staged_single = trunk(
        lengths,
        pair,
        single.reshape(128, 384),
        tri_in[0], tri_gate[0], tri_out[0], pt_in[0], pt_out[0], st_in[0], st_out[0],
    )
    out, sout = restore(lengths, staged, staged_single)
    return out.reshape(1, 2, 64, 32, 128), sout.reshape(1, 2, 64, 384)


def solution(mesh):
    section = P("section", None, None)
    in_specs = (P(None, "gr", "gc", None), P(None, "gr", None), P()) + (section,) * 7
    out_specs = (P("section", None, "gr", "gc", None), P("section", None, "gr", None))
    return jax.shard_map(
        on_device, mesh=mesh, in_specs=in_specs, out_specs=out_specs, check_vma=False
    )
```

```python
import jax
import jax.numpy as jnp
from jax import lax
from jax.experimental import pallas as pl
from jax.experimental.pallas import tpu as pltpu
from jax.sharding import PartitionSpec as P

MESH = pl.DeviceIdType.MESH
FULL, HALF = 0, 1
BF = jnp.bfloat16
F32 = jnp.float32


def dot(a, b):
    return jnp.dot(a, b, preferred_element_type=F32)


def dot_nt(a, b):
    return lax.dot_general(a, b, (((1,), (1,)), ((), ())), preferred_element_type=F32)


def sigmoid(v):
    return 0.5 + 0.5 * jnp.tanh(0.5 * v)


def norm_lanes(v):
    center = v - jnp.mean(v, axis=-1, keepdims=True)
    spread = jnp.mean(center * center, axis=-1, keepdims=True)
    return center * lax.rsqrt(spread + 1e-05)


def norm_pair(v, mean_of):
    center = v.astype(F32) - dot(v, mean_of)
    spread = dot((center * center).astype(BF), mean_of)
    return (center * lax.rsqrt(spread + 1e-05)).astype(BF)


def silu_times(gates, ups):
    half = 0.5 * gates
    return ((half + half * jnp.tanh(half)) * ups).astype(BF)


def iota(shape, axis):
    return lax.broadcasted_iota(jnp.int32, shape, axis)


def trunk_kernel(
    lengths, pair, sin, tin, tgate, tout, pin, pout, st_in, st_out,
    out, sout,
    w_tin, w_gate, w_out, w_pin, w_pout, w_t, st_in_v, st_out_v, sin_next,
    zin, zout, normed, stage, settled, perm, order_full, order_half,
    sbuf, rbuf_full, rbuf_half, lm_full, raw_full, all_full, lm_half, raw_half, all_half,
    ts_full, ts_half, tr_full, tr_half,
    relayed, relay_send, relay_recv, fwd_send, fwd_recv, sib_send, sib_recv, back_send, back_recv,
    met, w_send, w_recv, st_sem, single_send, single_recv, out_send, out_recv,
):
    sec, gr, gc = lax.axis_index("section"), lax.axis_index("gr"), lax.axis_index("gc")
    y, core = lax.shift_right_logical(gr, 1), lax.bitwise_and(gr, 1)
    sy = sec * 4 + y
    x_hi, z_at = lax.shift_right_logical(gc, 3), lax.bitwise_and(gc, 7)
    plane = x_hi * 8 + sy
    channel = plane * 8 + z_at
    slot = gc * 8 + sy
    active = jnp.logical_and(y < 2, gc < 8)
    peer = {"section": 1 - sec, "gr": gr, "gc": gc}
    sibling = {"section": sec, "gr": gr + 1 - 2 * core, "gc": gc}

    def place(step):
        to_gc = lax.bitwise_and(gc + step, 15)
        to_sy = lax.bitwise_and(sy + lax.shift_right_logical(step, 4), 7)
        to_sec = lax.shift_right_logical(to_sy, 2)
        to_y = lax.bitwise_and(to_sy, 3)
        return to_gc, to_sy, {"section": to_sec, "gr": to_y * 2 + core, "gc": to_gc}

    def channel_of(at_gc, at_sy):
        at_plane = lax.shift_right_logical(at_gc, 3) * 8 + at_sy
        return at_plane * 8 + lax.bitwise_and(at_gc, 7)

    st_copies = [
        pltpu.make_async_copy(st_in, st_in_v, st_sem.at[0]),
        pltpu.make_async_copy(st_out, st_out_v, st_sem.at[1]),
    ]
    for copy in st_copies:
        copy.start()

    barrier = pltpu.get_barrier_semaphore()

    def greet_line(semaphore):
        def greet(step, carry):
            to_gc = lax.bitwise_and(gc + step, 15)
            pl.semaphore_signal(
                semaphore, inc=1, device_id={"section": sec, "gr": gr, "gc": to_gc},
                device_id_type=MESH,
            )
            return carry

        lax.fori_loop(1, 16, greet, 0)

    pl.semaphore_signal(barrier, inc=1, device_id=sibling, device_id_type=MESH)
    for step in range(1, 8):
        pl.semaphore_signal(
            barrier, inc=1, device_id=place(step * 16)[2], device_id_type=MESH
        )
    greet_line(barrier)

    weights = [(tin, w_tin), (tgate, w_gate), (tout, w_out), (pin, w_pin), (pout, w_pout)]
    for own, held in weights:
        held[sec] = own[...]

    def weight_copy(index):
        own, held = weights[index]
        return pltpu.make_async_remote_copy(
            own, held.at[sec], w_send.at[index], w_recv.at[index],
            device_id=peer, device_id_type=MESH,
        )

    pl.semaphore_wait(barrier, 23)
    weight_copy(0).start()
    greet_line(met)

    from_lane, to_lane = iota((128, 512), 0), iota((128, 512), 1)
    for low in range(4):
        target = (from_lane >> 5) * 128 + low * 32 + (from_lane & 31)
        perm[low] = jnp.where(to_lane == target, 1.0, 0.0).astype(BF)
    o, i = iota((256, 256), 0), iota((256, 256), 1)
    source = (o & 3) * 64 + ((o >> 5) & 1) * 32 + (o >> 6) * 8 + ((o >> 2) & 7)
    order_full[...] = jnp.where(i == source, 1.0, 0.0).astype(BF)
    o, i = iota((128, 128), 0), iota((128, 128), 1)
    source = (o & 3) * 32 + ((o >> 5) & 1) * 16 + (o >> 6) * 8 + ((o >> 2) & 7)
    order_half[...] = jnp.where(i == source, 1.0, 0.0).astype(BF)

    mean_of = jnp.full((128, 128), 1 / 128, BF)
    first = jnp.where(lengths[0] > lengths[1], 0, 1)
    for kind, crop in ((FULL, first), (HALF, 1 - first)):
        for part in range(4):
            rows = pl.ds(part * 256, 256)
            z = pair[crop, pl.ds(sec * 32 + part * 8, 8)].reshape(256, 128)
            zin[kind, rows] = z
            normed[kind, rows] = norm_pair(z, mean_of)

    pl.semaphore_wait(met, 15)

    def await_weight(block, index):
        @pl.when(sec != block)
        def _():
            held = weights[index][1].at[block]
            pltpu.make_async_copy(held, held, w_recv.at[index]).wait()

    def project(block, kind):
        for part in range(4):
            rows = pl.ds(part * 256, 256)
            p = dot_nt(w_t[...], normed[kind, rows])
            left = sigmoid(p[0:128]) * p[128:256]
            right = sigmoid(p[256:384]) * p[384:512]
            for sub in range(2):
                cols = slice(sub * 128, sub * 128 + 128)
                stage[pl.ds(part * 2 + sub, 128, stride=16), :] = left[:, cols]
                stage[pl.ds(8 + part * 2 + sub, 128, stride=16), :] = right[:, cols]
        for part in range(8):
            values = stage[part * 256 : part * 256 + 256, :].astype(BF)
            sbuf[block, kind, part * 16 : part * 16 + 16] = values.reshape(16, 16, 128)

    def send_full(block, begin, end):
        def send(step, carry):
            to_gc, to_sy, device = place(step)
            pltpu.make_async_remote_copy(
                sbuf.at[block, FULL, channel_of(to_gc, to_sy)], rbuf_full.at[block, slot],
                fwd_send.at[block, FULL], fwd_recv.at[block, FULL],
                device_id=device, device_id_type=MESH,
            ).start()
            return carry

        lax.fori_loop(begin, end, send, 0)
        if begin == 1:
            pltpu.make_async_copy(
                sbuf.at[block, FULL, channel], rbuf_full.at[block, slot],
                fwd_recv.at[block, FULL],
            ).start()

    def send_half(block):
        source = sec * 2 + y
        for step in range(1, 16):
            to_plane = lax.bitwise_and(plane + step, 15)
            to_sy = lax.bitwise_and(to_plane, 7)
            pltpu.make_async_remote_copy(
                sbuf.at[block, HALF, pl.ds(to_plane * 8, 8)], relayed.at[block, source],
                relay_send.at[block], relay_recv.at[block],
                device_id={
                    "section": lax.shift_right_logical(to_sy, 2),
                    "gr": lax.bitwise_and(to_sy, 3) * 2 + core,
                    "gc": lax.shift_right_logical(to_plane, 3) * 8 + z_at,
                },
                device_id_type=MESH,
            ).start()
        pltpu.make_async_copy(
            sbuf.at[block, HALF, pl.ds(plane * 8, 8)], relayed.at[block, source],
            relay_recv.at[block],
        ).start()

    def relay(block):
        landed = relayed.at[block]
        pltpu.make_async_copy(landed, landed, relay_recv.at[block]).wait()
        at = rbuf_half.at[block, pl.ds(z_at * 4, 4)]
        for step in range(1, 8):
            to_z = lax.bitwise_and(z_at + step, 7)
            pltpu.make_async_remote_copy(
                relayed.at[block, :, to_z], at, fwd_send.at[block, HALF], fwd_recv.at[block, HALF],
                device_id={"section": sec, "gr": gr, "gc": x_hi * 8 + to_z},
                device_id_type=MESH,
            ).start()
        pltpu.make_async_copy(relayed.at[block, :, z_at], at, fwd_recv.at[block, HALF]).start()

    def forward(block, kind):
        if kind == FULL:
            project(block, FULL)
            send_full(block, 1, 64)
            relay(block)
            send_full(block, 64, 128)
        else:

            @pl.when(active)
            def _():
                project(block, HALF)
                send_half(block)

    def parts_of(kind):
        if kind == FULL:
            return rbuf_full, lm_full, raw_full, all_full, ts_full, tr_full, order_full, 4, 8
        return rbuf_half, lm_half, raw_half, all_half, ts_half, tr_half, order_half, 2, 4

    def triangle_in(block, kind):
        rbuf, lm, raw, whole, ts, tr, order, groups, tiles = parts_of(kind)
        rows = tiles * 8
        landed = rbuf.at[block]
        pltpu.make_async_copy(landed, landed, fwd_recv.at[block, kind]).wait()
        for g in range(groups):
            total = None
            for low in range(4):
                col = g * 4 + low
                block_in = rbuf[block, col * tiles : (col + 1) * tiles].reshape(tiles * 16, 128)
                term = dot(block_in, perm[low])
                total = term if total is None else total + term
            total = total.reshape(tiles, 16, 512)
            left = total[:, 0:8].reshape(rows, 512).astype(BF)
            right = total[:, 8:16].reshape(rows, 512).astype(BF)
            lanes = slice(g * 128, g * 128 + 128)
            for low in range(4):
                cols = slice(low * 128, low * 128 + 128)
                lm[low * rows : (low + 1) * rows, lanes] = left[:, cols]
                raw[low * rows : (low + 1) * rows, lanes] = right[:, cols]
            ordered = dot(order[...], raw[:, lanes]).astype(BF)
            whole[block, core, :, :, lanes] = ordered.reshape(tiles // 2, 64, 128)
            mine = whole.at[block, core, :, :, lanes]
            pltpu.make_async_remote_copy(
                mine, mine, sib_send.at[block, kind], sib_recv.at[block, kind],
                device_id=sibling, device_id_type=MESH,
            ).start()

    def triangle_out(block, kind):
        rbuf, lm, raw, whole, ts, tr, order, groups, tiles = parts_of(kind)
        rows = tiles * 8
        full = kind == FULL
        other = whole.at[block, 1 - core]
        pltpu.make_async_copy(other, other, sib_recv.at[block, kind]).wait()
        home = lax.bitwise_and(lax.shift_right_logical(gc, 2), groups - 1)
        source = sy if full else sec * 2 + y

        for turn in range(groups):
            g = lax.bitwise_and(home + turn, groups - 1)
            right = jnp.concatenate([whole[block, 0, g], whole[block, 1, g]], axis=0)
            product = dot_nt(lm[...], right).astype(BF)
            total = None
            for low in range(4):
                term = dot(product[low * rows : (low + 1) * rows], perm[low])
                total = term if total is None else total + term
            total = total.astype(BF)
            for low in range(4):
                ts[block, g * 4 + low] = total[:, low * 128 : low * 128 + 128].reshape(
                    tiles, 8, 128
                )

            def send(step, carry):
                to_gc = g * 4 + lax.bitwise_and(gc + step, 3)
                to_tile = lax.bitwise_and(source + lax.shift_right_logical(step, 2), tiles - 1)
                to_sec = lax.shift_right_logical(to_tile, 2 if full else 1)
                to_y = lax.bitwise_and(to_tile, tiles // 2 - 1)

                def local():
                    pltpu.make_async_copy(
                        ts.at[block, to_gc, to_tile], tr.at[block, channel],
                        back_recv.at[block, kind],
                    ).start()

                def remote():
                    pltpu.make_async_remote_copy(
                        ts.at[block, to_gc, to_tile], tr.at[block, channel],
                        back_send.at[block, kind], back_recv.at[block, kind],
                        device_id={"section": to_sec, "gr": to_y * 2 + core, "gc": to_gc},
                        device_id_type=MESH,
                    ).start()

                if turn == 0:
                    itself = step == 0
                    if not full:
                        itself = jnp.logical_and(itself, active)
                    pl.when(itself)(local)
                    pl.when(jnp.logical_not(itself))(remote)
                else:
                    remote()
                return carry

            lax.fori_loop(0, tiles * 4, send, 0)

    def finish(block, kind):
        z = zin if block == 0 else zout.at[0]
        tr = tr_full if kind == FULL else tr_half
        landed = tr.at[block]
        if kind == FULL:
            pltpu.make_async_copy(landed, landed, back_recv.at[block, kind]).wait()
        else:

            @pl.when(active)
            def _():
                pltpu.make_async_copy(landed, landed, back_recv.at[block, kind]).wait()

            @pl.when(jnp.logical_not(active))
            def _():
                tr[block] = jnp.zeros((128, 8, 128), BF)

        values = tr[block].astype(F32)
        center = values - jnp.mean(values, axis=0, keepdims=True)
        spread = jnp.mean(center * center, axis=0, keepdims=True)
        center = center * lax.rsqrt(spread + 1e-05)
        stage[0:1024, :] = center.reshape(1024, 128)
        for r in range(8):
            tile = stage[pl.ds(r, 128, stride=8), :]
            settled[r * 128 : r * 128 + 128] = tile.astype(BF).T
        for part in range(4):
            rows = pl.ds(part * 256, 256)
            gate = sigmoid(dot(normed[kind, rows], w_gate[block]))
            update = dot(settled[rows], w_out[block])
            updated = (z[kind, rows].astype(F32) + gate * update).astype(BF)
            trans_in = norm_pair(updated, mean_of)
            gates = dot(trans_in, w_pin[block, :, 0:512])
            ups = dot(trans_in, w_pin[block, :, 512:1024])
            inner = silu_times(gates, ups)
            done = (updated.astype(F32) + dot(inner, w_pout[block])).astype(BF)
            zout[block, kind, rows] = done
            if block == 0:
                normed[kind, rows] = norm_pair(done, mean_of)
            else:
                deliver(block, kind, part, 1)

    def deliver(block, kind, part=0, parts=4):
        rows = pl.ds(part * 256, parts * 256)

        @pl.when(sec == block)
        def _():
            out[kind, sec, rows] = zout[block, kind, rows]

        @pl.when(sec != block)
        def _():
            pltpu.make_async_remote_copy(
                zout.at[block, kind, rows], out.at[kind, sec, rows],
                out_send.at[kind], out_recv.at[kind],
                device_id=peer, device_id_type=MESH,
            ).start()

    def single(rows_in):
        value = rows_in[...].astype(F32)
        value_in = norm_lanes(value).astype(BF)
        total = value
        for part in range(6):
            cols = part * 256
            gates = dot(value_in, st_in_v[:, cols : cols + 256])
            ups = dot(value_in, st_in_v[:, 1536 + cols : 1536 + cols + 256])
            inner = silu_times(gates, ups)
            total = total + dot(inner, st_out_v[cols : cols + 256])
        sout[...] = total.astype(BF)

    single_copy = pltpu.make_async_remote_copy(
        sout, sin_next, single_send, single_recv, device_id=peer, device_id_type=MESH
    )

    def start_block(block):
        await_weight(block, 0)
        w_t[...] = w_tin[block].astype(F32).T.astype(BF)

    def more_weights():
        for index in range(1, 5):
            weight_copy(index).start()

    def rest_weights(block):
        for index in range(1, 5):
            await_weight(block, index)

    def single_turn(block):
        @pl.when(sec == block)
        def _():
            for copy in st_copies:
                copy.wait()
            if block == 0:
                single(sin)
                single_copy.start()
            else:
                single_copy.wait_recv()
                single(sin_next)

    start_block(0)
    forward(0, HALF)
    forward(0, FULL)
    more_weights()
    single_turn(0)
    triangle_in(0, HALF)
    triangle_out(0, HALF)
    triangle_in(0, FULL)
    triangle_out(0, FULL)
    rest_weights(0)
    finish(0, HALF)
    start_block(1)
    forward(1, HALF)
    finish(0, FULL)
    forward(1, FULL)
    deliver(0, HALF)
    deliver(0, FULL)
    single_turn(1)
    triangle_in(1, HALF)
    triangle_out(1, HALF)
    triangle_in(1, FULL)
    triangle_out(1, FULL)
    rest_weights(1)
    finish(1, HALF)
    finish(1, FULL)

    def end_forward(block, kind):
        sent = rbuf_full.at[block, pl.ds(0, 127 if kind == FULL else 28)]
        pltpu.make_async_copy(sent, sent, fwd_send.at[block, kind]).wait()
        if kind == HALF:
            sent = sbuf.at[block, HALF, pl.ds(0, 120)]
            pl.when(active)(pltpu.make_async_copy(sent, sent, relay_send.at[block]).wait)

    def end_triangle(block, kind):
        mine = (all_full if kind == FULL else all_half).at[block, core]
        pltpu.make_async_copy(mine, mine, sib_send.at[block, kind]).wait()

    def end_back(block, kind):
        def wait(count):
            sent = tr_full.at[block, pl.ds(0, count)]
            pltpu.make_async_copy(sent, sent, back_send.at[block, kind]).wait()

        if kind == FULL:
            wait(127)
        else:
            pl.when(active)(lambda: wait(31))
            pl.when(jnp.logical_not(active))(lambda: wait(32))

    def end_rest():
        for index in range(5):
            weight_copy(index).wait_send()
        pl.when(sec == 0)(single_copy.wait_send)

    def end_deliver(kind):
        given = zout.at[0, kind]
        pltpu.make_async_copy(given, given, out_send.at[kind]).wait()
        taken = out.at[kind, 1 - sec]
        pltpu.make_async_copy(taken, taken, out_recv.at[kind]).wait()

    for block in range(2):
        for kind in (FULL, HALF):
            end_forward(block, kind)
            end_triangle(block, kind)
            end_back(block, kind)
    end_rest()
    end_deliver(FULL)
    end_deliver(HALF)


def trunk(lengths, pair, sin, tin, tgate, tout, pin, pout, st_in, st_out):
    vmem = pl.BlockSpec(memory_space=pltpu.VMEM)
    anywhere = pl.BlockSpec(memory_space=pl.ANY)
    dma = pltpu.SemaphoreType.DMA
    return pl.pallas_call(
        trunk_kernel,
        out_shape=(
            jax.ShapeDtypeStruct((2, 2, 1024, 128), BF),
            jax.ShapeDtypeStruct((128, 384), BF),
        ),
        in_specs=[pl.BlockSpec(memory_space=pltpu.SMEM)] + [vmem] * 7 + [anywhere] * 2,
        out_specs=(vmem, vmem),
        scratch_shapes=[
            pltpu.VMEM((2, 128, 512), BF),
            pltpu.VMEM((2, 128, 128), BF),
            pltpu.VMEM((2, 128, 128), BF),
            pltpu.VMEM((2, 128, 1024), BF),
            pltpu.VMEM((2, 512, 128), BF),
            pltpu.VMEM((512, 128), BF),
            pltpu.VMEM((384, 3072), BF),
            pltpu.VMEM((1536, 384), BF),
            pltpu.VMEM((128, 384), BF),
            pltpu.VMEM((2, 1024, 128), BF),
            pltpu.VMEM((2, 2, 1024, 128), BF),
            pltpu.VMEM((2, 1024, 128), BF),
            pltpu.VMEM((2048, 128), F32),
            pltpu.VMEM((1024, 128), BF),
            pltpu.VMEM((4, 128, 512), BF),
            pltpu.VMEM((256, 256), BF),
            pltpu.VMEM((128, 128), BF),
            pltpu.VMEM((2, 2, 128, 16, 128), BF),
            pltpu.VMEM((2, 128, 16, 128), BF),
            pltpu.VMEM((2, 32, 16, 128), BF),
            pltpu.VMEM((256, 512), BF),
            pltpu.VMEM((256, 512), BF),
            pltpu.VMEM((2, 2, 4, 64, 512), BF),
            pltpu.VMEM((128, 256), BF),
            pltpu.VMEM((128, 256), BF),
            pltpu.VMEM((2, 2, 2, 64, 256), BF),
            pltpu.VMEM((2, 16, 8, 8, 128), BF),
            pltpu.VMEM((2, 8, 4, 8, 128), BF),
            pltpu.VMEM((2, 128, 8, 128), BF),
            pltpu.VMEM((2, 128, 8, 128), BF),
            pltpu.VMEM((2, 4, 8, 16, 128), BF),
            dma((2,)),
            dma((2,)),
            dma((2, 2)),
            dma((2, 2)),
            dma((2, 2)),
            dma((2, 2)),
            dma((2, 2)),
            dma((2, 2)),
            pltpu.SemaphoreType.REGULAR,
            dma((5,)),
            dma((5,)),
            dma((2,)),
            dma,
            dma,
            dma((2,)),
            dma((2,)),
        ],
        compiler_params=pltpu.CompilerParams(
            collective_id=0, has_side_effects=True, vmem_limit_bytes=56 << 20
        ),
    )(lengths, pair, sin, tin, tgate, tout, pin, pout, st_in, st_out)


def restore_kernel(lengths, staged, staged_single, out, sout, sems):
    mean_of = jnp.full((128, 128), 1 / 128, BF)
    first = jnp.where(lengths[0] > lengths[1], 0, 1)
    copies = [
        pltpu.make_async_copy(staged.at[micro ^ first, half], out.at[0, micro, half], sems.at[micro, half])
        for micro in range(2)
        for half in range(2)
    ]
    copies.append(pltpu.make_async_copy(staged_single, sout, sems.at[2, 0]))
    for copy in copies:
        copy.start()
    for copy in copies:
        copy.wait()


def restore(lengths, staged, staged_single):
    anywhere = pl.BlockSpec(memory_space=pl.ANY)
    return pl.pallas_call(
        restore_kernel,
        out_shape=(
            jax.ShapeDtypeStruct((1, 2, 2, 1024, 128), BF),
            jax.ShapeDtypeStruct((128, 384), BF),
        ),
        in_specs=[pl.BlockSpec(memory_space=pltpu.SMEM), anywhere, anywhere],
        out_specs=(pl.BlockSpec(memory_space=pltpu.VMEM),) * 2,
        scratch_shapes=[pltpu.SemaphoreType.DMA((3, 2))],
    )(lengths, staged, staged_single)


def on_device(pair, single, lengths, tri_in, tri_gate, tri_out, pt_in, pt_out, st_in, st_out):
    staged, staged_single = trunk(
        lengths,
        pair,
        single.reshape(128, 384),
        tri_in[0], tri_gate[0], tri_out[0], pt_in[0], pt_out[0], st_in[0], st_out[0],
    )
    out, sout = restore(lengths, staged, staged_single)
    return out.reshape(1, 2, 64, 32, 128), sout.reshape(1, 2, 64, 384)


def solution(mesh):
    section = P("section", None, None)
    in_specs = (P(None, "gr", "gc", None), P(None, "gr", None), P()) + (section,) * 7
    out_specs = (P("section", None, "gr", "gc", None), P("section", None, "gr", None))
    return jax.shard_map(
        on_device, mesh=mesh, in_specs=in_specs, out_specs=out_specs, check_vma=False
    )
```

```python
import jax
import jax.numpy as jnp
from jax import lax
from jax.experimental import pallas as pl
from jax.experimental.pallas import tpu as pltpu
from jax.sharding import PartitionSpec as P

MESH = pl.DeviceIdType.MESH
FULL, HALF = 0, 1
RIGHT, LEFT = 0, 1
BF = jnp.bfloat16
F32 = jnp.float32


def dot(a, b):
    return jnp.dot(a, b, preferred_element_type=F32)


def dot_nt(a, b):
    return lax.dot_general(a, b, (((1,), (1,)), ((), ())), preferred_element_type=F32)


def sigmoid(v):
    return 0.5 + 0.5 * jnp.tanh(0.5 * v)


def norm_lanes(v):
    center = v - jnp.mean(v, axis=-1, keepdims=True)
    spread = jnp.mean(center * center, axis=-1, keepdims=True)
    return center * lax.rsqrt(spread + 1e-05)


def norm_pair(v, mean_of):
    center = v.astype(F32) - dot(v, mean_of)
    spread = dot((center * center).astype(BF), mean_of)
    return (center * lax.rsqrt(spread + 1e-05)).astype(BF)


def silu_times(gates, ups):
    half = 0.5 * gates
    return ((half + half * jnp.tanh(half)) * ups).astype(BF)


def iota(shape, axis):
    return lax.broadcasted_iota(jnp.int32, shape, axis)


def trunk_kernel(
    lengths, pair, sin, tin, tgate, tout, pin, pout, st_in, st_out,
    out, sout,
    w_tin, w_gate, w_out, w_pin, w_pout, w_t, st_in_v, st_out_v, sin_next,
    own_sem, out_local, pair_in, zin, zout, normed, stage, settled, perm, order_full, order_half,
    sfull, sbuf, rbuf_full, rbuf_half, lm_full, raw_full, all_full, lm_half, raw_half, all_half,
    ts_full, ts_half, tr_full, tr_half,
    relayed, relay_send, relay_recv, full_send, full_recv, fwd_send, fwd_recv, sib_send, sib_recv, back_send, back_recv,
    met, w_first, w_send, w_recv, st_sem, single_send, single_recv, out_send, out_recv,
):
    sec, gr, gc = lax.axis_index("section"), lax.axis_index("gr"), lax.axis_index("gc")
    y, core = lax.shift_right_logical(gr, 1), lax.bitwise_and(gr, 1)
    sy = sec * 4 + y
    x_hi, z_at = lax.shift_right_logical(gc, 3), lax.bitwise_and(gc, 7)
    plane = x_hi * 8 + sy
    channel = plane * 8 + z_at
    slot = gc * 8 + sy
    active = jnp.logical_and(y < 2, gc < 8)
    peer = {"section": 1 - sec, "gr": gr, "gc": gc}
    sibling = {"section": sec, "gr": gr + 1 - 2 * core, "gc": gc}

    def place(step):
        to_gc = lax.bitwise_and(gc + step, 15)
        to_sy = lax.bitwise_and(sy + lax.shift_right_logical(step, 4), 7)
        to_sec = lax.shift_right_logical(to_sy, 2)
        to_y = lax.bitwise_and(to_sy, 3)
        return to_gc, to_sy, {"section": to_sec, "gr": to_y * 2 + core, "gc": to_gc}

    def channel_of(at_gc, at_sy):
        at_plane = lax.shift_right_logical(at_gc, 3) * 8 + at_sy
        return at_plane * 8 + lax.bitwise_and(at_gc, 7)

    st_copies = [
        pltpu.make_async_copy(st_in, st_in_v, st_sem.at[0]),
        pltpu.make_async_copy(st_out, st_out_v, st_sem.at[1]),
    ]
    weights = [(tin, w_tin), (tgate, w_gate), (tout, w_out), (pin, w_pin), (pout, w_pout)]
    pair_copy = pltpu.make_async_copy(pair.at[:, pl.ds(sec * 32, 32)], pair_in, own_sem.at[5])
    own_copies = [
        pltpu.make_async_copy(own, held.at[sec], own_sem.at[index])
        for index, (own, held) in enumerate(weights)
    ]
    for copy in [pair_copy] + own_copies + st_copies:
        copy.start()

    barrier = pltpu.get_barrier_semaphore()

    def greet_line(semaphore):
        def greet(step, carry):
            to_gc = lax.bitwise_and(gc + step, 15)
            pl.semaphore_signal(
                semaphore, inc=1, device_id={"section": sec, "gr": gr, "gc": to_gc},
                device_id_type=MESH,
            )
            return carry

        lax.fori_loop(1, 16, greet, 0)

    pl.semaphore_signal(barrier, inc=1, device_id=sibling, device_id_type=MESH)
    for step in range(1, 8):
        pl.semaphore_signal(
            barrier, inc=1, device_id=place(step * 16)[2], device_id_type=MESH
        )
    greet_line(barrier)

    def weight_copy(index):
        own, held = weights[index]
        return pltpu.make_async_remote_copy(
            own, held.at[sec], w_send.at[index], w_recv.at[index],
            device_id=peer, device_id_type=MESH,
        )

    def first_copy(side):
        cols = pl.ds(256 - 256 * side, 256)
        return pltpu.make_async_remote_copy(
            tin.at[:, cols], w_tin.at[sec, :, cols], w_first.at[0, side], w_first.at[1, side],
            device_id=peer, device_id_type=MESH,
        )

    pl.semaphore_wait(barrier, 23)
    first_copy(RIGHT).start()
    first_copy(LEFT).start()
    greet_line(met)

    from_lane, to_lane = iota((128, 512), 0), iota((128, 512), 1)
    for low in range(4):
        target = (from_lane >> 5) * 128 + low * 32 + (from_lane & 31)
        perm[low] = jnp.where(to_lane == target, 1.0, 0.0).astype(BF)
    o, i = iota((256, 256), 0), iota((256, 256), 1)
    source = (o & 3) * 64 + ((o >> 5) & 1) * 32 + (o >> 6) * 8 + ((o >> 2) & 7)
    order_full[...] = jnp.where(i == source, 1.0, 0.0).astype(BF)
    o, i = iota((128, 128), 0), iota((128, 128), 1)
    source = (o & 3) * 32 + ((o >> 5) & 1) * 16 + (o >> 6) * 8 + ((o >> 2) & 7)
    order_half[...] = jnp.where(i == source, 1.0, 0.0).astype(BF)

    for copy in [pair_copy] + own_copies:
        copy.wait()
    mean_of = jnp.full((128, 128), 1 / 128, BF)
    first = jnp.where(lengths[0] > lengths[1], 0, 1)
    for kind, crop in ((FULL, first), (HALF, 1 - first)):
        for part in range(4):
            rows = pl.ds(part * 256, 256)
            z = pair_in[crop, part * 8 : part * 8 + 8].reshape(256, 128)
            zin[kind, rows] = z
            normed[kind, rows] = norm_pair(z, mean_of)

    pl.semaphore_wait(met, 15)

    def await_weight(block, index):
        @pl.when(sec != block)
        def _():
            held = weights[index][1].at[block]
            pltpu.make_async_copy(held, held, w_recv.at[index]).wait()

    def gated(block, side, values):
        cols = slice(256 - 256 * side, 512 - 256 * side)
        p = dot_nt(w_t[block, cols], values)
        return sigmoid(p[0:128]) * p[128:256]

    def project_full(block, side):
        for part in range(4):
            value = gated(block, side, normed[FULL, pl.ds(part * 256, 256)])
            for sub in range(2):
                stage[pl.ds(part * 2 + sub, 128, stride=8), :] = value[:, sub * 128 : sub * 128 + 128]
        for part in range(4):
            values = stage[part * 256 : part * 256 + 256, :].astype(BF)
            sfull[block, side, part * 32 : part * 32 + 32] = values.reshape(32, 8, 128)

    def project_half(block):
        for part in range(4):
            values = normed[HALF, pl.ds(part * 256, 256)]
            for side in (LEFT, RIGHT):
                value = gated(block, side, values)
                row = part * 2 + 8 * (1 - side)
                for sub in range(2):
                    stage[pl.ds(row + sub, 128, stride=16), :] = value[:, sub * 128 : sub * 128 + 128]
        for part in range(8):
            values = stage[part * 256 : part * 256 + 256, :].astype(BF)
            sbuf[block, part * 16 : part * 16 + 16] = values.reshape(16, 16, 128)

    def send_full(block, side):
        def send(step, carry):
            to_gc, to_sy, device = place(step)
            pltpu.make_async_remote_copy(
                sfull.at[block, side, channel_of(to_gc, to_sy)], rbuf_full.at[block, side, slot],
                full_send.at[block, side], full_recv.at[block, side],
                device_id=device, device_id_type=MESH,
            ).start()
            return carry

        lax.fori_loop(1, 128, send, 0)
        pltpu.make_async_copy(
            sfull.at[block, side, channel], rbuf_full.at[block, side, slot],
            full_recv.at[block, side],
        ).start()

    def send_half(block):
        source = sec * 2 + y
        for step in range(1, 16):
            to_plane = lax.bitwise_and(plane + step, 15)
            to_sy = lax.bitwise_and(to_plane, 7)
            pltpu.make_async_remote_copy(
                sbuf.at[block, pl.ds(to_plane * 8, 8)], relayed.at[block, source],
                relay_send.at[block], relay_recv.at[block],
                device_id={
                    "section": lax.shift_right_logical(to_sy, 2),
                    "gr": lax.bitwise_and(to_sy, 3) * 2 + core,
                    "gc": lax.shift_right_logical(to_plane, 3) * 8 + z_at,
                },
                device_id_type=MESH,
            ).start()
        pltpu.make_async_copy(
            sbuf.at[block, pl.ds(plane * 8, 8)], relayed.at[block, source],
            relay_recv.at[block],
        ).start()

    def relay(block):
        landed = relayed.at[block]
        pltpu.make_async_copy(landed, landed, relay_recv.at[block]).wait()
        at = rbuf_half.at[block, pl.ds(z_at * 4, 4)]
        for step in range(1, 8):
            to_z = lax.bitwise_and(z_at + step, 7)
            pltpu.make_async_remote_copy(
                relayed.at[block, :, to_z], at, fwd_send.at[block], fwd_recv.at[block],
                device_id={"section": sec, "gr": gr, "gc": x_hi * 8 + to_z},
                device_id_type=MESH,
            ).start()
        pltpu.make_async_copy(relayed.at[block, :, z_at], at, fwd_recv.at[block]).start()

    def forward(block, kind):
        if kind == FULL:
            for side in (RIGHT, LEFT):
                project_full(block, side)
                send_full(block, side)
        else:

            @pl.when(active)
            def _():
                project_half(block)
                send_half(block)

    def parts_of(kind):
        if kind == FULL:
            return rbuf_full, lm_full, raw_full, all_full, ts_full, tr_full, order_full, 4, 8
        return rbuf_half, lm_half, raw_half, all_half, ts_half, tr_half, order_half, 2, 4

    def share_right(block, kind, g, ordered):
        whole = all_full if kind == FULL else all_half
        lanes = slice(g * 128, g * 128 + 128)
        whole[block, core, :, :, lanes] = ordered.astype(BF).reshape(-1, 64, 128)
        mine = whole.at[block, core, :, :, lanes]
        pltpu.make_async_remote_copy(
            mine, mine, sib_send.at[block, kind], sib_recv.at[block, kind],
            device_id=sibling, device_id_type=MESH,
        ).start()

    def triangle_full(block, side):
        landed = rbuf_full.at[block, side]
        pltpu.make_async_copy(landed, landed, full_recv.at[block, side]).wait()
        held = raw_full if side == RIGHT else lm_full
        for g in range(4):
            total = None
            for low in range(4):
                col = (g * 4 + low) * 8
                block_in = rbuf_full[block, side, col : col + 8].astype(F32)
                term = dot(block_in.reshape(64, 128).astype(BF), perm[low])
                total = term if total is None else total + term
            total = total.astype(BF)
            lanes = slice(g * 128, g * 128 + 128)
            for low in range(4):
                held[low * 64 : low * 64 + 64, lanes] = total[:, low * 128 : low * 128 + 128]
            if side == RIGHT:
                share_right(block, FULL, g, dot(order_full[...], raw_full[:, lanes]))

    def triangle_half(block):
        landed = rbuf_half.at[block]
        pltpu.make_async_copy(landed, landed, fwd_recv.at[block]).wait()
        for g in range(2):
            total = None
            for low in range(4):
                col = (g * 4 + low) * 4
                block_in = rbuf_half[block, col : col + 4].reshape(64, 128)
                term = dot(block_in, perm[low])
                total = term if total is None else total + term
            total = total.reshape(4, 16, 512)
            left = total[:, 0:8].reshape(32, 512).astype(BF)
            right = total[:, 8:16].reshape(32, 512).astype(BF)
            lanes = slice(g * 128, g * 128 + 128)
            for low in range(4):
                cols = slice(low * 128, low * 128 + 128)
                lm_half[low * 32 : low * 32 + 32, lanes] = left[:, cols]
                raw_half[low * 32 : low * 32 + 32, lanes] = right[:, cols]
            share_right(block, HALF, g, dot(order_half[...], raw_half[:, lanes]))

    def triangle_out(block, kind):
        rbuf, lm, raw, whole, ts, tr, order, groups, tiles = parts_of(kind)
        rows = tiles * 8
        full = kind == FULL
        other = whole.at[block, 1 - core]
        pltpu.make_async_copy(other, other, sib_recv.at[block, kind]).wait()
        home = lax.bitwise_and(lax.shift_right_logical(gc, 2), groups - 1)
        source = sy if full else sec * 2 + y

        for turn in range(groups):
            g = lax.bitwise_and(home + turn, groups - 1)
            right = jnp.concatenate([whole[block, 0, g], whole[block, 1, g]], axis=0)
            product = dot_nt(lm[...], right).astype(BF)
            total = None
            for low in range(4):
                term = dot(product[low * rows : (low + 1) * rows], perm[low])
                total = term if total is None else total + term
            total = total.astype(BF)
            for low in range(4):
                ts[block, g * 4 + low] = total[:, low * 128 : low * 128 + 128].reshape(
                    tiles, 8, 128
                )

            def send(step, carry):
                to_gc = g * 4 + lax.bitwise_and(gc + step, 3)
                to_tile = lax.bitwise_and(source + lax.shift_right_logical(step, 2), tiles - 1)
                to_sec = lax.shift_right_logical(to_tile, 2 if full else 1)
                to_y = lax.bitwise_and(to_tile, tiles // 2 - 1)

                def local():
                    pltpu.make_async_copy(
                        ts.at[block, to_gc, to_tile], tr.at[block, channel],
                        back_recv.at[block, kind],
                    ).start()

                def remote():
                    pltpu.make_async_remote_copy(
                        ts.at[block, to_gc, to_tile], tr.at[block, channel],
                        back_send.at[block, kind], back_recv.at[block, kind],
                        device_id={"section": to_sec, "gr": to_y * 2 + core, "gc": to_gc},
                        device_id_type=MESH,
                    ).start()

                if turn == 0:
                    itself = step == 0
                    if not full:
                        itself = jnp.logical_and(itself, active)
                    pl.when(itself)(local)
                    pl.when(jnp.logical_not(itself))(remote)
                else:
                    remote()
                return carry

            lax.fori_loop(0, tiles * 4, send, 0)

    def finish(block, kind):
        z = zin if block == 0 else zout.at[0]
        tr = tr_full if kind == FULL else tr_half
        landed = tr.at[block]
        if kind == FULL:
            pltpu.make_async_copy(landed, landed, back_recv.at[block, kind]).wait()
        else:

            @pl.when(active)
            def _():
                pltpu.make_async_copy(landed, landed, back_recv.at[block, kind]).wait()

            @pl.when(jnp.logical_not(active))
            def _():
                tr[block] = jnp.zeros((128, 8, 128), BF)

        values = tr[block].astype(F32)
        center = values - jnp.mean(values, axis=0, keepdims=True)
        spread = jnp.mean(center * center, axis=0, keepdims=True)
        center = center * lax.rsqrt(spread + 1e-05)
        stage[0:1024, :] = center.reshape(1024, 128)
        for r in range(8):
            tile = stage[pl.ds(r, 128, stride=8), :]
            settled[r * 128 : r * 128 + 128] = tile.astype(BF).T
        for part in range(4):
            rows = pl.ds(part * 256, 256)
            gate = sigmoid(dot(normed[kind, rows], w_gate[block]))
            update = dot(settled[rows], w_out[block])
            updated = (z[kind, rows].astype(F32) + gate * update).astype(BF)
            trans_in = norm_pair(updated, mean_of)
            gates = dot(trans_in, w_pin[block, :, 0:512])
            ups = dot(trans_in, w_pin[block, :, 512:1024])
            inner = silu_times(gates, ups)
            done = (updated.astype(F32) + dot(inner, w_pout[block])).astype(BF)
            zout[block, kind, rows] = done
            if block == 0:
                normed[kind, rows] = norm_pair(done, mean_of)
            else:
                deliver(block, kind, part, 1)

    def deliver(block, kind, part=0, parts=4):
        rows = pl.ds(part * 256, parts * 256)

        @pl.when(sec == block)
        def _():
            pltpu.make_async_copy(
                zout.at[block, kind, rows], out.at[kind, sec, rows], out_local.at[kind]
            ).start()

        @pl.when(sec != block)
        def _():
            pltpu.make_async_remote_copy(
                zout.at[block, kind, rows], out.at[kind, sec, rows],
                out_send.at[kind], out_recv.at[kind],
                device_id=peer, device_id_type=MESH,
            ).start()

    def single(rows_in):
        value = rows_in[...].astype(F32)
        value_in = norm_lanes(value).astype(BF)
        total = value
        for part in range(6):
            cols = part * 256
            gates = dot(value_in, st_in_v[:, cols : cols + 256])
            ups = dot(value_in, st_in_v[:, 1536 + cols : 1536 + cols + 256])
            inner = silu_times(gates, ups)
            total = total + dot(inner, st_out_v[cols : cols + 256])
        sout[...] = total.astype(BF)

    single_copy = pltpu.make_async_remote_copy(
        sout, sin_next, single_send, single_recv, device_id=peer, device_id_type=MESH
    )

    def start_block(block, side):
        cols = slice(256 - 256 * side, 512 - 256 * side)

        @pl.when(sec != block)
        def _():
            held = w_tin.at[block, :, cols]
            pltpu.make_async_copy(held, held, w_first.at[1, side]).wait()

        w_t[block, cols] = w_tin[block, :, cols].astype(F32).T.astype(BF)

    def more_weights():
        for index in range(1, 5):
            weight_copy(index).start()

    def rest_weights(block):
        for index in range(1, 5):
            await_weight(block, index)

    def single_turn(block):
        @pl.when(sec == block)
        def _():
            for copy in st_copies:
                copy.wait()
            if block == 0:
                single(sin)
                single_copy.start()
            else:
                single_copy.wait_recv()
                single(sin_next)

    start_block(0, RIGHT)
    project_full(0, RIGHT)
    send_full(0, RIGHT)
    start_block(0, LEFT)
    project_full(0, LEFT)
    send_full(0, LEFT)
    forward(0, HALF)
    more_weights()
    single_turn(0)
    triangle_full(0, RIGHT)
    triangle_full(0, LEFT)
    relay(0)
    triangle_out(0, FULL)
    triangle_half(0)
    triangle_out(0, HALF)
    start_block(1, RIGHT)
    start_block(1, LEFT)
    rest_weights(0)
    finish(0, FULL)
    forward(1, FULL)
    finish(0, HALF)
    forward(1, HALF)
    deliver(0, FULL)
    deliver(0, HALF)
    single_turn(1)
    triangle_full(1, RIGHT)
    triangle_full(1, LEFT)
    relay(1)
    triangle_out(1, FULL)
    triangle_half(1)
    triangle_out(1, HALF)
    rest_weights(1)
    finish(1, FULL)
    finish(1, HALF)

    def end_forward(block, kind):
        if kind == FULL:
            for side in (RIGHT, LEFT):
                sent = rbuf_full.at[block, side, pl.ds(0, 127)]
                pltpu.make_async_copy(sent, sent, full_send.at[block, side]).wait()
        else:
            sent = sbuf.at[block, pl.ds(0, 28)]
            pltpu.make_async_copy(sent, sent, fwd_send.at[block]).wait()
            sent = sbuf.at[block, pl.ds(0, 120)]
            pl.when(active)(pltpu.make_async_copy(sent, sent, relay_send.at[block]).wait)

    def end_triangle(block, kind):
        mine = (all_full if kind == FULL else all_half).at[block, core]
        pltpu.make_async_copy(mine, mine, sib_send.at[block, kind]).wait()

    def end_back(block, kind):
        def wait(count):
            sent = tr_full.at[block, pl.ds(0, count)]
            pltpu.make_async_copy(sent, sent, back_send.at[block, kind]).wait()

        if kind == FULL:
            wait(127)
        else:
            pl.when(active)(lambda: wait(31))
            pl.when(jnp.logical_not(active))(lambda: wait(32))

    def end_rest():
        first_copy(RIGHT).wait_send()
        first_copy(LEFT).wait_send()
        for index in range(1, 5):
            weight_copy(index).wait_send()
        pl.when(sec == 0)(single_copy.wait_send)

    def end_deliver(kind):
        given = zout.at[0, kind]
        pltpu.make_async_copy(given, given, out_send.at[kind]).wait()
        kept = out.at[kind, sec]
        pltpu.make_async_copy(kept, kept, out_local.at[kind]).wait()
        taken = out.at[kind, 1 - sec]
        pltpu.make_async_copy(taken, taken, out_recv.at[kind]).wait()

    for block in range(2):
        for kind in (FULL, HALF):
            end_forward(block, kind)
            end_triangle(block, kind)
            end_back(block, kind)
    end_rest()
    end_deliver(FULL)
    end_deliver(HALF)


def trunk(lengths, pair, sin, tin, tgate, tout, pin, pout, st_in, st_out):
    vmem = pl.BlockSpec(memory_space=pltpu.VMEM)
    anywhere = pl.BlockSpec(memory_space=pl.ANY)
    dma = pltpu.SemaphoreType.DMA
    return pl.pallas_call(
        trunk_kernel,
        out_shape=(
            jax.ShapeDtypeStruct((2, 2, 1024, 128), BF),
            jax.ShapeDtypeStruct((128, 384), BF),
        ),
        in_specs=[pl.BlockSpec(memory_space=pltpu.SMEM), anywhere, vmem] + [anywhere] * 7,
        out_specs=(anywhere, vmem),
        scratch_shapes=[
            pltpu.VMEM((2, 128, 512), BF),
            pltpu.VMEM((2, 128, 128), BF),
            pltpu.VMEM((2, 128, 128), BF),
            pltpu.VMEM((2, 128, 1024), BF),
            pltpu.VMEM((2, 512, 128), BF),
            pltpu.VMEM((2, 512, 128), BF),
            pltpu.VMEM((384, 3072), BF),
            pltpu.VMEM((1536, 384), BF),
            pltpu.VMEM((128, 384), BF),
            dma((6,)),
            dma((2,)),
            pltpu.VMEM((2, 32, 32, 128), BF),
            pltpu.VMEM((2, 1024, 128), BF),
            pltpu.VMEM((2, 2, 1024, 128), BF),
            pltpu.VMEM((2, 1024, 128), BF),
            pltpu.VMEM((2048, 128), F32),
            pltpu.VMEM((1024, 128), BF),
            pltpu.VMEM((4, 128, 512), BF),
            pltpu.VMEM((256, 256), BF),
            pltpu.VMEM((128, 128), BF),
            pltpu.VMEM((2, 2, 128, 8, 128), BF),
            pltpu.VMEM((2, 128, 16, 128), BF),
            pltpu.VMEM((2, 2, 128, 8, 128), BF),
            pltpu.VMEM((2, 32, 16, 128), BF),
            pltpu.VMEM((256, 512), BF),
            pltpu.VMEM((256, 512), BF),
            pltpu.VMEM((2, 2, 4, 64, 512), BF),
            pltpu.VMEM((128, 256), BF),
            pltpu.VMEM((128, 256), BF),
            pltpu.VMEM((2, 2, 2, 64, 256), BF),
            pltpu.VMEM((2, 16, 8, 8, 128), BF),
            pltpu.VMEM((2, 8, 4, 8, 128), BF),
            pltpu.VMEM((2, 128, 8, 128), BF),
            pltpu.VMEM((2, 128, 8, 128), BF),
            pltpu.VMEM((2, 4, 8, 16, 128), BF),
            dma((2,)),
            dma((2,)),
            dma((2, 2)),
            dma((2, 2)),
            dma((2,)),
            dma((2,)),
            dma((2, 2)),
            dma((2, 2)),
            dma((2, 2)),
            dma((2, 2)),
            pltpu.SemaphoreType.REGULAR,
            dma((2, 2)),
            dma((5,)),
            dma((5,)),
            dma((2,)),
            dma,
            dma,
            dma((2,)),
            dma((2,)),
        ],
        compiler_params=pltpu.CompilerParams(
            collective_id=0, has_side_effects=True, vmem_limit_bytes=56 << 20
        ),
    )(lengths, pair, sin, tin, tgate, tout, pin, pout, st_in, st_out)


def restore_kernel(lengths, staged, staged_single, out, sout, sems):
    first = jnp.where(lengths[0] > lengths[1], 0, 1)
    copies = [
        pltpu.make_async_copy(staged.at[micro ^ first, half], out.at[0, micro, half], sems.at[micro, half])
        for micro in range(2)
        for half in range(2)
    ]
    copies.append(pltpu.make_async_copy(staged_single, sout, sems.at[2, 0]))
    for copy in copies:
        copy.start()
    for copy in copies:
        copy.wait()


def restore(lengths, staged, staged_single):
    anywhere = pl.BlockSpec(memory_space=pl.ANY)
    return pl.pallas_call(
        restore_kernel,
        out_shape=(
            jax.ShapeDtypeStruct((1, 2, 2, 1024, 128), BF),
            jax.ShapeDtypeStruct((128, 384), BF),
        ),
        in_specs=[pl.BlockSpec(memory_space=pltpu.SMEM), anywhere, anywhere],
        out_specs=(pl.BlockSpec(memory_space=pltpu.VMEM),) * 2,
        scratch_shapes=[pltpu.SemaphoreType.DMA((3, 2))],
    )(lengths, staged, staged_single)


def on_device(pair, single, lengths, tri_in, tri_gate, tri_out, pt_in, pt_out, st_in, st_out):
    staged, staged_single = trunk(
        lengths,
        pair,
        single.reshape(128, 384),
        tri_in[0], tri_gate[0], tri_out[0], pt_in[0], pt_out[0], st_in[0], st_out[0],
    )
    out, sout = restore(lengths, staged, staged_single)
    return out.reshape(1, 2, 64, 32, 128), sout.reshape(1, 2, 64, 384)


def solution(mesh):
    section = P("section", None, None)
    in_specs = (P(None, "gr", "gc", None), P(None, "gr", None), P()) + (section,) * 7
    out_specs = (P("section", None, "gr", "gc", None), P("section", None, "gr", None))
    return jax.shard_map(
        on_device, mesh=mesh, in_specs=in_specs, out_specs=out_specs, check_vma=False
    )
```

```python
import jax
import jax.numpy as jnp
from jax import lax
from jax.experimental import pallas as pl
from jax.experimental.pallas import tpu as pltpu
from jax.sharding import PartitionSpec as P

MESH = pl.DeviceIdType.MESH
FULL, HALF = 0, 1
RIGHT, LEFT = 0, 1
BF = jnp.bfloat16
F32 = jnp.float32


def dot(a, b):
    return jnp.dot(a, b, preferred_element_type=F32)


def dot_nt(a, b):
    return lax.dot_general(a, b, (((1,), (1,)), ((), ())), preferred_element_type=F32)


def sigmoid(v):
    return 0.5 + 0.5 * jnp.tanh(0.5 * v)


def norm_lanes(v):
    center = v - jnp.mean(v, axis=-1, keepdims=True)
    spread = jnp.mean(center * center, axis=-1, keepdims=True)
    return center * lax.rsqrt(spread + 1e-05)


def silu_times(gates, ups):
    half = 0.5 * gates
    return ((half + half * jnp.tanh(half)) * ups).astype(BF)


def iota(shape, axis):
    return lax.broadcasted_iota(jnp.int32, shape, axis)


def trunk_kernel(
    lengths, pair, sin, tin, tgate, tout, pin, pout, st_in, st_out,
    out, sout,
    w_tin, w_gate, w_out, w_pin, w_pout, w_t, st_in_v, st_out_v, sin_next,
    own_sem, out_local, pair_in, zin, zout, normed, stage, settled, perm, order_full, order_half,
    sfull, sbuf, rbuf_full, rbuf_half, lm_full, raw_full, all_full, lm_half, raw_half, all_half,
    ts_full, ts_half, tr_full, tr_half,
    relayed, relay_send, relay_recv, full_send, full_recv, fwd_send, fwd_recv, sib_send, sib_recv, back_send, back_recv,
    met, w_first, w_send, w_recv, st_sem, single_send, single_recv, out_send, out_recv,
):
    sec, gr, gc = lax.axis_index("section"), lax.axis_index("gr"), lax.axis_index("gc")
    y, core = lax.shift_right_logical(gr, 1), lax.bitwise_and(gr, 1)
    sy = sec * 4 + y
    x_hi, z_at = lax.shift_right_logical(gc, 3), lax.bitwise_and(gc, 7)
    plane = x_hi * 8 + sy
    channel = plane * 8 + z_at
    slot = gc * 8 + sy
    active = jnp.logical_and(y < 2, gc < 8)
    peer = {"section": 1 - sec, "gr": gr, "gc": gc}
    sibling = {"section": sec, "gr": gr + 1 - 2 * core, "gc": gc}

    def place(step):
        to_gc = lax.bitwise_and(gc + step, 15)
        to_sy = lax.bitwise_and(sy + lax.shift_right_logical(step, 4), 7)
        to_sec = lax.shift_right_logical(to_sy, 2)
        to_y = lax.bitwise_and(to_sy, 3)
        return to_gc, to_sy, {"section": to_sec, "gr": to_y * 2 + core, "gc": to_gc}

    def channel_of(at_gc, at_sy):
        at_plane = lax.shift_right_logical(at_gc, 3) * 8 + at_sy
        return at_plane * 8 + lax.bitwise_and(at_gc, 7)

    st_copies = [
        pltpu.make_async_copy(st_in, st_in_v, st_sem.at[0]),
        pltpu.make_async_copy(st_out, st_out_v, st_sem.at[1]),
    ]
    weights = [(tin, w_tin), (tgate, w_gate), (tout, w_out), (pin, w_pin), (pout, w_pout)]
    pair_copy = pltpu.make_async_copy(pair.at[:, pl.ds(sec * 32, 32)], pair_in, own_sem.at[5])
    own_copies = [
        pltpu.make_async_copy(own, held.at[sec], own_sem.at[index])
        for index, (own, held) in enumerate(weights)
    ]
    for copy in [pair_copy] + own_copies + st_copies:
        copy.start()

    barrier = pltpu.get_barrier_semaphore()

    def greet_line(semaphore):
        def greet(step, carry):
            to_gc = lax.bitwise_and(gc + step, 15)
            pl.semaphore_signal(
                semaphore, inc=1, device_id={"section": sec, "gr": gr, "gc": to_gc},
                device_id_type=MESH,
            )
            return carry

        lax.fori_loop(1, 16, greet, 0)

    pl.semaphore_signal(barrier, inc=1, device_id=sibling, device_id_type=MESH)
    for step in range(1, 8):
        pl.semaphore_signal(
            barrier, inc=1, device_id=place(step * 16)[2], device_id_type=MESH
        )
    greet_line(barrier)

    def weight_copy(index):
        own, held = weights[index]
        return pltpu.make_async_remote_copy(
            own, held.at[sec], w_send.at[index], w_recv.at[index],
            device_id=peer, device_id_type=MESH,
        )

    def first_copy(side):
        cols = pl.ds(256 - 256 * side, 256)
        return pltpu.make_async_remote_copy(
            tin.at[:, cols], w_tin.at[sec, :, cols], w_first.at[0, side], w_first.at[1, side],
            device_id=peer, device_id_type=MESH,
        )

    pl.semaphore_wait(barrier, 23)
    first_copy(RIGHT).start()
    first_copy(LEFT).start()
    greet_line(met)

    from_lane, to_lane = iota((128, 512), 0), iota((128, 512), 1)
    for low in range(4):
        target = (from_lane >> 5) * 128 + low * 32 + (from_lane & 31)
        perm[low] = jnp.where(to_lane == target, 1.0, 0.0).astype(BF)
    o, i = iota((256, 256), 0), iota((256, 256), 1)
    source = (o & 3) * 64 + ((o >> 5) & 1) * 32 + (o >> 6) * 8 + ((o >> 2) & 7)
    order_full[...] = jnp.where(i == source, 1.0, 0.0).astype(BF)
    o, i = iota((128, 128), 0), iota((128, 128), 1)
    source = (o & 3) * 32 + ((o >> 5) & 1) * 16 + (o >> 6) * 8 + ((o >> 2) & 7)
    order_half[...] = jnp.where(i == source, 1.0, 0.0).astype(BF)

    for copy in [pair_copy] + own_copies:
        copy.wait()
    first = jnp.where(lengths[0] > lengths[1], 0, 1)
    for kind, crop in ((FULL, first), (HALF, 1 - first)):
        z = pair_in[crop].reshape(1024, 128)
        zin[kind] = z
        normed[kind] = norm_lanes(z.astype(F32)).astype(BF)

    pl.semaphore_wait(met, 15)

    def await_weight(block, index):
        @pl.when(sec != block)
        def _():
            held = weights[index][1].at[block]
            pltpu.make_async_copy(held, held, w_recv.at[index]).wait()

    def gated(block, side, values):
        cols = slice(256 - 256 * side, 512 - 256 * side)
        p = dot_nt(w_t[block, cols], values)
        return sigmoid(p[0:128]) * p[128:256]

    def project_full(block, side):
        for part in range(2):
            value = gated(block, side, normed[FULL, pl.ds(part * 512, 512)])
            for sub in range(4):
                stage[pl.ds(part * 4 + sub, 128, stride=8), :] = value[:, sub * 128 : sub * 128 + 128]
        for part in range(4):
            values = stage[part * 256 : part * 256 + 256, :].astype(BF)
            sfull[block, side, part * 32 : part * 32 + 32] = values.reshape(32, 8, 128)

    def project_half(block):
        for part in range(4):
            values = normed[HALF, pl.ds(part * 256, 256)]
            for side in (LEFT, RIGHT):
                value = gated(block, side, values)
                row = part * 2 + 8 * (1 - side)
                for sub in range(2):
                    stage[pl.ds(row + sub, 128, stride=16), :] = value[:, sub * 128 : sub * 128 + 128]
        for part in range(8):
            values = stage[part * 256 : part * 256 + 256, :].astype(BF)
            sbuf[block, part * 16 : part * 16 + 16] = values.reshape(16, 16, 128)

    def send_full(block, side):
        def send(step, carry):
            to_gc, to_sy, device = place(step)
            pltpu.make_async_remote_copy(
                sfull.at[block, side, channel_of(to_gc, to_sy)], rbuf_full.at[block, side, slot],
                full_send.at[block, side], full_recv.at[block, side],
                device_id=device, device_id_type=MESH,
            ).start()
            return carry

        lax.fori_loop(1, 128, send, 0)
        pltpu.make_async_copy(
            sfull.at[block, side, channel], rbuf_full.at[block, side, slot],
            full_recv.at[block, side],
        ).start()

    def send_half(block):
        source = sec * 2 + y
        for step in range(1, 16):
            to_plane = lax.bitwise_and(plane + step, 15)
            to_sy = lax.bitwise_and(to_plane, 7)
            pltpu.make_async_remote_copy(
                sbuf.at[block, pl.ds(to_plane * 8, 8)], relayed.at[block, source],
                relay_send.at[block], relay_recv.at[block],
                device_id={
                    "section": lax.shift_right_logical(to_sy, 2),
                    "gr": lax.bitwise_and(to_sy, 3) * 2 + core,
                    "gc": lax.shift_right_logical(to_plane, 3) * 8 + z_at,
                },
                device_id_type=MESH,
            ).start()
        pltpu.make_async_copy(
            sbuf.at[block, pl.ds(plane * 8, 8)], relayed.at[block, source],
            relay_recv.at[block],
        ).start()

    def relay(block):
        landed = relayed.at[block]
        pltpu.make_async_copy(landed, landed, relay_recv.at[block]).wait()
        at = rbuf_half.at[block, pl.ds(z_at * 4, 4)]
        for step in range(1, 8):
            to_z = lax.bitwise_and(z_at + step, 7)
            pltpu.make_async_remote_copy(
                relayed.at[block, :, to_z], at, fwd_send.at[block], fwd_recv.at[block],
                device_id={"section": sec, "gr": gr, "gc": x_hi * 8 + to_z},
                device_id_type=MESH,
            ).start()
        pltpu.make_async_copy(relayed.at[block, :, z_at], at, fwd_recv.at[block]).start()

    def forward(block, kind):
        if kind == FULL:
            for side in (RIGHT, LEFT):
                project_full(block, side)
                send_full(block, side)
        else:

            @pl.when(active)
            def _():
                project_half(block)
                send_half(block)

    def parts_of(kind):
        if kind == FULL:
            return rbuf_full, lm_full, raw_full, all_full, ts_full, tr_full, order_full, 4, 8
        return rbuf_half, lm_half, raw_half, all_half, ts_half, tr_half, order_half, 2, 4

    def share_right(block, kind, g, ordered):
        whole = all_full if kind == FULL else all_half
        lanes = slice(g * 128, g * 128 + 128)
        whole[block, core, :, :, lanes] = ordered.astype(BF).reshape(-1, 64, 128)
        mine = whole.at[block, core, :, :, lanes]
        pltpu.make_async_remote_copy(
            mine, mine, sib_send.at[block, kind], sib_recv.at[block, kind],
            device_id=sibling, device_id_type=MESH,
        ).start()

    def triangle_full(block, side):
        landed = rbuf_full.at[block, side]
        pltpu.make_async_copy(landed, landed, full_recv.at[block, side]).wait()
        held = raw_full if side == RIGHT else lm_full
        for g in range(4):
            total = None
            for low in range(4):
                col = (g * 4 + low) * 8
                block_in = rbuf_full[block, side, col : col + 8].astype(F32)
                term = dot(block_in.reshape(64, 128).astype(BF), perm[low])
                total = term if total is None else total + term
            total = total.astype(BF)
            lanes = slice(g * 128, g * 128 + 128)
            for low in range(4):
                held[low * 64 : low * 64 + 64, lanes] = total[:, low * 128 : low * 128 + 128]
            if side == RIGHT:
                share_right(block, FULL, g, dot(order_full[...], raw_full[:, lanes]))

    def triangle_half(block):
        landed = rbuf_half.at[block]
        pltpu.make_async_copy(landed, landed, fwd_recv.at[block]).wait()
        for g in range(2):
            total = None
            for low in range(4):
                col = (g * 4 + low) * 4
                block_in = rbuf_half[block, col : col + 4].reshape(64, 128)
                term = dot(block_in, perm[low])
                total = term if total is None else total + term
            total = total.reshape(4, 16, 512)
            left = total[:, 0:8].reshape(32, 512).astype(BF)
            right = total[:, 8:16].reshape(32, 512).astype(BF)
            lanes = slice(g * 128, g * 128 + 128)
            for low in range(4):
                cols = slice(low * 128, low * 128 + 128)
                lm_half[low * 32 : low * 32 + 32, lanes] = left[:, cols]
                raw_half[low * 32 : low * 32 + 32, lanes] = right[:, cols]
            share_right(block, HALF, g, dot(order_half[...], raw_half[:, lanes]))

    def triangle_out(block, kind):
        rbuf, lm, raw, whole, ts, tr, order, groups, tiles = parts_of(kind)
        rows = tiles * 8
        full = kind == FULL
        other = whole.at[block, 1 - core]
        pltpu.make_async_copy(other, other, sib_recv.at[block, kind]).wait()
        home = lax.bitwise_and(lax.shift_right_logical(gc, 2), groups - 1)
        source = sy if full else sec * 2 + y

        for turn in range(groups):
            g = lax.bitwise_and(home + turn, groups - 1)
            right = jnp.concatenate([whole[block, 0, g], whole[block, 1, g]], axis=0)
            product = dot_nt(lm[...], right).astype(BF)
            total = None
            for low in range(4):
                term = dot(product[low * rows : (low + 1) * rows], perm[low])
                total = term if total is None else total + term
            total = total.astype(BF)
            for low in range(4):
                ts[block, g * 4 + low] = total[:, low * 128 : low * 128 + 128].reshape(
                    tiles, 8, 128
                )

            def send(step, carry):
                to_gc = g * 4 + lax.bitwise_and(gc + step, 3)
                to_tile = lax.bitwise_and(source + lax.shift_right_logical(step, 2), tiles - 1)
                to_sec = lax.shift_right_logical(to_tile, 2 if full else 1)
                to_y = lax.bitwise_and(to_tile, tiles // 2 - 1)

                def local():
                    pltpu.make_async_copy(
                        ts.at[block, to_gc, to_tile], tr.at[block, channel],
                        back_recv.at[block, kind],
                    ).start()

                def remote():
                    pltpu.make_async_remote_copy(
                        ts.at[block, to_gc, to_tile], tr.at[block, channel],
                        back_send.at[block, kind], back_recv.at[block, kind],
                        device_id={"section": to_sec, "gr": to_y * 2 + core, "gc": to_gc},
                        device_id_type=MESH,
                    ).start()

                if turn == 0:
                    itself = step == 0
                    if not full:
                        itself = jnp.logical_and(itself, active)
                    pl.when(itself)(local)
                    pl.when(jnp.logical_not(itself))(remote)
                else:
                    remote()
                return carry

            lax.fori_loop(0, tiles * 4, send, 0)

    def finish(block, kind):
        z = zin if block == 0 else zout.at[0]
        tr = tr_full if kind == FULL else tr_half
        landed = tr.at[block]
        if kind == FULL:
            pltpu.make_async_copy(landed, landed, back_recv.at[block, kind]).wait()
        else:

            @pl.when(active)
            def _():
                pltpu.make_async_copy(landed, landed, back_recv.at[block, kind]).wait()

            @pl.when(jnp.logical_not(active))
            def _():
                tr[block] = jnp.zeros((128, 8, 128), BF)

        values = tr[block].astype(F32)
        center = values - jnp.mean(values, axis=0, keepdims=True)
        spread = jnp.mean(center * center, axis=0, keepdims=True)
        center = center * lax.rsqrt(spread + 1e-05)
        stage[0:1024, :] = center.reshape(1024, 128)
        for r in range(8):
            tile = stage[pl.ds(r, 128, stride=8), :]
            settled[r * 128 : r * 128 + 128] = tile.astype(BF).T
        parts = 1 if block == 0 else 2
        for part in range(parts):
            rows = pl.ds(part * (1024 // parts), 1024 // parts)
            gate = sigmoid(dot(normed[kind, rows], w_gate[block]))
            update = dot(settled[rows], w_out[block])
            updated = (z[kind, rows].astype(F32) + gate * update).astype(BF)
            trans_in = norm_lanes(updated.astype(F32)).astype(BF)
            gates = dot(trans_in, w_pin[block, :, 0:512])
            ups = dot(trans_in, w_pin[block, :, 512:1024])
            inner = silu_times(gates, ups)
            done = (updated.astype(F32) + dot(inner, w_pout[block])).astype(BF)
            zout[block, kind, rows] = done
            if block == 0:
                normed[kind, rows] = norm_lanes(done.astype(F32)).astype(BF)
            else:
                deliver(block, kind, part, parts)

    def deliver(block, kind, part=0, parts=1):
        rows = pl.ds(part * (1024 // parts), 1024 // parts)

        @pl.when(sec == block)
        def _():
            pltpu.make_async_copy(
                zout.at[block, kind, rows], out.at[kind, sec, rows], out_local.at[kind]
            ).start()

        @pl.when(sec != block)
        def _():
            pltpu.make_async_remote_copy(
                zout.at[block, kind, rows], out.at[kind, sec, rows],
                out_send.at[kind], out_recv.at[kind],
                device_id=peer, device_id_type=MESH,
            ).start()

    def single(rows_in):
        value = rows_in[...].astype(F32)
        value_in = norm_lanes(value).astype(BF)
        total = value
        for part in range(6):
            cols = part * 256
            gates = dot(value_in, st_in_v[:, cols : cols + 256])
            ups = dot(value_in, st_in_v[:, 1536 + cols : 1536 + cols + 256])
            inner = silu_times(gates, ups)
            total = total + dot(inner, st_out_v[cols : cols + 256])
        sout[...] = total.astype(BF)

    single_copy = pltpu.make_async_remote_copy(
        sout, sin_next, single_send, single_recv, device_id=peer, device_id_type=MESH
    )

    def start_block(block, side):
        cols = slice(256 - 256 * side, 512 - 256 * side)

        @pl.when(sec != block)
        def _():
            held = w_tin.at[block, :, cols]
            pltpu.make_async_copy(held, held, w_first.at[1, side]).wait()

        w_t[block, cols] = w_tin[block, :, cols].astype(F32).T.astype(BF)

    def more_weights():
        for index in range(1, 5):
            weight_copy(index).start()

    def rest_weights(block):
        for index in range(1, 5):
            await_weight(block, index)

    def single_turn(block):
        @pl.when(sec == block)
        def _():
            for copy in st_copies:
                copy.wait()
            if block == 0:
                single(sin)
                single_copy.start()
            else:
                single_copy.wait_recv()
                single(sin_next)

    start_block(0, RIGHT)
    project_full(0, RIGHT)
    send_full(0, RIGHT)
    start_block(0, LEFT)
    project_full(0, LEFT)
    send_full(0, LEFT)
    forward(0, HALF)
    more_weights()
    single_turn(0)
    triangle_full(0, RIGHT)
    triangle_full(0, LEFT)
    relay(0)
    triangle_out(0, FULL)
    triangle_half(0)
    triangle_out(0, HALF)
    start_block(1, RIGHT)
    start_block(1, LEFT)
    rest_weights(0)
    finish(0, FULL)
    forward(1, FULL)
    finish(0, HALF)
    forward(1, HALF)
    deliver(0, FULL)
    deliver(0, HALF)
    single_turn(1)
    triangle_full(1, RIGHT)
    triangle_full(1, LEFT)
    relay(1)
    triangle_out(1, FULL)
    triangle_half(1)
    triangle_out(1, HALF)
    rest_weights(1)
    finish(1, FULL)
    finish(1, HALF)

    def end_forward(block, kind):
        if kind == FULL:
            for side in (RIGHT, LEFT):
                sent = rbuf_full.at[block, side, pl.ds(0, 127)]
                pltpu.make_async_copy(sent, sent, full_send.at[block, side]).wait()
        else:
            sent = sbuf.at[block, pl.ds(0, 28)]
            pltpu.make_async_copy(sent, sent, fwd_send.at[block]).wait()
            sent = sbuf.at[block, pl.ds(0, 120)]
            pl.when(active)(pltpu.make_async_copy(sent, sent, relay_send.at[block]).wait)

    def end_triangle(block, kind):
        mine = (all_full if kind == FULL else all_half).at[block, core]
        pltpu.make_async_copy(mine, mine, sib_send.at[block, kind]).wait()

    def end_back(block, kind):
        def wait(count):
            sent = tr_full.at[block, pl.ds(0, count)]
            pltpu.make_async_copy(sent, sent, back_send.at[block, kind]).wait()

        if kind == FULL:
            wait(127)
        else:
            pl.when(active)(lambda: wait(31))
            pl.when(jnp.logical_not(active))(lambda: wait(32))

    def end_rest():
        first_copy(RIGHT).wait_send()
        first_copy(LEFT).wait_send()
        for index in range(1, 5):
            weight_copy(index).wait_send()
        pl.when(sec == 0)(single_copy.wait_send)

    def end_deliver(kind):
        given = zout.at[0, kind]
        pltpu.make_async_copy(given, given, out_send.at[kind]).wait()
        kept = out.at[kind, sec]
        pltpu.make_async_copy(kept, kept, out_local.at[kind]).wait()
        taken = out.at[kind, 1 - sec]
        pltpu.make_async_copy(taken, taken, out_recv.at[kind]).wait()

    for block in range(2):
        for kind in (FULL, HALF):
            end_forward(block, kind)
            end_triangle(block, kind)
            end_back(block, kind)
    end_rest()
    end_deliver(FULL)
    end_deliver(HALF)


def trunk(lengths, pair, sin, tin, tgate, tout, pin, pout, st_in, st_out):
    vmem = pl.BlockSpec(memory_space=pltpu.VMEM)
    anywhere = pl.BlockSpec(memory_space=pl.ANY)
    dma = pltpu.SemaphoreType.DMA
    return pl.pallas_call(
        trunk_kernel,
        out_shape=(
            jax.ShapeDtypeStruct((2, 2, 1024, 128), BF),
            jax.ShapeDtypeStruct((128, 384), BF),
        ),
        in_specs=[pl.BlockSpec(memory_space=pltpu.SMEM), anywhere, vmem] + [anywhere] * 7,
        out_specs=(anywhere, vmem),
        scratch_shapes=[
            pltpu.VMEM((2, 128, 512), BF),
            pltpu.VMEM((2, 128, 128), BF),
            pltpu.VMEM((2, 128, 128), BF),
            pltpu.VMEM((2, 128, 1024), BF),
            pltpu.VMEM((2, 512, 128), BF),
            pltpu.VMEM((2, 512, 128), BF),
            pltpu.VMEM((384, 3072), BF),
            pltpu.VMEM((1536, 384), BF),
            pltpu.VMEM((128, 384), BF),
            dma((6,)),
            dma((2,)),
            pltpu.VMEM((2, 32, 32, 128), BF),
            pltpu.VMEM((2, 1024, 128), BF),
            pltpu.VMEM((2, 2, 1024, 128), BF),
            pltpu.VMEM((2, 1024, 128), BF),
            pltpu.VMEM((2048, 128), F32),
            pltpu.VMEM((1024, 128), BF),
            pltpu.VMEM((4, 128, 512), BF),
            pltpu.VMEM((256, 256), BF),
            pltpu.VMEM((128, 128), BF),
            pltpu.VMEM((2, 2, 128, 8, 128), BF),
            pltpu.VMEM((2, 128, 16, 128), BF),
            pltpu.VMEM((2, 2, 128, 8, 128), BF),
            pltpu.VMEM((2, 32, 16, 128), BF),
            pltpu.VMEM((256, 512), BF),
            pltpu.VMEM((256, 512), BF),
            pltpu.VMEM((2, 2, 4, 64, 512), BF),
            pltpu.VMEM((128, 256), BF),
            pltpu.VMEM((128, 256), BF),
            pltpu.VMEM((2, 2, 2, 64, 256), BF),
            pltpu.VMEM((2, 16, 8, 8, 128), BF),
            pltpu.VMEM((2, 8, 4, 8, 128), BF),
            pltpu.VMEM((2, 128, 8, 128), BF),
            pltpu.VMEM((2, 128, 8, 128), BF),
            pltpu.VMEM((2, 4, 8, 16, 128), BF),
            dma((2,)),
            dma((2,)),
            dma((2, 2)),
            dma((2, 2)),
            dma((2,)),
            dma((2,)),
            dma((2, 2)),
            dma((2, 2)),
            dma((2, 2)),
            dma((2, 2)),
            pltpu.SemaphoreType.REGULAR,
            dma((2, 2)),
            dma((5,)),
            dma((5,)),
            dma((2,)),
            dma,
            dma,
            dma((2,)),
            dma((2,)),
        ],
        compiler_params=pltpu.CompilerParams(
            collective_id=0, has_side_effects=True, vmem_limit_bytes=56 << 20
        ),
    )(lengths, pair, sin, tin, tgate, tout, pin, pout, st_in, st_out)


def restore_kernel(lengths, staged, staged_single, out, sout, sems):
    first = jnp.where(lengths[0] > lengths[1], 0, 1)
    copies = [
        pltpu.make_async_copy(staged.at[micro ^ first, half], out.at[0, micro, half], sems.at[micro, half])
        for micro in range(2)
        for half in range(2)
    ]
    copies.append(pltpu.make_async_copy(staged_single, sout, sems.at[2, 0]))
    for copy in copies:
        copy.start()
    for copy in copies:
        copy.wait()


def restore(lengths, staged, staged_single):
    anywhere = pl.BlockSpec(memory_space=pl.ANY)
    return pl.pallas_call(
        restore_kernel,
        out_shape=(
            jax.ShapeDtypeStruct((1, 2, 2, 1024, 128), BF),
            jax.ShapeDtypeStruct((128, 384), BF),
        ),
        in_specs=[pl.BlockSpec(memory_space=pltpu.SMEM), anywhere, anywhere],
        out_specs=(pl.BlockSpec(memory_space=pltpu.VMEM),) * 2,
        scratch_shapes=[pltpu.SemaphoreType.DMA((3, 2))],
    )(lengths, staged, staged_single)


def on_device(pair, single, lengths, tri_in, tri_gate, tri_out, pt_in, pt_out, st_in, st_out):
    staged, staged_single = trunk(
        lengths,
        pair,
        single.reshape(128, 384),
        tri_in[0], tri_gate[0], tri_out[0], pt_in[0], pt_out[0], st_in[0], st_out[0],
    )
    out, sout = restore(lengths, staged, staged_single)
    return out.reshape(1, 2, 64, 32, 128), sout.reshape(1, 2, 64, 384)


def solution(mesh):
    section = P("section", None, None)
    in_specs = (P(None, "gr", "gc", None), P(None, "gr", None), P()) + (section,) * 7
    out_specs = (P("section", None, "gr", "gc", None), P("section", None, "gr", None))
    return jax.shard_map(
        on_device, mesh=mesh, in_specs=in_specs, out_specs=out_specs, check_vma=False
    )
```

```python
import jax
import jax.numpy as jnp
from jax import lax
from jax.experimental import pallas as pl
from jax.experimental.pallas import tpu as pltpu
from jax.sharding import PartitionSpec as P

MESH = pl.DeviceIdType.MESH
FULL, HALF = 0, 1
RIGHT, LEFT = 0, 1
BF = jnp.bfloat16
F32 = jnp.float32


def dot(a, b):
    return jnp.dot(a, b, preferred_element_type=F32)


def dot_nt(a, b):
    return lax.dot_general(a, b, (((1,), (1,)), ((), ())), preferred_element_type=F32)


def sigmoid(v):
    return 0.5 + 0.5 * jnp.tanh(0.5 * v)


def norm_lanes(v):
    center = v - jnp.mean(v, axis=-1, keepdims=True)
    spread = jnp.mean(center * center, axis=-1, keepdims=True)
    return center * lax.rsqrt(spread + 1e-05)


def silu_times(gates, ups):
    half = 0.5 * gates
    return ((half + half * jnp.tanh(half)) * ups).astype(BF)


def iota(shape, axis):
    return lax.broadcasted_iota(jnp.int32, shape, axis)


def trunk_kernel(
    lengths, pair, sin, tin, tgate, tout, pin, pout, st_in, st_out,
    out, sout,
    w_tin, w_gate, w_out, w_pin, w_pout, w_t, st_in_v, st_out_v, sin_next,
    own_sem, out_local, pair_in, zin, zout, normed, stage, settled, perm, order_full, order_half,
    sfull, sbuf, rbuf_full, rbuf_half, lm_full, raw_full, all_full, lm_half, raw_half, all_half,
    ts_full, ts_half, tr_full, tr_half, tr_last, z_peer, normed_peer, zlast, peer_send, peer_recv,
    relayed, relay_send, relay_recv, full_send, full_recv, fwd_send, fwd_recv, sib_send, sib_recv, back_send, back_recv,
    met, w_first, w_send, w_recv, st_sem, single_send, single_recv, out_send, out_recv,
):
    sec, gr, gc = lax.axis_index("section"), lax.axis_index("gr"), lax.axis_index("gc")
    y, core = lax.shift_right_logical(gr, 1), lax.bitwise_and(gr, 1)
    sy = sec * 4 + y
    x_hi, z_at = lax.shift_right_logical(gc, 3), lax.bitwise_and(gc, 7)
    plane = x_hi * 8 + sy
    channel = plane * 8 + z_at
    slot = gc * 8 + sy
    active = jnp.logical_and(y < 2, gc < 8)
    peer = {"section": 1 - sec, "gr": gr, "gc": gc}
    sibling = {"section": sec, "gr": gr + 1 - 2 * core, "gc": gc}

    def place(step):
        to_gc = lax.bitwise_and(gc + step, 15)
        to_sy = lax.bitwise_and(sy + lax.shift_right_logical(step, 4), 7)
        to_sec = lax.shift_right_logical(to_sy, 2)
        to_y = lax.bitwise_and(to_sy, 3)
        return to_gc, to_sy, {"section": to_sec, "gr": to_y * 2 + core, "gc": to_gc}

    def channel_of(at_gc, at_sy):
        at_plane = lax.shift_right_logical(at_gc, 3) * 8 + at_sy
        return at_plane * 8 + lax.bitwise_and(at_gc, 7)

    st_copies = [
        pltpu.make_async_copy(st_in, st_in_v, st_sem.at[0]),
        pltpu.make_async_copy(st_out, st_out_v, st_sem.at[1]),
    ]
    weights = [(tin, w_tin), (tgate, w_gate), (tout, w_out), (pin, w_pin), (pout, w_pout)]
    pair_copy = pltpu.make_async_copy(pair.at[:, pl.ds(sec * 32, 32)], pair_in, own_sem.at[5])
    own_copies = [
        pltpu.make_async_copy(own, held.at[sec], own_sem.at[index])
        for index, (own, held) in enumerate(weights)
    ]
    for copy in [pair_copy] + own_copies + st_copies:
        copy.start()

    barrier = pltpu.get_barrier_semaphore()

    def greet_line(semaphore):
        def greet(step, carry):
            to_gc = lax.bitwise_and(gc + step, 15)
            pl.semaphore_signal(
                semaphore, inc=1, device_id={"section": sec, "gr": gr, "gc": to_gc},
                device_id_type=MESH,
            )
            return carry

        lax.fori_loop(1, 16, greet, 0)

    pl.semaphore_signal(barrier, inc=1, device_id=sibling, device_id_type=MESH)
    for step in range(1, 8):
        pl.semaphore_signal(
            barrier, inc=1, device_id=place(step * 16)[2], device_id_type=MESH
        )
    greet_line(barrier)

    def weight_copy(index):
        own, held = weights[index]
        return pltpu.make_async_remote_copy(
            own, held.at[sec], w_send.at[index], w_recv.at[index],
            device_id=peer, device_id_type=MESH,
        )

    def first_copy(side):
        cols = pl.ds(256 - 256 * side, 256)
        return pltpu.make_async_remote_copy(
            tin.at[:, cols], w_tin.at[sec, :, cols], w_first.at[0, side], w_first.at[1, side],
            device_id=peer, device_id_type=MESH,
        )

    pl.semaphore_wait(barrier, 23)
    first_copy(RIGHT).start()
    first_copy(LEFT).start()
    greet_line(met)

    from_lane, to_lane = iota((128, 512), 0), iota((128, 512), 1)
    for low in range(4):
        target = (from_lane >> 5) * 128 + low * 32 + (from_lane & 31)
        perm[low] = jnp.where(to_lane == target, 1.0, 0.0).astype(BF)
    o, i = iota((256, 256), 0), iota((256, 256), 1)
    source = (o & 3) * 64 + ((o >> 5) & 1) * 32 + (o >> 6) * 8 + ((o >> 2) & 7)
    order_full[...] = jnp.where(i == source, 1.0, 0.0).astype(BF)
    o, i = iota((128, 128), 0), iota((128, 128), 1)
    source = (o & 3) * 32 + ((o >> 5) & 1) * 16 + (o >> 6) * 8 + ((o >> 2) & 7)
    order_half[...] = jnp.where(i == source, 1.0, 0.0).astype(BF)

    for copy in [pair_copy] + own_copies:
        copy.wait()
    first = jnp.where(lengths[0] > lengths[1], 0, 1)
    for kind, crop in ((FULL, first), (HALF, 1 - first)):
        z = pair_in[crop].reshape(1024, 128)
        zin[kind] = z
        normed[kind] = norm_lanes(z.astype(F32)).astype(BF)

    pl.semaphore_wait(met, 15)

    def await_weight(block, index):
        @pl.when(sec != block)
        def _():
            held = weights[index][1].at[block]
            pltpu.make_async_copy(held, held, w_recv.at[index]).wait()

    def gated(block, side, values):
        cols = slice(256 - 256 * side, 512 - 256 * side)
        p = dot_nt(w_t[block, cols], values)
        return sigmoid(p[0:128]) * p[128:256]

    def project_full(block, side):
        for part in range(2):
            value = gated(block, side, normed[FULL, pl.ds(part * 512, 512)])
            for sub in range(4):
                stage[pl.ds(part * 4 + sub, 128, stride=8), :] = value[:, sub * 128 : sub * 128 + 128]
        for part in range(4):
            values = stage[part * 256 : part * 256 + 256, :].astype(BF)
            sfull[block, side, part * 32 : part * 32 + 32] = values.reshape(32, 8, 128)

    def project_half(block):
        for part in range(4):
            values = normed[HALF, pl.ds(part * 256, 256)]
            for side in (LEFT, RIGHT):
                value = gated(block, side, values)
                row = part * 2 + 8 * (1 - side)
                for sub in range(2):
                    stage[pl.ds(row + sub, 128, stride=16), :] = value[:, sub * 128 : sub * 128 + 128]
        for part in range(8):
            values = stage[part * 256 : part * 256 + 256, :].astype(BF)
            sbuf[block, part * 16 : part * 16 + 16] = values.reshape(16, 16, 128)

    def send_full(block, side):
        def send(step, carry):
            to_gc, to_sy, device = place(step)
            pltpu.make_async_remote_copy(
                sfull.at[block, side, channel_of(to_gc, to_sy)], rbuf_full.at[block, side, slot],
                full_send.at[block, side], full_recv.at[block, side],
                device_id=device, device_id_type=MESH,
            ).start()
            return carry

        lax.fori_loop(1, 128, send, 0)
        pltpu.make_async_copy(
            sfull.at[block, side, channel], rbuf_full.at[block, side, slot],
            full_recv.at[block, side],
        ).start()

    def send_half(block):
        source = sec * 2 + y
        for step in range(1, 16):
            to_plane = lax.bitwise_and(plane + step, 15)
            to_sy = lax.bitwise_and(to_plane, 7)
            pltpu.make_async_remote_copy(
                sbuf.at[block, pl.ds(to_plane * 8, 8)], relayed.at[block, source],
                relay_send.at[block], relay_recv.at[block],
                device_id={
                    "section": lax.shift_right_logical(to_sy, 2),
                    "gr": lax.bitwise_and(to_sy, 3) * 2 + core,
                    "gc": lax.shift_right_logical(to_plane, 3) * 8 + z_at,
                },
                device_id_type=MESH,
            ).start()
        pltpu.make_async_copy(
            sbuf.at[block, pl.ds(plane * 8, 8)], relayed.at[block, source],
            relay_recv.at[block],
        ).start()

    def relay(block):
        landed = relayed.at[block]
        pltpu.make_async_copy(landed, landed, relay_recv.at[block]).wait()
        at = rbuf_half.at[block, pl.ds(z_at * 4, 4)]
        for step in range(1, 8):
            to_z = lax.bitwise_and(z_at + step, 7)
            pltpu.make_async_remote_copy(
                relayed.at[block, :, to_z], at, fwd_send.at[block], fwd_recv.at[block],
                device_id={"section": sec, "gr": gr, "gc": x_hi * 8 + to_z},
                device_id_type=MESH,
            ).start()
        pltpu.make_async_copy(relayed.at[block, :, z_at], at, fwd_recv.at[block]).start()

    def forward(block, kind):
        if kind == FULL:
            for side in (RIGHT, LEFT):
                project_full(block, side)
                send_full(block, side)
        else:

            @pl.when(active)
            def _():
                project_half(block)
                send_half(block)

    def parts_of(kind):
        if kind == FULL:
            return lm_full, all_full, ts_full, 4, 8
        return lm_half, all_half, ts_half, 2, 4

    def share_right(block, kind, g, ordered):
        whole = all_full if kind == FULL else all_half
        lanes = slice(g * 128, g * 128 + 128)
        whole[block, core, :, :, lanes] = ordered.astype(BF).reshape(-1, 64, 128)
        mine = whole.at[block, core, :, :, lanes]
        pltpu.make_async_remote_copy(
            mine, mine, sib_send.at[block, kind], sib_recv.at[block, kind],
            device_id=sibling, device_id_type=MESH,
        ).start()

    def triangle_full(block, side):
        landed = rbuf_full.at[block, side]
        pltpu.make_async_copy(landed, landed, full_recv.at[block, side]).wait()
        held = raw_full if side == RIGHT else lm_full
        for g in range(4):
            total = None
            for low in range(4):
                col = (g * 4 + low) * 8
                block_in = rbuf_full[block, side, col : col + 8].astype(F32)
                term = dot(block_in.reshape(64, 128).astype(BF), perm[low])
                total = term if total is None else total + term
            total = total.astype(BF)
            lanes = slice(g * 128, g * 128 + 128)
            for low in range(4):
                held[low * 64 : low * 64 + 64, lanes] = total[:, low * 128 : low * 128 + 128]
            if side == RIGHT:
                share_right(block, FULL, g, dot(order_full[...], raw_full[:, lanes]))

    def triangle_half(block):
        landed = rbuf_half.at[block]
        pltpu.make_async_copy(landed, landed, fwd_recv.at[block]).wait()
        for g in range(2):
            total = None
            for low in range(4):
                col = (g * 4 + low) * 4
                block_in = rbuf_half[block, col : col + 4].reshape(64, 128)
                term = dot(block_in, perm[low])
                total = term if total is None else total + term
            total = total.reshape(4, 16, 512)
            left = total[:, 0:8].reshape(32, 512).astype(BF)
            right = total[:, 8:16].reshape(32, 512).astype(BF)
            lanes = slice(g * 128, g * 128 + 128)
            for low in range(4):
                cols = slice(low * 128, low * 128 + 128)
                lm_half[low * 32 : low * 32 + 32, lanes] = left[:, cols]
                raw_half[low * 32 : low * 32 + 32, lanes] = right[:, cols]
            share_right(block, HALF, g, dot(order_half[...], raw_half[:, lanes]))

    def triangle_out(block, kind):
        lm, whole, ts, groups, tiles = parts_of(kind)
        rows = tiles * 8
        full = kind == FULL
        other = whole.at[block, 1 - core]
        pltpu.make_async_copy(other, other, sib_recv.at[block, kind]).wait()
        home = lax.bitwise_and(lax.shift_right_logical(gc, 2), groups - 1)
        source = sy if full else sec * 2 + y

        for turn in range(groups):
            g = lax.bitwise_and(home + turn, groups - 1)
            right = jnp.concatenate([whole[block, 0, g], whole[block, 1, g]], axis=0)
            product = dot_nt(lm[...], right).astype(BF)
            total = None
            for low in range(4):
                term = dot(product[low * rows : (low + 1) * rows], perm[low])
                total = term if total is None else total + term
            total = total.astype(BF)
            for low in range(4):
                ts[block, g * 4 + low] = total[:, low * 128 : low * 128 + 128].reshape(
                    tiles, 8, 128
                )

            def send(step, carry):
                to_gc = g * 4 + lax.bitwise_and(gc + step, 3)
                to_tile = lax.bitwise_and(source + lax.shift_right_logical(step, 2), tiles - 1)
                to_sec = lax.shift_right_logical(to_tile, 2 if full else 1)
                to_y = lax.bitwise_and(to_tile, tiles // 2 - 1)

                if full:
                    target = tr_full.at[block, channel]
                elif block == 0:
                    target = tr_half.at[channel]
                else:
                    target = tr_last.at[to_sec, channel]
                    to_sec = 1

                def local():
                    pltpu.make_async_copy(
                        ts.at[block, to_gc, to_tile], target,
                        back_recv.at[block, kind],
                    ).start()

                def remote():
                    pltpu.make_async_remote_copy(
                        ts.at[block, to_gc, to_tile], target,
                        back_send.at[block, kind], back_recv.at[block, kind],
                        device_id={"section": to_sec, "gr": to_y * 2 + core, "gc": to_gc},
                        device_id_type=MESH,
                    ).start()

                if turn == 0:
                    itself = step == 0
                    if not full and block == 1:
                        itself = jnp.logical_and(to_gc == gc, to_y == y)
                        itself = jnp.logical_and(itself, sec == 1)
                    if not full:
                        itself = jnp.logical_and(itself, active)
                    pl.when(itself)(local)
                    pl.when(jnp.logical_not(itself))(remote)
                else:
                    remote()
                return carry

            lax.fori_loop(0, tiles * 4, send, 0)

    def complete(block, tr, z, normed_in, parts, put):
        values = tr[...].astype(F32)
        center = values - jnp.mean(values, axis=0, keepdims=True)
        spread = jnp.mean(center * center, axis=0, keepdims=True)
        center = center * lax.rsqrt(spread + 1e-05)
        stage[0:1024, :] = center.reshape(1024, 128)
        for r in range(8):
            tile = stage[pl.ds(r, 128, stride=8), :]
            settled[r * 128 : r * 128 + 128] = tile.astype(BF).T
        for part in range(parts):
            rows = pl.ds(part * (1024 // parts), 1024 // parts)
            gate = sigmoid(dot(normed_in[rows], w_gate[block]))
            update = dot(settled[rows], w_out[block])
            updated = (z[rows].astype(F32) + gate * update).astype(BF)
            trans_in = norm_lanes(updated.astype(F32)).astype(BF)
            gates = dot(trans_in, w_pin[block, :, 0:512])
            ups = dot(trans_in, w_pin[block, :, 512:1024])
            inner = silu_times(gates, ups)
            done = (updated.astype(F32) + dot(inner, w_pout[block])).astype(BF)
            put(part, rows, done)

    def await_back(block, kind, landed):
        if kind == FULL:
            pltpu.make_async_copy(landed, landed, back_recv.at[block, kind]).wait()
        else:

            @pl.when(active)
            def _():
                pltpu.make_async_copy(landed, landed, back_recv.at[block, kind]).wait()

            @pl.when(jnp.logical_not(active))
            def _():
                landed[...] = jnp.zeros(landed.shape, BF)

    def finish(block, kind):
        z = (zin if block == 0 else zout.at[0]).at[kind]
        landed = tr_full.at[block] if kind == FULL else tr_half
        parts = 1 if block == 0 else 2
        await_back(block, kind, landed)

        def put(part, rows, done):
            zout[block, kind, rows] = done
            if block == 0:
                normed[kind, rows] = norm_lanes(done.astype(F32)).astype(BF)
            else:
                deliver(block, kind, part, parts)

        complete(block, landed, z, normed.at[kind], parts, put)

    def finish_last():
        await_back(1, HALF, tr_last)
        pltpu.make_async_copy(z_peer, z_peer, peer_recv).wait()
        normed_peer[...] = norm_lanes(z_peer[...].astype(F32)).astype(BF)
        for half in range(2):

            def put(part, rows, done):
                zlast[half, rows] = done
                pltpu.make_async_copy(
                    zlast.at[half, rows], out.at[HALF, half, rows], out_local.at[HALF]
                ).start()

            own = half == 1
            complete(
                1,
                tr_last.at[half],
                zout.at[0, HALF] if own else z_peer,
                normed.at[HALF] if own else normed_peer,
                1,
                put,
            )

    peer_copy = pltpu.make_async_remote_copy(
        zout.at[0, HALF], z_peer, peer_send, peer_recv, device_id=peer, device_id_type=MESH
    )

    def deliver(block, kind, part=0, parts=1):
        rows = pl.ds(part * (1024 // parts), 1024 // parts)

        @pl.when(sec == block)
        def _():
            pltpu.make_async_copy(
                zout.at[block, kind, rows], out.at[kind, sec, rows], out_local.at[kind]
            ).start()

        @pl.when(sec != block)
        def _():
            pltpu.make_async_remote_copy(
                zout.at[block, kind, rows], out.at[kind, sec, rows],
                out_send.at[kind], out_recv.at[kind],
                device_id=peer, device_id_type=MESH,
            ).start()

    def single(rows_in):
        value = rows_in[...].astype(F32)
        value_in = norm_lanes(value).astype(BF)
        total = value
        for part in range(6):
            cols = part * 256
            gates = dot(value_in, st_in_v[:, cols : cols + 256])
            ups = dot(value_in, st_in_v[:, 1536 + cols : 1536 + cols + 256])
            inner = silu_times(gates, ups)
            total = total + dot(inner, st_out_v[cols : cols + 256])
        sout[...] = total.astype(BF)

    single_copy = pltpu.make_async_remote_copy(
        sout, sin_next, single_send, single_recv, device_id=peer, device_id_type=MESH
    )

    def start_block(block, side):
        cols = slice(256 - 256 * side, 512 - 256 * side)

        @pl.when(sec != block)
        def _():
            held = w_tin.at[block, :, cols]
            pltpu.make_async_copy(held, held, w_first.at[1, side]).wait()

        w_t[block, cols] = w_tin[block, :, cols].astype(F32).T.astype(BF)

    def more_weights():
        for index in range(1, 5):
            weight_copy(index).start()

    def rest_weights(block):
        for index in range(1, 5):
            await_weight(block, index)

    def single_turn(block):
        @pl.when(sec == block)
        def _():
            for copy in st_copies:
                copy.wait()
            if block == 0:
                single(sin)
                single_copy.start()
            else:
                single_copy.wait_recv()
                single(sin_next)

    start_block(0, RIGHT)
    project_full(0, RIGHT)
    send_full(0, RIGHT)
    start_block(0, LEFT)
    project_full(0, LEFT)
    send_full(0, LEFT)
    forward(0, HALF)
    more_weights()
    single_turn(0)
    triangle_full(0, RIGHT)
    triangle_full(0, LEFT)
    relay(0)
    triangle_out(0, FULL)
    triangle_half(0)
    triangle_out(0, HALF)
    start_block(1, RIGHT)
    start_block(1, LEFT)
    rest_weights(0)
    finish(0, FULL)
    forward(1, FULL)
    finish(0, HALF)
    forward(1, HALF)
    deliver(0, FULL)
    deliver(0, HALF)
    pl.when(sec == 0)(peer_copy.start)
    single_turn(1)
    triangle_full(1, RIGHT)
    triangle_full(1, LEFT)
    relay(1)
    triangle_out(1, FULL)
    triangle_half(1)
    triangle_out(1, HALF)
    rest_weights(1)
    pl.when(jnp.logical_and(sec == 1, jnp.logical_not(active)))(finish_last)
    finish(1, FULL)
    pl.when(jnp.logical_and(sec == 1, active))(finish_last)

    def end_forward(block, kind):
        if kind == FULL:
            for side in (RIGHT, LEFT):
                sent = rbuf_full.at[block, side, pl.ds(0, 127)]
                pltpu.make_async_copy(sent, sent, full_send.at[block, side]).wait()
        else:
            sent = sbuf.at[block, pl.ds(0, 28)]
            pltpu.make_async_copy(sent, sent, fwd_send.at[block]).wait()
            sent = sbuf.at[block, pl.ds(0, 120)]
            pl.when(active)(pltpu.make_async_copy(sent, sent, relay_send.at[block]).wait)

    def end_triangle(block, kind):
        mine = (all_full if kind == FULL else all_half).at[block, core]
        pltpu.make_async_copy(mine, mine, sib_send.at[block, kind]).wait()

    def end_back(block, kind):
        def wait(count):
            sent = tr_full.at[block, pl.ds(0, count)]
            pltpu.make_async_copy(sent, sent, back_send.at[block, kind]).wait()

        if kind == FULL:
            wait(127)
        else:
            own = active if block == 0 else jnp.logical_and(active, sec == 1)
            pl.when(own)(lambda: wait(31 if block == 0 else 30))
            pl.when(jnp.logical_not(own))(lambda: wait(32))

    def end_rest():
        first_copy(RIGHT).wait_send()
        first_copy(LEFT).wait_send()
        for index in range(1, 5):
            weight_copy(index).wait_send()
        pl.when(sec == 0)(single_copy.wait_send)

    def end_deliver(kind):
        given = pltpu.make_async_copy(zout.at[0, kind], zout.at[0, kind], out_send.at[kind])
        kept = out.at[kind, sec]
        kept = pltpu.make_async_copy(kept, kept, out_local.at[kind])
        taken = out.at[kind, 1 - sec]
        taken = pltpu.make_async_copy(taken, taken, out_recv.at[kind])
        if kind == FULL:
            given.wait()
            kept.wait()
            taken.wait()
        else:

            @pl.when(sec == 0)
            def _():
                peer_copy.wait_send()
                kept.wait()
                taken.wait()

            @pl.when(sec == 1)
            def _():
                given.wait()
                both = out.at[kind]
                pltpu.make_async_copy(both, both, out_local.at[kind]).wait()

    for block in range(2):
        for kind in (FULL, HALF):
            end_forward(block, kind)
            end_triangle(block, kind)
            end_back(block, kind)
    end_rest()
    end_deliver(FULL)
    end_deliver(HALF)


def trunk(lengths, pair, sin, tin, tgate, tout, pin, pout, st_in, st_out):
    vmem = pl.BlockSpec(memory_space=pltpu.VMEM)
    anywhere = pl.BlockSpec(memory_space=pl.ANY)
    dma = pltpu.SemaphoreType.DMA
    return pl.pallas_call(
        trunk_kernel,
        out_shape=(
            jax.ShapeDtypeStruct((2, 2, 1024, 128), BF),
            jax.ShapeDtypeStruct((128, 384), BF),
        ),
        in_specs=[pl.BlockSpec(memory_space=pltpu.SMEM), anywhere, vmem] + [anywhere] * 7,
        out_specs=(anywhere, vmem),
        scratch_shapes=[
            pltpu.VMEM((2, 128, 512), BF),
            pltpu.VMEM((2, 128, 128), BF),
            pltpu.VMEM((2, 128, 128), BF),
            pltpu.VMEM((2, 128, 1024), BF),
            pltpu.VMEM((2, 512, 128), BF),
            pltpu.VMEM((2, 512, 128), BF),
            pltpu.VMEM((384, 3072), BF),
            pltpu.VMEM((1536, 384), BF),
            pltpu.VMEM((128, 384), BF),
            dma((6,)),
            dma((2,)),
            pltpu.VMEM((2, 32, 32, 128), BF),
            pltpu.VMEM((2, 1024, 128), BF),
            pltpu.VMEM((2, 2, 1024, 128), BF),
            pltpu.VMEM((2, 1024, 128), BF),
            pltpu.VMEM((2048, 128), F32),
            pltpu.VMEM((1024, 128), BF),
            pltpu.VMEM((4, 128, 512), BF),
            pltpu.VMEM((256, 256), BF),
            pltpu.VMEM((128, 128), BF),
            pltpu.VMEM((2, 2, 128, 8, 128), BF),
            pltpu.VMEM((2, 128, 16, 128), BF),
            pltpu.VMEM((2, 2, 128, 8, 128), BF),
            pltpu.VMEM((2, 32, 16, 128), BF),
            pltpu.VMEM((256, 512), BF),
            pltpu.VMEM((256, 512), BF),
            pltpu.VMEM((2, 2, 4, 64, 512), BF),
            pltpu.VMEM((128, 256), BF),
            pltpu.VMEM((128, 256), BF),
            pltpu.VMEM((2, 2, 2, 64, 256), BF),
            pltpu.VMEM((2, 16, 8, 8, 128), BF),
            pltpu.VMEM((2, 8, 4, 8, 128), BF),
            pltpu.VMEM((2, 128, 8, 128), BF),
            pltpu.VMEM((128, 8, 128), BF),
            pltpu.VMEM((2, 128, 8, 128), BF),
            pltpu.VMEM((1024, 128), BF),
            pltpu.VMEM((1024, 128), BF),
            pltpu.VMEM((2, 1024, 128), BF),
            dma,
            dma,
            pltpu.VMEM((2, 4, 8, 16, 128), BF),
            dma((2,)),
            dma((2,)),
            dma((2, 2)),
            dma((2, 2)),
            dma((2,)),
            dma((2,)),
            dma((2, 2)),
            dma((2, 2)),
            dma((2, 2)),
            dma((2, 2)),
            pltpu.SemaphoreType.REGULAR,
            dma((2, 2)),
            dma((5,)),
            dma((5,)),
            dma((2,)),
            dma,
            dma,
            dma((2,)),
            dma((2,)),
        ],
        compiler_params=pltpu.CompilerParams(
            collective_id=0, has_side_effects=True, vmem_limit_bytes=56 << 20
        ),
    )(lengths, pair, sin, tin, tgate, tout, pin, pout, st_in, st_out)


def restore_kernel(lengths, staged, staged_single, out, sout, sems):
    first = jnp.where(lengths[0] > lengths[1], 0, 1)
    copies = [
        pltpu.make_async_copy(staged.at[micro ^ first, half], out.at[0, micro, half], sems.at[micro, half])
        for micro in range(2)
        for half in range(2)
    ]
    copies.append(pltpu.make_async_copy(staged_single, sout, sems.at[2, 0]))
    for copy in copies:
        copy.start()
    for copy in copies:
        copy.wait()


def restore(lengths, staged, staged_single):
    anywhere = pl.BlockSpec(memory_space=pl.ANY)
    return pl.pallas_call(
        restore_kernel,
        out_shape=(
            jax.ShapeDtypeStruct((1, 2, 2, 1024, 128), BF),
            jax.ShapeDtypeStruct((128, 384), BF),
        ),
        in_specs=[pl.BlockSpec(memory_space=pltpu.SMEM), anywhere, anywhere],
        out_specs=(pl.BlockSpec(memory_space=pltpu.VMEM),) * 2,
        scratch_shapes=[pltpu.SemaphoreType.DMA((3, 2))],
    )(lengths, staged, staged_single)


def on_device(pair, single, lengths, tri_in, tri_gate, tri_out, pt_in, pt_out, st_in, st_out):
    staged, staged_single = trunk(
        lengths,
        pair,
        single.reshape(128, 384),
        tri_in[0], tri_gate[0], tri_out[0], pt_in[0], pt_out[0], st_in[0], st_out[0],
    )
    out, sout = restore(lengths, staged, staged_single)
    return out.reshape(1, 2, 64, 32, 128), sout.reshape(1, 2, 64, 384)


def solution(mesh):
    section = P("section", None, None)
    in_specs = (P(None, "gr", "gc", None), P(None, "gr", None), P()) + (section,) * 7
    out_specs = (P("section", None, "gr", "gc", None), P("section", None, "gr", None))
    return jax.shard_map(
        on_device, mesh=mesh, in_specs=in_specs, out_specs=out_specs, check_vma=False
    )
```

```python
import jax
import jax.numpy as jnp
from jax import lax
from jax.experimental import pallas as pl
from jax.experimental.pallas import tpu as pltpu
from jax.sharding import PartitionSpec as P

MESH = pl.DeviceIdType.MESH
FULL, HALF = 0, 1
RIGHT, LEFT = 0, 1
BF = jnp.bfloat16
F32 = jnp.float32


def dot(a, b):
    return jnp.dot(a, b, preferred_element_type=F32)


def dot_nt(a, b):
    return lax.dot_general(a, b, (((1,), (1,)), ((), ())), preferred_element_type=F32)


def sigmoid(v):
    return 0.5 + 0.5 * jnp.tanh(0.5 * v)


def norm_lanes(v):
    center = v - jnp.mean(v, axis=-1, keepdims=True)
    spread = jnp.mean(center * center, axis=-1, keepdims=True)
    return center * lax.rsqrt(spread + 1e-05)


def silu_times(gates, ups):
    half = 0.5 * gates
    return ((half + half * jnp.tanh(half)) * ups).astype(BF)


def iota(shape, axis):
    return lax.broadcasted_iota(jnp.int32, shape, axis)


def trunk_kernel(
    lengths, pair, sin, tin, tgate, tout, pin, pout, st_in, st_out,
    out, sout,
    w_tin, w_gate, w_out, w_pin, w_pout, w_t, st_in_v, st_out_v, sin_next,
    own_sem, out_local, pair_in, zin, zout, normed, stage, settled, perm, order_full, order_half,
    sfull, sbuf, rbuf_full, rbuf_half, lm_full, raw_full, all_full, lm_half, raw_half, all_half,
    ts_full, ts_half, tr_full, tr_half, tr_last, z_peer, normed_peer, zlast, peer_send, peer_recv,
    relayed, relay_send, relay_recv, full_send, full_recv, fwd_send, fwd_recv, sib_send, sib_recv, back_send, back_recv,
    met, w_first, w_send, w_recv, st_sem, single_send, single_recv, out_send, out_recv,
):
    sec, gr, gc = lax.axis_index("section"), lax.axis_index("gr"), lax.axis_index("gc")
    y, core = lax.shift_right_logical(gr, 1), lax.bitwise_and(gr, 1)
    sy = sec * 4 + y
    x_hi, z_at = lax.shift_right_logical(gc, 3), lax.bitwise_and(gc, 7)
    plane = x_hi * 8 + sy
    channel = plane * 8 + z_at
    slot = gc * 8 + sy
    active = jnp.logical_and(y < 2, gc < 8)
    peer = {"section": 1 - sec, "gr": gr, "gc": gc}
    sibling = {"section": sec, "gr": gr + 1 - 2 * core, "gc": gc}

    def place(step):
        to_gc = lax.bitwise_and(gc + step, 15)
        to_sy = lax.bitwise_and(sy + lax.shift_right_logical(step, 4), 7)
        to_sec = lax.shift_right_logical(to_sy, 2)
        to_y = lax.bitwise_and(to_sy, 3)
        return to_gc, to_sy, {"section": to_sec, "gr": to_y * 2 + core, "gc": to_gc}

    def channel_of(at_gc, at_sy):
        at_plane = lax.shift_right_logical(at_gc, 3) * 8 + at_sy
        return at_plane * 8 + lax.bitwise_and(at_gc, 7)

    st_copies = [
        pltpu.make_async_copy(st_in, st_in_v, st_sem.at[0]),
        pltpu.make_async_copy(st_out, st_out_v, st_sem.at[1]),
    ]
    weights = [(tin, w_tin), (tgate, w_gate), (tout, w_out), (pin, w_pin), (pout, w_pout)]
    pair_copy = pltpu.make_async_copy(pair.at[:, pl.ds(sec * 32, 32)], pair_in, own_sem.at[5])
    own_copies = [
        pltpu.make_async_copy(own, held.at[sec], own_sem.at[index])
        for index, (own, held) in enumerate(weights)
    ]
    for copy in [pair_copy] + own_copies + st_copies:
        copy.start()

    barrier = pltpu.get_barrier_semaphore()

    def greet_line(semaphore):
        def greet(step, carry):
            to_gc = lax.bitwise_and(gc + step, 15)
            pl.semaphore_signal(
                semaphore, inc=1, device_id={"section": sec, "gr": gr, "gc": to_gc},
                device_id_type=MESH,
            )
            return carry

        lax.fori_loop(1, 16, greet, 0)

    pl.semaphore_signal(barrier, inc=1, device_id=sibling, device_id_type=MESH)
    for step in range(1, 8):
        pl.semaphore_signal(
            barrier, inc=1, device_id=place(step * 16)[2], device_id_type=MESH
        )
    greet_line(barrier)

    def weight_copy(index):
        own, held = weights[index]
        return pltpu.make_async_remote_copy(
            own, held.at[sec], w_send.at[index], w_recv.at[index],
            device_id=peer, device_id_type=MESH,
        )

    def first_copy(side):
        cols = pl.ds(256 - 256 * side, 256)
        return pltpu.make_async_remote_copy(
            tin.at[:, cols], w_tin.at[sec, :, cols], w_first.at[0, side], w_first.at[1, side],
            device_id=peer, device_id_type=MESH,
        )

    pl.semaphore_wait(barrier, 23)
    first_copy(RIGHT).start()
    first_copy(LEFT).start()
    greet_line(met)

    from_lane, to_lane = iota((128, 512), 0), iota((128, 512), 1)
    for low in range(4):
        target = (from_lane >> 5) * 128 + low * 32 + (from_lane & 31)
        perm[low] = jnp.where(to_lane == target, 1.0, 0.0).astype(BF)
    o, i = iota((256, 256), 0), iota((256, 256), 1)
    source = (o & 3) * 64 + ((o >> 5) & 1) * 32 + (o >> 6) * 8 + ((o >> 2) & 7)
    order_full[...] = jnp.where(i == source, 1.0, 0.0).astype(BF)
    o, i = iota((128, 128), 0), iota((128, 128), 1)
    source = (o & 3) * 32 + ((o >> 5) & 1) * 16 + (o >> 6) * 8 + ((o >> 2) & 7)
    order_half[...] = jnp.where(i == source, 1.0, 0.0).astype(BF)

    for copy in [pair_copy] + own_copies:
        copy.wait()
    first = jnp.where(lengths[0] > lengths[1], 0, 1)
    for kind, crop in ((FULL, first), (HALF, 1 - first)):
        z = pair_in[crop].reshape(1024, 128)
        zin[kind] = z
        normed[kind] = norm_lanes(z.astype(F32)).astype(BF)

    pl.semaphore_wait(met, 15)

    def await_weight(block, index):
        @pl.when(sec != block)
        def _():
            held = weights[index][1].at[block]
            pltpu.make_async_copy(held, held, w_recv.at[index]).wait()

    def gated(block, side, values):
        cols = slice(256 - 256 * side, 512 - 256 * side)
        p = dot_nt(w_t[block, cols], values)
        return sigmoid(p[0:128]) * p[128:256]

    def project_full(block, side):
        for part in range(2):
            value = gated(block, side, normed[FULL, pl.ds(part * 512, 512)])
            for sub in range(4):
                stage[pl.ds(part * 4 + sub, 128, stride=8), :] = value[:, sub * 128 : sub * 128 + 128]
        for part in range(4):
            values = stage[part * 256 : part * 256 + 256, :].astype(BF)
            sfull[block, side, part * 32 : part * 32 + 32] = values.reshape(32, 8, 128)

    def project_half(block):
        for part in range(4):
            values = normed[HALF, pl.ds(part * 256, 256)]
            for side in (LEFT, RIGHT):
                value = gated(block, side, values)
                row = part * 2 + 8 * (1 - side)
                for sub in range(2):
                    stage[pl.ds(row + sub, 128, stride=16), :] = value[:, sub * 128 : sub * 128 + 128]
        for part in range(8):
            values = stage[part * 256 : part * 256 + 256, :].astype(BF)
            sbuf[block, part * 16 : part * 16 + 16] = values.reshape(16, 16, 128)

    def send_full(block, side):
        for turn in range(8):
            to_sy = lax.bitwise_and(sy + turn, 7)
            to_row = lax.bitwise_and(to_sy, 3) * 2 + core
            to_sec = lax.shift_right_logical(to_sy, 2)

            def send(step, carry):
                to_gc = lax.bitwise_and(gc + step, 15)
                pltpu.make_async_remote_copy(
                    sfull.at[block, side, channel_of(to_gc, to_sy)],
                    rbuf_full.at[block, side, slot],
                    full_send.at[block, side], full_recv.at[block, side],
                    device_id={"section": to_sec, "gr": to_row, "gc": to_gc},
                    device_id_type=MESH,
                ).start()
                return carry

            first = 1 if turn == 0 else 0
            lax.fori_loop(first, 16, send, 0, unroll=5 if turn == 0 else 4)
        pltpu.make_async_copy(
            sfull.at[block, side, channel], rbuf_full.at[block, side, slot],
            full_recv.at[block, side],
        ).start()

    def send_half(block):
        source = sec * 2 + y
        for step in range(1, 16):
            to_plane = lax.bitwise_and(plane + step, 15)
            to_sy = lax.bitwise_and(to_plane, 7)
            pltpu.make_async_remote_copy(
                sbuf.at[block, pl.ds(to_plane * 8, 8)], relayed.at[block, source],
                relay_send.at[block], relay_recv.at[block],
                device_id={
                    "section": lax.shift_right_logical(to_sy, 2),
                    "gr": lax.bitwise_and(to_sy, 3) * 2 + core,
                    "gc": lax.shift_right_logical(to_plane, 3) * 8 + z_at,
                },
                device_id_type=MESH,
            ).start()
        pltpu.make_async_copy(
            sbuf.at[block, pl.ds(plane * 8, 8)], relayed.at[block, source],
            relay_recv.at[block],
        ).start()

    def relay(block):
        landed = relayed.at[block]
        pltpu.make_async_copy(landed, landed, relay_recv.at[block]).wait()
        at = rbuf_half.at[block, pl.ds(z_at * 4, 4)]
        for step in range(1, 8):
            to_z = lax.bitwise_and(z_at + step, 7)
            pltpu.make_async_remote_copy(
                relayed.at[block, :, to_z], at, fwd_send.at[block], fwd_recv.at[block],
                device_id={"section": sec, "gr": gr, "gc": x_hi * 8 + to_z},
                device_id_type=MESH,
            ).start()
        pltpu.make_async_copy(relayed.at[block, :, z_at], at, fwd_recv.at[block]).start()

    def forward(block, kind):
        if kind == FULL:
            for side in (RIGHT, LEFT):
                project_full(block, side)
                send_full(block, side)
        else:

            @pl.when(active)
            def _():
                project_half(block)
                send_half(block)

    def parts_of(kind):
        if kind == FULL:
            return lm_full, all_full, ts_full, 4, 8
        return lm_half, all_half, ts_half, 2, 4

    def share_right(block, kind, g, ordered):
        whole = all_full if kind == FULL else all_half
        lanes = slice(g * 128, g * 128 + 128)
        whole[block, core, :, :, lanes] = ordered.astype(BF).reshape(-1, 64, 128)
        mine = whole.at[block, core, :, :, lanes]
        pltpu.make_async_remote_copy(
            mine, mine, sib_send.at[block, kind], sib_recv.at[block, kind],
            device_id=sibling, device_id_type=MESH,
        ).start()

    def triangle_full(block, side):
        landed = rbuf_full.at[block, side]
        pltpu.make_async_copy(landed, landed, full_recv.at[block, side]).wait()
        held = raw_full if side == RIGHT else lm_full
        for g in range(4):
            total = None
            for low in range(4):
                col = (g * 4 + low) * 8
                block_in = rbuf_full[block, side, col : col + 8].astype(F32)
                term = dot(block_in.reshape(64, 128).astype(BF), perm[low])
                total = term if total is None else total + term
            total = total.astype(BF)
            lanes = slice(g * 128, g * 128 + 128)
            for low in range(4):
                held[low * 64 : low * 64 + 64, lanes] = total[:, low * 128 : low * 128 + 128]
            if side == RIGHT:
                share_right(block, FULL, g, dot(order_full[...], raw_full[:, lanes]))

    def triangle_half(block):
        landed = rbuf_half.at[block]
        pltpu.make_async_copy(landed, landed, fwd_recv.at[block]).wait()
        for g in range(2):
            total = None
            for low in range(4):
                col = (g * 4 + low) * 4
                block_in = rbuf_half[block, col : col + 4].reshape(64, 128)
                term = dot(block_in, perm[low])
                total = term if total is None else total + term
            total = total.reshape(4, 16, 512)
            left = total[:, 0:8].reshape(32, 512).astype(BF)
            right = total[:, 8:16].reshape(32, 512).astype(BF)
            lanes = slice(g * 128, g * 128 + 128)
            for low in range(4):
                cols = slice(low * 128, low * 128 + 128)
                lm_half[low * 32 : low * 32 + 32, lanes] = left[:, cols]
                raw_half[low * 32 : low * 32 + 32, lanes] = right[:, cols]
            share_right(block, HALF, g, dot(order_half[...], raw_half[:, lanes]))

    def triangle_out(block, kind):
        lm, whole, ts, groups, tiles = parts_of(kind)
        rows = tiles * 8
        full = kind == FULL
        other = whole.at[block, 1 - core]
        pltpu.make_async_copy(other, other, sib_recv.at[block, kind]).wait()
        home = lax.bitwise_and(lax.shift_right_logical(gc, 2), groups - 1)
        source = sy if full else sec * 2 + y

        for turn in range(groups):
            g = lax.bitwise_and(home + turn, groups - 1)
            right = jnp.concatenate([whole[block, 0, g], whole[block, 1, g]], axis=0)
            product = dot_nt(lm[...], right).astype(BF)
            total = None
            for low in range(4):
                term = dot(product[low * rows : (low + 1) * rows], perm[low])
                total = term if total is None else total + term
            total = total.astype(BF)
            for low in range(4):
                ts[block, g * 4 + low] = total[:, low * 128 : low * 128 + 128].reshape(
                    tiles, 8, 128
                )

            def send(step, carry):
                to_gc = g * 4 + lax.bitwise_and(gc + step, 3)
                to_tile = lax.bitwise_and(source + lax.shift_right_logical(step, 2), tiles - 1)
                to_sec = lax.shift_right_logical(to_tile, 2 if full else 1)
                to_y = lax.bitwise_and(to_tile, tiles // 2 - 1)

                if full:
                    target = tr_full.at[block, channel]
                elif block == 0:
                    target = tr_half.at[channel]
                else:
                    target = tr_last.at[to_sec, channel]
                    to_sec = 1

                def local():
                    pltpu.make_async_copy(
                        ts.at[block, to_gc, to_tile], target,
                        back_recv.at[block, kind],
                    ).start()

                def remote():
                    pltpu.make_async_remote_copy(
                        ts.at[block, to_gc, to_tile], target,
                        back_send.at[block, kind], back_recv.at[block, kind],
                        device_id={"section": to_sec, "gr": to_y * 2 + core, "gc": to_gc},
                        device_id_type=MESH,
                    ).start()

                if turn == 0:
                    itself = step == 0
                    if not full and block == 1:
                        itself = jnp.logical_and(to_gc == gc, to_y == y)
                        itself = jnp.logical_and(itself, sec == 1)
                    if not full:
                        itself = jnp.logical_and(itself, active)
                    pl.when(itself)(local)
                    pl.when(jnp.logical_not(itself))(remote)
                else:
                    remote()
                return carry

            lax.fori_loop(0, tiles * 4, send, 0, unroll=4)

    def complete(block, tr, z, normed_in, parts, put):
        values = tr[...].astype(F32)
        center = values - jnp.mean(values, axis=0, keepdims=True)
        spread = jnp.mean(center * center, axis=0, keepdims=True)
        center = center * lax.rsqrt(spread + 1e-05)
        stage[0:1024, :] = center.reshape(1024, 128)
        for r in range(8):
            tile = stage[pl.ds(r, 128, stride=8), :]
            settled[r * 128 : r * 128 + 128] = tile.astype(BF).T
        for part in range(parts):
            rows = pl.ds(part * (1024 // parts), 1024 // parts)
            gate = sigmoid(dot(normed_in[rows], w_gate[block]))
            update = dot(settled[rows], w_out[block])
            updated = (z[rows].astype(F32) + gate * update).astype(BF)
            trans_in = norm_lanes(updated.astype(F32)).astype(BF)
            gates = dot(trans_in, w_pin[block, :, 0:512])
            ups = dot(trans_in, w_pin[block, :, 512:1024])
            inner = silu_times(gates, ups)
            done = (updated.astype(F32) + dot(inner, w_pout[block])).astype(BF)
            put(part, rows, done)

    def await_back(block, kind, landed):
        if kind == FULL:
            pltpu.make_async_copy(landed, landed, back_recv.at[block, kind]).wait()
        else:

            @pl.when(active)
            def _():
                pltpu.make_async_copy(landed, landed, back_recv.at[block, kind]).wait()

            @pl.when(jnp.logical_not(active))
            def _():
                landed[...] = jnp.zeros(landed.shape, BF)

    def finish(block, kind):
        z = (zin if block == 0 else zout.at[0]).at[kind]
        landed = tr_full.at[block] if kind == FULL else tr_half
        parts = 1 if block == 0 else 2
        await_back(block, kind, landed)

        def put(part, rows, done):
            zout[block, kind, rows] = done
            if block == 0:
                normed[kind, rows] = norm_lanes(done.astype(F32)).astype(BF)
            else:
                deliver(block, kind, part, parts)

        complete(block, landed, z, normed.at[kind], parts, put)

    def finish_last():
        await_back(1, HALF, tr_last)
        pltpu.make_async_copy(z_peer, z_peer, peer_recv).wait()
        normed_peer[...] = norm_lanes(z_peer[...].astype(F32)).astype(BF)
        for half in range(2):

            def put(part, rows, done):
                zlast[half, rows] = done
                pltpu.make_async_copy(
                    zlast.at[half, rows], out.at[HALF, half, rows], out_local.at[HALF]
                ).start()

            own = half == 1
            complete(
                1,
                tr_last.at[half],
                zout.at[0, HALF] if own else z_peer,
                normed.at[HALF] if own else normed_peer,
                1,
                put,
            )

    peer_copy = pltpu.make_async_remote_copy(
        zout.at[0, HALF], z_peer, peer_send, peer_recv, device_id=peer, device_id_type=MESH
    )

    def deliver(block, kind, part=0, parts=1):
        rows = pl.ds(part * (1024 // parts), 1024 // parts)

        @pl.when(sec == block)
        def _():
            pltpu.make_async_copy(
                zout.at[block, kind, rows], out.at[kind, sec, rows], out_local.at[kind]
            ).start()

        @pl.when(sec != block)
        def _():
            pltpu.make_async_remote_copy(
                zout.at[block, kind, rows], out.at[kind, sec, rows],
                out_send.at[kind], out_recv.at[kind],
                device_id=peer, device_id_type=MESH,
            ).start()

    def single(rows_in):
        value = rows_in[...].astype(F32)
        value_in = norm_lanes(value).astype(BF)
        total = value
        for part in range(6):
            cols = part * 256
            gates = dot(value_in, st_in_v[:, cols : cols + 256])
            ups = dot(value_in, st_in_v[:, 1536 + cols : 1536 + cols + 256])
            inner = silu_times(gates, ups)
            total = total + dot(inner, st_out_v[cols : cols + 256])
        sout[...] = total.astype(BF)

    single_copy = pltpu.make_async_remote_copy(
        sout, sin_next, single_send, single_recv, device_id=peer, device_id_type=MESH
    )

    def start_block(block, side):
        cols = slice(256 - 256 * side, 512 - 256 * side)

        @pl.when(sec != block)
        def _():
            held = w_tin.at[block, :, cols]
            pltpu.make_async_copy(held, held, w_first.at[1, side]).wait()

        w_t[block, cols] = w_tin[block, :, cols].astype(F32).T.astype(BF)

    def more_weights():
        for index in range(1, 5):
            weight_copy(index).start()

    def rest_weights(block):
        for index in range(1, 5):
            await_weight(block, index)

    def single_turn(block):
        @pl.when(sec == block)
        def _():
            for copy in st_copies:
                copy.wait()
            if block == 0:
                single(sin)
                single_copy.start()
            else:
                single_copy.wait_recv()
                single(sin_next)

    start_block(0, RIGHT)
    project_full(0, RIGHT)
    send_full(0, RIGHT)
    start_block(0, LEFT)
    forward(0, HALF)
    project_full(0, LEFT)
    send_full(0, LEFT)
    more_weights()
    single_turn(0)
    triangle_full(0, RIGHT)
    relay(0)
    triangle_full(0, LEFT)
    triangle_out(0, FULL)
    triangle_half(0)
    triangle_out(0, HALF)
    start_block(1, RIGHT)
    start_block(1, LEFT)
    rest_weights(0)
    finish(0, FULL)
    project_full(1, RIGHT)
    send_full(1, RIGHT)
    finish(0, HALF)
    forward(1, HALF)
    project_full(1, LEFT)
    send_full(1, LEFT)
    deliver(0, FULL)
    deliver(0, HALF)
    pl.when(sec == 0)(peer_copy.start)
    single_turn(1)
    triangle_full(1, RIGHT)
    relay(1)
    triangle_full(1, LEFT)
    triangle_out(1, FULL)
    triangle_half(1)
    triangle_out(1, HALF)
    rest_weights(1)
    pl.when(jnp.logical_and(sec == 1, jnp.logical_not(active)))(finish_last)
    finish(1, FULL)
    pl.when(jnp.logical_and(sec == 1, active))(finish_last)

    def end_forward(block, kind):
        if kind == FULL:
            for side in (RIGHT, LEFT):
                sent = rbuf_full.at[block, side, pl.ds(0, 127)]
                pltpu.make_async_copy(sent, sent, full_send.at[block, side]).wait()
        else:
            sent = sbuf.at[block, pl.ds(0, 28)]
            pltpu.make_async_copy(sent, sent, fwd_send.at[block]).wait()
            sent = sbuf.at[block, pl.ds(0, 120)]
            pl.when(active)(pltpu.make_async_copy(sent, sent, relay_send.at[block]).wait)

    def end_triangle(block, kind):
        mine = (all_full if kind == FULL else all_half).at[block, core]
        pltpu.make_async_copy(mine, mine, sib_send.at[block, kind]).wait()

    def end_back(block, kind):
        def wait(count):
            sent = tr_full.at[block, pl.ds(0, count)]
            pltpu.make_async_copy(sent, sent, back_send.at[block, kind]).wait()

        if kind == FULL:
            wait(127)
        else:
            own = active if block == 0 else jnp.logical_and(active, sec == 1)
            pl.when(own)(lambda: wait(31 if block == 0 else 30))
            pl.when(jnp.logical_not(own))(lambda: wait(32))

    def end_rest():
        first_copy(RIGHT).wait_send()
        first_copy(LEFT).wait_send()
        for index in range(1, 5):
            weight_copy(index).wait_send()
        pl.when(sec == 0)(single_copy.wait_send)

    def end_deliver(kind):
        given = pltpu.make_async_copy(zout.at[0, kind], zout.at[0, kind], out_send.at[kind])
        kept = out.at[kind, sec]
        kept = pltpu.make_async_copy(kept, kept, out_local.at[kind])
        taken = out.at[kind, 1 - sec]
        taken = pltpu.make_async_copy(taken, taken, out_recv.at[kind])
        if kind == FULL:
            given.wait()
            kept.wait()
            taken.wait()
        else:

            @pl.when(sec == 0)
            def _():
                peer_copy.wait_send()
                kept.wait()
                taken.wait()

            @pl.when(sec == 1)
            def _():
                given.wait()
                both = out.at[kind]
                pltpu.make_async_copy(both, both, out_local.at[kind]).wait()

    for block in range(2):
        for kind in (FULL, HALF):
            end_forward(block, kind)
            end_triangle(block, kind)
            end_back(block, kind)
    end_rest()
    end_deliver(FULL)
    end_deliver(HALF)


def trunk(lengths, pair, sin, tin, tgate, tout, pin, pout, st_in, st_out):
    vmem = pl.BlockSpec(memory_space=pltpu.VMEM)
    anywhere = pl.BlockSpec(memory_space=pl.ANY)
    dma = pltpu.SemaphoreType.DMA
    return pl.pallas_call(
        trunk_kernel,
        out_shape=(
            jax.ShapeDtypeStruct((2, 2, 1024, 128), BF),
            jax.ShapeDtypeStruct((128, 384), BF),
        ),
        in_specs=[pl.BlockSpec(memory_space=pltpu.SMEM), anywhere, vmem] + [anywhere] * 7,
        out_specs=(anywhere, vmem),
        scratch_shapes=[
            pltpu.VMEM((2, 128, 512), BF),
            pltpu.VMEM((2, 128, 128), BF),
            pltpu.VMEM((2, 128, 128), BF),
            pltpu.VMEM((2, 128, 1024), BF),
            pltpu.VMEM((2, 512, 128), BF),
            pltpu.VMEM((2, 512, 128), BF),
            pltpu.VMEM((384, 3072), BF),
            pltpu.VMEM((1536, 384), BF),
            pltpu.VMEM((128, 384), BF),
            dma((6,)),
            dma((2,)),
            pltpu.VMEM((2, 32, 32, 128), BF),
            pltpu.VMEM((2, 1024, 128), BF),
            pltpu.VMEM((2, 2, 1024, 128), BF),
            pltpu.VMEM((2, 1024, 128), BF),
            pltpu.VMEM((2048, 128), F32),
            pltpu.VMEM((1024, 128), BF),
            pltpu.VMEM((4, 128, 512), BF),
            pltpu.VMEM((256, 256), BF),
            pltpu.VMEM((128, 128), BF),
            pltpu.VMEM((2, 2, 128, 8, 128), BF),
            pltpu.VMEM((2, 128, 16, 128), BF),
            pltpu.VMEM((2, 2, 128, 8, 128), BF),
            pltpu.VMEM((2, 32, 16, 128), BF),
            pltpu.VMEM((256, 512), BF),
            pltpu.VMEM((256, 512), BF),
            pltpu.VMEM((2, 2, 4, 64, 512), BF),
            pltpu.VMEM((128, 256), BF),
            pltpu.VMEM((128, 256), BF),
            pltpu.VMEM((2, 2, 2, 64, 256), BF),
            pltpu.VMEM((2, 16, 8, 8, 128), BF),
            pltpu.VMEM((2, 8, 4, 8, 128), BF),
            pltpu.VMEM((2, 128, 8, 128), BF),
            pltpu.VMEM((128, 8, 128), BF),
            pltpu.VMEM((2, 128, 8, 128), BF),
            pltpu.VMEM((1024, 128), BF),
            pltpu.VMEM((1024, 128), BF),
            pltpu.VMEM((2, 1024, 128), BF),
            dma,
            dma,
            pltpu.VMEM((2, 4, 8, 16, 128), BF),
            dma((2,)),
            dma((2,)),
            dma((2, 2)),
            dma((2, 2)),
            dma((2,)),
            dma((2,)),
            dma((2, 2)),
            dma((2, 2)),
            dma((2, 2)),
            dma((2, 2)),
            pltpu.SemaphoreType.REGULAR,
            dma((2, 2)),
            dma((5,)),
            dma((5,)),
            dma((2,)),
            dma,
            dma,
            dma((2,)),
            dma((2,)),
        ],
        compiler_params=pltpu.CompilerParams(
            collective_id=0, has_side_effects=True, vmem_limit_bytes=56 << 20
        ),
    )(lengths, pair, sin, tin, tgate, tout, pin, pout, st_in, st_out)


def restore_kernel(lengths, staged, staged_single, out, sout, sems):
    first = jnp.where(lengths[0] > lengths[1], 0, 1)
    copies = [
        pltpu.make_async_copy(staged.at[micro ^ first, half], out.at[0, micro, half], sems.at[micro, half])
        for micro in range(2)
        for half in range(2)
    ]
    copies.append(pltpu.make_async_copy(staged_single, sout, sems.at[2, 0]))
    for copy in copies:
        copy.start()
    for copy in copies:
        copy.wait()


def restore(lengths, staged, staged_single):
    anywhere = pl.BlockSpec(memory_space=pl.ANY)
    return pl.pallas_call(
        restore_kernel,
        out_shape=(
            jax.ShapeDtypeStruct((1, 2, 2, 1024, 128), BF),
            jax.ShapeDtypeStruct((128, 384), BF),
        ),
        in_specs=[pl.BlockSpec(memory_space=pltpu.SMEM), anywhere, anywhere],
        out_specs=(pl.BlockSpec(memory_space=pltpu.VMEM),) * 2,
        scratch_shapes=[pltpu.SemaphoreType.DMA((3, 2))],
    )(lengths, staged, staged_single)


def on_device(pair, single, lengths, tri_in, tri_gate, tri_out, pt_in, pt_out, st_in, st_out):
    staged, staged_single = trunk(
        lengths,
        pair,
        single.reshape(128, 384),
        tri_in[0], tri_gate[0], tri_out[0], pt_in[0], pt_out[0], st_in[0], st_out[0],
    )
    out, sout = restore(lengths, staged, staged_single)
    return out.reshape(1, 2, 64, 32, 128), sout.reshape(1, 2, 64, 384)


def solution(mesh):
    section = P("section", None, None)
    in_specs = (P(None, "gr", "gc", None), P(None, "gr", None), P()) + (section,) * 7
    out_specs = (P("section", None, "gr", "gc", None), P("section", None, "gr", None))
    return jax.shard_map(
        on_device, mesh=mesh, in_specs=in_specs, out_specs=out_specs, check_vma=False
    )
```

```python
import jax
import jax.numpy as jnp
from jax import lax
from jax.experimental import pallas as pl
from jax.experimental.pallas import tpu as pltpu
from jax.sharding import PartitionSpec as P

MESH = pl.DeviceIdType.MESH
FULL, HALF = 0, 1
RIGHT, LEFT = 0, 1
BF = jnp.bfloat16
F32 = jnp.float32


def dot(a, b):
    return jnp.dot(a, b, preferred_element_type=F32)


def dot_nt(a, b):
    return lax.dot_general(a, b, (((1,), (1,)), ((), ())), preferred_element_type=F32)


def sigmoid(v):
    return 0.5 + 0.5 * jnp.tanh(0.5 * v)


def norm_lanes(v):
    center = v - jnp.mean(v, axis=-1, keepdims=True)
    spread = jnp.mean(center * center, axis=-1, keepdims=True)
    return center * lax.rsqrt(spread + 1e-05)


def silu_times(gates, ups):
    half = 0.5 * gates
    return ((half + half * jnp.tanh(half)) * ups).astype(BF)


def iota(shape, axis):
    return lax.broadcasted_iota(jnp.int32, shape, axis)


def trunk_kernel(
    lengths, pair, sin, tin, tgate, tout, pin, pout, st_in, st_out,
    out, sout,
    w_tin, w_gate, w_out, w_pin, w_pout, w_t, st_in_v, st_out_v, sin_next,
    own_sem, out_local, pair_in, zin, zout, normed, stage, settled, perm, order_full, order_half,
    sfull, sbuf, rbuf_full, rbuf_half, lm_full, raw_full, all_full, lm_half, raw_half, all_half,
    ts_full, ts_half, tr_full, tr_half, tr_last, z_peer, normed_peer, zlast, peer_send, peer_recv,
    relayed, relay_send, relay_recv, full_send, full_recv, fwd_send, fwd_recv, sib_send, sib_recv, back_send, back_recv,
    met, w_first, w_send, w_recv, st_sem, single_send, single_recv, out_send, out_recv,
):
    sec, gr, gc = lax.axis_index("section"), lax.axis_index("gr"), lax.axis_index("gc")
    y, core = lax.shift_right_logical(gr, 1), lax.bitwise_and(gr, 1)
    sy = sec * 4 + y
    x_hi, z_at = lax.shift_right_logical(gc, 3), lax.bitwise_and(gc, 7)
    plane = x_hi * 8 + sy
    channel = plane * 8 + z_at
    slot = gc * 8 + sy
    active = jnp.logical_and(y < 2, gc < 8)
    peer = {"section": 1 - sec, "gr": gr, "gc": gc}
    sibling = {"section": sec, "gr": gr + 1 - 2 * core, "gc": gc}

    def place(step):
        to_gc = lax.bitwise_and(gc + step, 15)
        to_sy = lax.bitwise_and(sy + lax.shift_right_logical(step, 4), 7)
        to_sec = lax.shift_right_logical(to_sy, 2)
        to_y = lax.bitwise_and(to_sy, 3)
        return to_gc, to_sy, {"section": to_sec, "gr": to_y * 2 + core, "gc": to_gc}

    def channel_of(at_gc, at_sy):
        at_plane = lax.shift_right_logical(at_gc, 3) * 8 + at_sy
        return at_plane * 8 + lax.bitwise_and(at_gc, 7)

    st_copies = [
        pltpu.make_async_copy(st_in, st_in_v, st_sem.at[0]),
        pltpu.make_async_copy(st_out, st_out_v, st_sem.at[1]),
    ]
    weights = [(tin, w_tin), (tgate, w_gate), (tout, w_out), (pin, w_pin), (pout, w_pout)]
    pair_copy = pltpu.make_async_copy(pair.at[:, pl.ds(sec * 32, 32)], pair_in, own_sem.at[5])
    own_copies = [
        pltpu.make_async_copy(own, held.at[sec], own_sem.at[index])
        for index, (own, held) in enumerate(weights)
    ]
    for copy in [pair_copy] + own_copies + st_copies:
        copy.start()

    barrier = pltpu.get_barrier_semaphore()

    def greet_line(semaphore):
        def greet(step, carry):
            to_gc = lax.bitwise_and(gc + step, 15)
            pl.semaphore_signal(
                semaphore, inc=1, device_id={"section": sec, "gr": gr, "gc": to_gc},
                device_id_type=MESH,
            )
            return carry

        lax.fori_loop(1, 16, greet, 0)

    pl.semaphore_signal(barrier, inc=1, device_id=sibling, device_id_type=MESH)
    for step in range(1, 8):
        pl.semaphore_signal(
            barrier, inc=1, device_id=place(step * 16)[2], device_id_type=MESH
        )
    greet_line(barrier)

    def weight_copy(index):
        own, held = weights[index]
        return pltpu.make_async_remote_copy(
            own, held.at[sec], w_send.at[index], w_recv.at[index],
            device_id=peer, device_id_type=MESH,
        )

    def first_copy(side):
        cols = pl.ds(256 - 256 * side, 256)
        return pltpu.make_async_remote_copy(
            tin.at[:, cols], w_tin.at[sec, :, cols], w_first.at[0, side], w_first.at[1, side],
            device_id=peer, device_id_type=MESH,
        )

    pl.semaphore_wait(barrier, 23)
    first_copy(RIGHT).start()
    first_copy(LEFT).start()
    greet_line(met)

    from_lane, to_lane = iota((128, 512), 0), iota((128, 512), 1)
    for low in range(4):
        target = (from_lane >> 5) * 128 + low * 32 + (from_lane & 31)
        perm[low] = jnp.where(to_lane == target, 1.0, 0.0).astype(BF)
    o, i = iota((256, 256), 0), iota((256, 256), 1)
    source = (o & 3) * 64 + ((o >> 5) & 1) * 32 + (o >> 6) * 8 + ((o >> 2) & 7)
    order_full[...] = jnp.where(i == source, 1.0, 0.0).astype(BF)
    o, i = iota((128, 128), 0), iota((128, 128), 1)
    source = (o & 3) * 32 + ((o >> 5) & 1) * 16 + (o >> 6) * 8 + ((o >> 2) & 7)
    order_half[...] = jnp.where(i == source, 1.0, 0.0).astype(BF)

    for copy in [pair_copy] + own_copies:
        copy.wait()
    first = jnp.where(lengths[0] > lengths[1], 0, 1)
    for kind, crop in ((FULL, first), (HALF, 1 - first)):
        z = pair_in[crop].reshape(1024, 128)
        zin[kind] = z
        normed[kind] = norm_lanes(z.astype(F32)).astype(BF)

    pl.semaphore_wait(met, 15)

    def await_weight(block, index):
        @pl.when(sec != block)
        def _():
            held = weights[index][1].at[block]
            pltpu.make_async_copy(held, held, w_recv.at[index]).wait()

    def gated(block, side, values):
        cols = slice(256 - 256 * side, 512 - 256 * side)
        p = dot_nt(w_t[block, cols], values)
        return sigmoid(p[0:128]) * p[128:256]

    def project_full(block, side):
        for part in range(2):
            value = gated(block, side, normed[FULL, pl.ds(part * 512, 512)])
            for sub in range(4):
                stage[pl.ds(part * 4 + sub, 128, stride=8), :] = value[:, sub * 128 : sub * 128 + 128]
        for part in range(4):
            values = stage[part * 256 : part * 256 + 256, :].astype(BF)
            sfull[block, side, part * 32 : part * 32 + 32] = values.reshape(32, 8, 128)

    def project_half(block):
        for part in range(4):
            values = normed[HALF, pl.ds(part * 256, 256)]
            for side in (LEFT, RIGHT):
                value = gated(block, side, values)
                row = part * 2 + 8 * (1 - side)
                for sub in range(2):
                    stage[pl.ds(row + sub, 128, stride=16), :] = value[:, sub * 128 : sub * 128 + 128]
        for part in range(8):
            values = stage[part * 256 : part * 256 + 256, :].astype(BF)
            sbuf[block, part * 16 : part * 16 + 16] = values.reshape(16, 16, 128)

    def send_full(block, side):
        for turn in range(8):
            to_sy = lax.bitwise_and(sy + turn, 7)
            to_row = lax.bitwise_and(to_sy, 3) * 2 + core
            to_sec = lax.shift_right_logical(to_sy, 2)

            def send(step, carry):
                to_gc = lax.bitwise_and(gc + step, 15)
                pltpu.make_async_remote_copy(
                    sfull.at[block, side, channel_of(to_gc, to_sy)],
                    rbuf_full.at[block, side, slot],
                    full_send.at[block, side], full_recv.at[block, side],
                    device_id={"section": to_sec, "gr": to_row, "gc": to_gc},
                    device_id_type=MESH,
                ).start()
                return carry

            first = 1 if turn == 0 else 0
            lax.fori_loop(first, 16, send, 0, unroll=5 if turn == 0 else 4)
        pltpu.make_async_copy(
            sfull.at[block, side, channel], rbuf_full.at[block, side, slot],
            full_recv.at[block, side],
        ).start()

    def send_half(block):
        source = sec * 2 + y
        for step in range(1, 16):
            to_plane = lax.bitwise_and(plane + step, 15)
            to_sy = lax.bitwise_and(to_plane, 7)
            pltpu.make_async_remote_copy(
                sbuf.at[block, pl.ds(to_plane * 8, 8)], relayed.at[block, source],
                relay_send.at[block], relay_recv.at[block],
                device_id={
                    "section": lax.shift_right_logical(to_sy, 2),
                    "gr": lax.bitwise_and(to_sy, 3) * 2 + core,
                    "gc": lax.shift_right_logical(to_plane, 3) * 8 + z_at,
                },
                device_id_type=MESH,
            ).start()
        pltpu.make_async_copy(
            sbuf.at[block, pl.ds(plane * 8, 8)], relayed.at[block, source],
            relay_recv.at[block],
        ).start()

    def relay(block):
        landed = relayed.at[block]
        pltpu.make_async_copy(landed, landed, relay_recv.at[block]).wait()
        at = rbuf_half.at[block, pl.ds(z_at * 4, 4)]
        for step in range(1, 8):
            to_z = lax.bitwise_and(z_at + step, 7)
            pltpu.make_async_remote_copy(
                relayed.at[block, :, to_z], at, fwd_send.at[block], fwd_recv.at[block],
                device_id={"section": sec, "gr": gr, "gc": x_hi * 8 + to_z},
                device_id_type=MESH,
            ).start()
        pltpu.make_async_copy(relayed.at[block, :, z_at], at, fwd_recv.at[block]).start()

    def forward(block, kind):
        if kind == FULL:
            for side in (RIGHT, LEFT):
                project_full(block, side)
                send_full(block, side)
        else:

            @pl.when(active)
            def _():
                project_half(block)
                send_half(block)

    def parts_of(kind):
        if kind == FULL:
            return lm_full, all_full, ts_full, 4, 8
        return lm_half, all_half, ts_half, 2, 4

    def share_right(block, kind, g, ordered):
        whole = all_full if kind == FULL else all_half
        lanes = slice(g * 128, g * 128 + 128)
        whole[block, core, :, :, lanes] = ordered.astype(BF).reshape(-1, 64, 128)
        mine = whole.at[block, core, :, :, lanes]
        pltpu.make_async_remote_copy(
            mine, mine, sib_send.at[block, kind], sib_recv.at[block, kind],
            device_id=sibling, device_id_type=MESH,
        ).start()

    def triangle_full(block, side):
        landed = rbuf_full.at[block, side]
        pltpu.make_async_copy(landed, landed, full_recv.at[block, side]).wait()
        held = raw_full if side == RIGHT else lm_full
        for g in range(4):
            total = None
            for low in range(4):
                col = (g * 4 + low) * 8
                block_in = rbuf_full[block, side, col : col + 8].astype(F32)
                term = dot(block_in.reshape(64, 128).astype(BF), perm[low])
                total = term if total is None else total + term
            total = total.astype(BF)
            lanes = slice(g * 128, g * 128 + 128)
            for low in range(4):
                held[low * 64 : low * 64 + 64, lanes] = total[:, low * 128 : low * 128 + 128]
            if side == RIGHT:
                share_right(block, FULL, g, dot(order_full[...], raw_full[:, lanes]))

    def triangle_half(block):
        landed = rbuf_half.at[block]
        pltpu.make_async_copy(landed, landed, fwd_recv.at[block]).wait()
        for g in range(2):
            total = None
            for low in range(4):
                col = (g * 4 + low) * 4
                block_in = rbuf_half[block, col : col + 4].reshape(64, 128)
                term = dot(block_in, perm[low])
                total = term if total is None else total + term
            total = total.reshape(4, 16, 512)
            left = total[:, 0:8].reshape(32, 512).astype(BF)
            right = total[:, 8:16].reshape(32, 512).astype(BF)
            lanes = slice(g * 128, g * 128 + 128)
            for low in range(4):
                cols = slice(low * 128, low * 128 + 128)
                lm_half[low * 32 : low * 32 + 32, lanes] = left[:, cols]
                raw_half[low * 32 : low * 32 + 32, lanes] = right[:, cols]
            share_right(block, HALF, g, dot(order_half[...], raw_half[:, lanes]))

    def triangle_out(block, kind):
        lm, whole, ts, groups, tiles = parts_of(kind)
        rows = tiles * 8
        full = kind == FULL
        other = whole.at[block, 1 - core]
        pltpu.make_async_copy(other, other, sib_recv.at[block, kind]).wait()
        home = lax.bitwise_and(lax.shift_right_logical(gc, 2), groups - 1)
        source = sy if full else sec * 2 + y

        for turn in range(groups):
            g = lax.bitwise_and(home + turn, groups - 1)
            right = jnp.concatenate([whole[block, 0, g], whole[block, 1, g]], axis=0)
            product = dot_nt(lm[...], right).astype(BF)
            total = None
            for low in range(4):
                term = dot(product[low * rows : (low + 1) * rows], perm[low])
                total = term if total is None else total + term
            total = total.astype(BF)
            for low in range(4):
                ts[block, g * 4 + low] = total[:, low * 128 : low * 128 + 128].reshape(
                    tiles, 8, 128
                )

            def send(step, carry):
                to_gc = g * 4 + lax.bitwise_and(gc + step, 3)
                to_tile = lax.bitwise_and(source + lax.shift_right_logical(step, 2), tiles - 1)
                to_sec = lax.shift_right_logical(to_tile, 2 if full else 1)
                to_y = lax.bitwise_and(to_tile, tiles // 2 - 1)

                if full:
                    target = tr_full.at[block, channel]
                elif block == 0:
                    target = tr_half.at[channel]
                else:
                    target = tr_last.at[to_sec, channel]
                    to_sec = 1

                def local():
                    pltpu.make_async_copy(
                        ts.at[block, to_gc, to_tile], target,
                        back_recv.at[block, kind],
                    ).start()

                def remote():
                    pltpu.make_async_remote_copy(
                        ts.at[block, to_gc, to_tile], target,
                        back_send.at[block, kind], back_recv.at[block, kind],
                        device_id={"section": to_sec, "gr": to_y * 2 + core, "gc": to_gc},
                        device_id_type=MESH,
                    ).start()

                if turn == 0:
                    itself = step == 0
                    if not full and block == 1:
                        itself = jnp.logical_and(to_gc == gc, to_y == y)
                        itself = jnp.logical_and(itself, sec == 1)
                    if not full:
                        itself = jnp.logical_and(itself, active)
                    pl.when(itself)(local)
                    pl.when(jnp.logical_not(itself))(remote)
                else:
                    remote()
                return carry

            lax.fori_loop(0, tiles * 4, send, 0, unroll=4)

    def complete(block, tr, z, normed_in, parts, put):
        values = tr[...].astype(F32)
        center = values - jnp.mean(values, axis=0, keepdims=True)
        spread = jnp.mean(center * center, axis=0, keepdims=True)
        center = center * lax.rsqrt(spread + 1e-05)
        stage[0:1024, :] = center.reshape(1024, 128)
        for r in range(8):
            tile = stage[pl.ds(r, 128, stride=8), :]
            settled[r * 128 : r * 128 + 128] = tile.astype(BF).T
        for part in range(parts):
            rows = pl.ds(part * (1024 // parts), 1024 // parts)
            gate = sigmoid(dot(normed_in[rows], w_gate[block]))
            update = dot(settled[rows], w_out[block])
            updated = (z[rows].astype(F32) + gate * update).astype(BF)
            trans_in = norm_lanes(updated.astype(F32)).astype(BF)
            gates = dot(trans_in, w_pin[block, :, 0:512])
            ups = dot(trans_in, w_pin[block, :, 512:1024])
            inner = silu_times(gates, ups)
            done = (updated.astype(F32) + dot(inner, w_pout[block])).astype(BF)
            put(part, rows, done)

    def await_back(block, kind, landed):
        if kind == FULL:
            pltpu.make_async_copy(landed, landed, back_recv.at[block, kind]).wait()
        else:

            @pl.when(active)
            def _():
                pltpu.make_async_copy(landed, landed, back_recv.at[block, kind]).wait()

            @pl.when(jnp.logical_not(active))
            def _():
                landed[...] = jnp.zeros(landed.shape, BF)

    def finish(block, kind):
        z = (zin if block == 0 else zout.at[0]).at[kind]
        landed = tr_full.at[block] if kind == FULL else tr_half
        parts = 1 if block == 0 else 2
        await_back(block, kind, landed)

        def put(part, rows, done):
            zout[block, kind, rows] = done
            if block == 0:
                normed[kind, rows] = norm_lanes(done.astype(F32)).astype(BF)
            else:
                deliver(block, kind, part, parts)

        complete(block, landed, z, normed.at[kind], parts, put)

    def finish_last():
        await_back(1, HALF, tr_last)
        pltpu.make_async_copy(z_peer, z_peer, peer_recv).wait()
        normed_peer[...] = norm_lanes(z_peer[...].astype(F32)).astype(BF)
        for half in range(2):

            def put(part, rows, done):
                zlast[half, rows] = done
                pltpu.make_async_copy(
                    zlast.at[half, rows], out.at[HALF, half, rows], out_local.at[HALF]
                ).start()

            own = half == 1
            complete(
                1,
                tr_last.at[half],
                zout.at[0, HALF] if own else z_peer,
                normed.at[HALF] if own else normed_peer,
                1,
                put,
            )

    peer_copy = pltpu.make_async_remote_copy(
        zout.at[0, HALF], z_peer, peer_send, peer_recv, device_id=peer, device_id_type=MESH
    )

    def deliver(block, kind, part=0, parts=1):
        rows = pl.ds(part * (1024 // parts), 1024 // parts)

        @pl.when(sec == block)
        def _():
            pltpu.make_async_copy(
                zout.at[block, kind, rows], out.at[kind, sec, rows], out_local.at[kind]
            ).start()

        @pl.when(sec != block)
        def _():
            pltpu.make_async_remote_copy(
                zout.at[block, kind, rows], out.at[kind, sec, rows],
                out_send.at[kind], out_recv.at[kind],
                device_id=peer, device_id_type=MESH,
            ).start()

    def single(rows_in):
        value = rows_in[...].astype(F32)
        value_in = norm_lanes(value).astype(BF)
        total = value
        for part in range(6):
            cols = part * 256
            gates = dot(value_in, st_in_v[:, cols : cols + 256])
            ups = dot(value_in, st_in_v[:, 1536 + cols : 1536 + cols + 256])
            inner = silu_times(gates, ups)
            total = total + dot(inner, st_out_v[cols : cols + 256])
        sout[...] = total.astype(BF)

    single_copy = pltpu.make_async_remote_copy(
        sout, sin_next, single_send, single_recv, device_id=peer, device_id_type=MESH
    )

    def start_block(block, side):
        cols = slice(256 - 256 * side, 512 - 256 * side)

        @pl.when(sec != block)
        def _():
            held = w_tin.at[block, :, cols]
            pltpu.make_async_copy(held, held, w_first.at[1, side]).wait()

        w_t[block, cols] = w_tin[block, :, cols].astype(F32).T.astype(BF)

    def more_weights():
        for index in range(1, 5):
            weight_copy(index).start()

    def rest_weights(block):
        for index in range(1, 5):
            await_weight(block, index)

    def single_turn(block):
        @pl.when(sec == block)
        def _():
            for copy in st_copies:
                copy.wait()
            if block == 0:
                single(sin)
                single_copy.start()
            else:
                single_copy.wait_recv()
                single(sin_next)

    start_block(0, RIGHT)
    project_full(0, RIGHT)
    send_full(0, RIGHT)
    start_block(0, LEFT)
    forward(0, HALF)
    project_full(0, LEFT)
    send_full(0, LEFT)
    more_weights()
    single_turn(0)
    triangle_full(0, RIGHT)
    relay(0)
    triangle_full(0, LEFT)
    triangle_out(0, FULL)
    triangle_half(0)
    triangle_out(0, HALF)
    start_block(1, RIGHT)
    start_block(1, LEFT)
    rest_weights(0)
    finish(0, FULL)
    project_full(1, RIGHT)
    send_full(1, RIGHT)
    finish(0, HALF)
    forward(1, HALF)
    project_full(1, LEFT)
    send_full(1, LEFT)
    deliver(0, FULL)
    deliver(0, HALF)
    pl.when(sec == 0)(peer_copy.start)
    single_turn(1)
    triangle_full(1, RIGHT)
    relay(1)
    triangle_full(1, LEFT)
    triangle_out(1, FULL)
    triangle_half(1)
    triangle_out(1, HALF)
    rest_weights(1)
    pl.when(jnp.logical_and(sec == 1, jnp.logical_not(active)))(finish_last)
    finish(1, FULL)
    pl.when(jnp.logical_and(sec == 1, active))(finish_last)

    def end_forward(block, kind):
        if kind == FULL:
            for side in (RIGHT, LEFT):
                sent = rbuf_full.at[block, side, pl.ds(0, 127)]
                pltpu.make_async_copy(sent, sent, full_send.at[block, side]).wait()
        else:
            sent = sbuf.at[block, pl.ds(0, 28)]
            pltpu.make_async_copy(sent, sent, fwd_send.at[block]).wait()
            sent = sbuf.at[block, pl.ds(0, 120)]
            pl.when(active)(pltpu.make_async_copy(sent, sent, relay_send.at[block]).wait)

    def end_triangle(block, kind):
        mine = (all_full if kind == FULL else all_half).at[block, core]
        pltpu.make_async_copy(mine, mine, sib_send.at[block, kind]).wait()

    def end_back(block, kind):
        def wait(count):
            sent = tr_full.at[block, pl.ds(0, count)]
            pltpu.make_async_copy(sent, sent, back_send.at[block, kind]).wait()

        if kind == FULL:
            wait(127)
        else:
            own = active if block == 0 else jnp.logical_and(active, sec == 1)
            pl.when(own)(lambda: wait(31 if block == 0 else 30))
            pl.when(jnp.logical_not(own))(lambda: wait(32))

    def end_rest():
        first_copy(RIGHT).wait_send()
        first_copy(LEFT).wait_send()
        for index in range(1, 5):
            weight_copy(index).wait_send()
        pl.when(sec == 0)(single_copy.wait_send)

    def end_deliver(kind):
        given = pltpu.make_async_copy(zout.at[0, kind], zout.at[0, kind], out_send.at[kind])
        kept = out.at[kind, sec]
        kept = pltpu.make_async_copy(kept, kept, out_local.at[kind])
        taken = out.at[kind, 1 - sec]
        taken = pltpu.make_async_copy(taken, taken, out_recv.at[kind])
        if kind == FULL:
            given.wait()
            kept.wait()
            taken.wait()
        else:

            @pl.when(sec == 0)
            def _():
                peer_copy.wait_send()
                kept.wait()
                taken.wait()

            @pl.when(sec == 1)
            def _():
                given.wait()
                both = out.at[kind]
                pltpu.make_async_copy(both, both, out_local.at[kind]).wait()

    for block in range(2):
        for kind in (FULL, HALF):
            end_forward(block, kind)
            end_triangle(block, kind)
            end_back(block, kind)
    end_rest()
    end_deliver(FULL)
    end_deliver(HALF)


def trunk(lengths, pair, sin, tin, tgate, tout, pin, pout, st_in, st_out):
    vmem = pl.BlockSpec(memory_space=pltpu.VMEM)
    anywhere = pl.BlockSpec(memory_space=pl.ANY)
    dma = pltpu.SemaphoreType.DMA
    return pl.pallas_call(
        trunk_kernel,
        out_shape=(
            jax.ShapeDtypeStruct((2, 2, 1024, 128), BF),
            jax.ShapeDtypeStruct((128, 384), BF),
        ),
        in_specs=[pl.BlockSpec(memory_space=pltpu.SMEM), anywhere, vmem] + [anywhere] * 7,
        out_specs=(anywhere, vmem),
        scratch_shapes=[
            pltpu.VMEM((2, 128, 512), BF),
            pltpu.VMEM((2, 128, 128), BF),
            pltpu.VMEM((2, 128, 128), BF),
            pltpu.VMEM((2, 128, 1024), BF),
            pltpu.VMEM((2, 512, 128), BF),
            pltpu.VMEM((2, 512, 128), BF),
            pltpu.VMEM((384, 3072), BF),
            pltpu.VMEM((1536, 384), BF),
            pltpu.VMEM((128, 384), BF),
            dma((6,)),
            dma((2,)),
            pltpu.VMEM((2, 32, 32, 128), BF),
            pltpu.VMEM((2, 1024, 128), BF),
            pltpu.VMEM((2, 2, 1024, 128), BF),
            pltpu.VMEM((2, 1024, 128), BF),
            pltpu.VMEM((2048, 128), F32),
            pltpu.VMEM((1024, 128), BF),
            pltpu.VMEM((4, 128, 512), BF),
            pltpu.VMEM((256, 256), BF),
            pltpu.VMEM((128, 128), BF),
            pltpu.VMEM((2, 2, 128, 8, 128), BF),
            pltpu.VMEM((2, 128, 16, 128), BF),
            pltpu.VMEM((2, 2, 128, 8, 128), BF),
            pltpu.VMEM((2, 32, 16, 128), BF),
            pltpu.VMEM((256, 512), BF),
            pltpu.VMEM((256, 512), BF),
            pltpu.VMEM((2, 2, 4, 64, 512), BF),
            pltpu.VMEM((128, 256), BF),
            pltpu.VMEM((128, 256), BF),
            pltpu.VMEM((2, 2, 2, 64, 256), BF),
            pltpu.VMEM((2, 16, 8, 8, 128), BF),
            pltpu.VMEM((2, 8, 4, 8, 128), BF),
            pltpu.VMEM((2, 128, 8, 128), BF),
            pltpu.VMEM((128, 8, 128), BF),
            pltpu.VMEM((2, 128, 8, 128), BF),
            pltpu.VMEM((1024, 128), BF),
            pltpu.VMEM((1024, 128), BF),
            pltpu.VMEM((2, 1024, 128), BF),
            dma,
            dma,
            pltpu.VMEM((2, 4, 8, 16, 128), BF),
            dma((2,)),
            dma((2,)),
            dma((2, 2)),
            dma((2, 2)),
            dma((2,)),
            dma((2,)),
            dma((2, 2)),
            dma((2, 2)),
            dma((2, 2)),
            dma((2, 2)),
            pltpu.SemaphoreType.REGULAR,
            dma((2, 2)),
            dma((5,)),
            dma((5,)),
            dma((2,)),
            dma,
            dma,
            dma((2,)),
            dma((2,)),
        ],
        compiler_params=pltpu.CompilerParams(
            collective_id=0, has_side_effects=True, vmem_limit_bytes=56 << 20
        ),
    )(lengths, pair, sin, tin, tgate, tout, pin, pout, st_in, st_out)


def restore_kernel(lengths, staged, staged_single, out, sout, held, held_single, arrive, leave):
    first = jnp.where(lengths[0] > lengths[1], 0, 1)
    steps = [
        (staged.at[micro ^ first, half], held.at[micro, half], out.at[0, micro, half])
        for micro in range(2)
        for half in range(2)
    ]
    steps.append((staged_single, held_single, sout))
    taken = [
        pltpu.make_async_copy(source, kept, arrive.at[index])
        for index, (source, kept, target) in enumerate(steps)
    ]
    given = [
        pltpu.make_async_copy(kept, target, leave.at[index])
        for index, (source, kept, target) in enumerate(steps)
    ]
    for copy in taken:
        copy.start()
    for arrived, onward in zip(taken, given):
        arrived.wait()
        onward.start()
    for copy in given:
        copy.wait()


def restore(lengths, staged, staged_single):
    anywhere = pl.BlockSpec(memory_space=pl.ANY)
    return pl.pallas_call(
        restore_kernel,
        out_shape=(
            jax.ShapeDtypeStruct((1, 2, 2, 1024, 128), BF),
            jax.ShapeDtypeStruct((128, 384), BF),
        ),
        in_specs=[pl.BlockSpec(memory_space=pltpu.SMEM), anywhere, anywhere],
        out_specs=(anywhere, anywhere),
        scratch_shapes=[
            pltpu.VMEM((2, 2, 1024, 128), BF),
            pltpu.VMEM((128, 384), BF),
            pltpu.SemaphoreType.DMA((5,)),
            pltpu.SemaphoreType.DMA((5,)),
        ],
    )(lengths, staged, staged_single)


def on_device(pair, single, lengths, tri_in, tri_gate, tri_out, pt_in, pt_out, st_in, st_out):
    staged, staged_single = trunk(
        lengths,
        pair,
        single.reshape(128, 384),
        tri_in[0], tri_gate[0], tri_out[0], pt_in[0], pt_out[0], st_in[0], st_out[0],
    )
    out, sout = restore(lengths, staged, staged_single)
    return out.reshape(1, 2, 64, 32, 128), sout.reshape(1, 2, 64, 384)


def solution(mesh):
    section = P("section", None, None)
    in_specs = (P(None, "gr", "gc", None), P(None, "gr", None), P()) + (section,) * 7
    out_specs = (P("section", None, "gr", "gc", None), P("section", None, "gr", None))
    return jax.shard_map(
        on_device, mesh=mesh, in_specs=in_specs, out_specs=out_specs, check_vma=False
    )
```
